32 devices in a mesh: replica: 2 (over y), expert: 4 (over z), fsdp: 4 (over x, core).
Axes of the slice: x: 2, y: 2, z: 4, core: 2. Of those that a mesh axis runs over, the one named last changes fastest.
Arguments:
- tokens: bfloat16 [8192, 2048], P(('replica', 'expert', 'fsdp')), parts along dimension 0, may hold values from -6 to 6
- cotangent: bfloat16 [8192, 2048], P(('replica', 'expert', 'fsdp')), parts along dimension 0, may hold values from -6 to 6
- route_ids: int32 [8192, 8], P(('replica', 'expert', 'fsdp')), parts along dimension 0, may hold values from 0 to 127, all different within a row
- route_gates: float32 [8192, 8], P(('replica', 'expert', 'fsdp')), parts along dimension 0, may hold values from 0.2 to 2
- served_order: int32 [32, 256], P(('replica', 'expert', 'fsdp')), parts along dimension 0, may hold values from 0 to 255, each once within a row
- w_in: bfloat16 [4, 2048, 1536], P('expert', 'fsdp'), may hold values from -0.125 to 0.125
- w_out: bfloat16 [4, 2048, 768], P('expert', 'fsdp'), may hold values from -0.21875 to 0.21875
Outputs:
- combined: bfloat16 [8192, 2048], P(('replica', 'expert', 'fsdp')), parts along dimension 0
- d_tokens: bfloat16 [8192, 2048], P(('replica', 'expert', 'fsdp')), parts along dimension 0
- d_w_out: float32 [8, 2048, 768], P(('replica', 'expert'), 'fsdp'), parts along dimension 0
The draws below stay inside these ranges and needn't reach their ends.
There are 2 independent parts, one for each index of `replica`. The reference program is written for one: setup_inputs(seed, part) draws one part's arguments, and reference() takes and returns one part's arrays. A program takes and returns all parts, laid end to end along the dimension named above; an argument that names none is the same for every part. Nothing has to cross between parts.
All inputs are finite; a program needn't handle non-finite values.
Results may differ from the reference program's by a relative error of at most 0.008.
Values may be sent and summed in bfloat16 or wider, within the bound.
No kernel may reach another device: no remote copies, remote signals or barrier semaphores. Data moves between devices by JAX's collectives and lax.ppermute only.
A program may use at most 64 MiB of HBM per device.

```python
import math
import jax
import jax.numpy as jnp
from jax import lax

D = 2048
FF = 768
EXPERTS = 128
TOP = 8
TOK_DEV = 256
LOCAL = 32
WINDOW = 4
CAP = 16
BLOCKS = 16
TOKENS = 4096
N_EXPERT = 4
N_FSDP = 4


def spiked(result, stream_key, source, target, parts, factor):
    def block_of(dim):
        return (jnp.arange(result.shape[dim]) // (result.shape[dim] // parts)).reshape((-1,) + (1,) * (result.ndim - 1 - dim))

    one_side = jax.random.permutation(stream_key, parts)[block_of(target)]
    second = (block_of(target) + parts // 2) % parts
    return jnp.where((block_of(source) == one_side) | (block_of(source) == second), factor * result, result)


def shard_levels(key, dims, split, least, top_value):
    def one(dim, blocks):
        heights = jax.random.uniform(jax.random.fold_in(jax.random.fold_in(key, 6), dim), (blocks,), jnp.float32, least / len(split), top_value / len(split))
        return jnp.repeat(jnp.exp(heights), dims[dim] // blocks).reshape((-1,) + (1,) * (len(dims) - dim - 1))

    loudness = one(*split[0])
    for cut in split[1:]:
        loudness = loudness * one(*cut)
    return loudness


def different_ones(stream_key, rows, number_of, top, lift):
    order = jax.random.permutation(jax.random.fold_in(stream_key, 1), number_of)
    favour = order
    for power in range(3):
        favour = favour * favour // number_of
    favour = favour * lift // number_of
    tickets = jax.random.randint(jax.random.fold_in(stream_key, 2), (rows, number_of), 0, 4096) + favour
    holders = jax.random.permutation(jax.random.fold_in(stream_key, 3), rows)[jnp.arange(number_of) % rows]
    tickets = jnp.where(jnp.arange(rows)[:, None] == holders[None, :], 1 << 14, tickets)
    priority = tickets * number_of + jnp.arange(number_of)
    return lax.top_k(priority.astype(jnp.int32), top)[1].astype(jnp.int32)


def bell_draw(rng, extent, spread, reach, shards=(), kind=jnp.bfloat16):
    entries = jax.random.normal(rng, extent, jnp.float32) * spread
    if len(shards) > 0:
        entries = shard_levels(rng, extent, shards, -0.22, 0.18) * entries
    return jnp.clip(entries, min=-reach, max=reach).astype(kind)


def heavy_noise(key, dims, spread, reach, split, heavy, held_as=jnp.bfloat16):
    entries = spread * jax.random.normal(key, dims, jnp.float32)
    if split:
        entries = entries * shard_levels(key, dims, split, -0.22, 0.18)
    return jnp.clip(spiked(entries, jax.random.fold_in(key, 3), *heavy), -reach, reach).astype(held_as)


def setup_inputs(seed: int = 0, part: int = 0) -> dict:
    keys = jax.random.split(jax.random.key(seed), 8)
    part_keys = jax.random.split(jax.random.fold_in(keys[7], part), 8)
    return {
        "tokens": bell_draw(part_keys[0], (TOKENS, D), 1.0, 6.0, ((0, 16),)),
        "cotangent": heavy_noise(part_keys[1], (TOKENS, D), 1.0, 6.0, ((0, 16),), (0, 1, 16, 2.0)),
        "route_ids": different_ones(part_keys[2], TOKENS, EXPERTS, TOP, 1024),
        "route_gates": jnp.clip(jnp.exp(math.log(2.0) - 2.3025851 * jax.random.uniform(part_keys[3], (TOKENS, TOP), jnp.float32) ** shard_levels(part_keys[3], (TOKENS, TOP), ((0, 16),), -0.2, 0.2)), 0.2, 2.0),
        "served_order": jax.vmap(lambda own: jax.random.permutation(own, TOK_DEV))(jax.random.split(part_keys[4], BLOCKS)).reshape((BLOCKS, TOK_DEV)).astype(jnp.int32),
        "w_in": bell_draw(keys[5], (WINDOW, D, 2 * FF), D ** -0.5, 0.125, ((0, 4), (1, 4))),
        "w_out": bell_draw(keys[6], (WINDOW, D, FF), FF ** -0.5, 0.21875, ((0, 4), (1, 4))),
    }


def slot_table(expert_ids, order_row):
    tok_count = expert_ids.shape[0]
    choices = expert_ids.shape[1]
    served = jnp.take(expert_ids, order_row, axis=0)
    inside = ((served % LOCAL) == 0).reshape(-1)
    target = (served // LOCAL).reshape(-1)
    onehot = ((target[:, None] == jnp.arange(N_EXPERT, dtype=jnp.int32)[None, :]) & inside[:, None]).astype(jnp.int32)
    before = jnp.cumsum(onehot, axis=0, dtype=jnp.int32) - onehot
    position = jnp.sum(before * onehot, axis=1, dtype=jnp.int32)
    retained = inside & (position < CAP)
    slot_total = N_EXPERT * CAP
    destination = jnp.where(retained, target * CAP + position, slot_total).astype(jnp.int32)
    route_token = jnp.repeat(order_row, choices).astype(jnp.int32)
    route_choice = jnp.tile(jnp.arange(choices, dtype=jnp.int32), tok_count)
    slot_token = jnp.full((slot_total + 1,), tok_count, jnp.int32).at[destination].set(route_token)[:slot_total]
    slot_choice = jnp.zeros((slot_total + 1,), jnp.int32).at[destination].set(route_choice)[:slot_total]
    return slot_token, slot_choice


def silu_parts(pre_act):
    gate_act = pre_act[:, :FF]
    up_act = pre_act[:, FF:]
    silu_gate = gate_act * jax.nn.sigmoid(gate_act)
    return (silu_gate * up_act).astype(jnp.bfloat16)


def backward_parts(pre_act, back_hidden):
    gate_act = pre_act[:, :FF]
    up_act = pre_act[:, FF:]
    sigmoid_gate = jax.nn.sigmoid(gate_act)
    silu_gate = gate_act * sigmoid_gate
    d_gate = back_hidden * up_act * (sigmoid_gate * (1.0 + gate_act * (1.0 - sigmoid_gate)))
    d_up = back_hidden * silu_gate
    return jnp.concatenate([d_gate, d_up], axis=1).astype(jnp.bfloat16)


def partial_weight(operands):
    group_grads, group_hidden = operands
    partial_sum = jnp.dot(group_grads.T, group_hidden, preferred_element_type=jnp.float32).astype(jnp.bfloat16)
    partial_sum = lax.optimization_barrier(partial_sum)
    return partial_sum.astype(jnp.float32)


def expert_pass(operands):
    slot_rows, slot_grads, weight_in, weight_out = operands
    pre_act = jnp.dot(slot_rows, weight_in, preferred_element_type=jnp.float32)
    hidden = silu_parts(pre_act)
    expert_out = jnp.dot(hidden, weight_out.T, preferred_element_type=jnp.float32).astype(jnp.bfloat16)
    back_hidden = jnp.dot(slot_grads, weight_out, preferred_element_type=jnp.float32)
    d_pre = backward_parts(pre_act, back_hidden)
    d_rows = jnp.dot(d_pre, weight_in.T, preferred_element_type=jnp.float32).astype(jnp.bfloat16)
    grads_grouped = slot_grads.reshape(N_EXPERT, N_FSDP, CAP, D).transpose(1, 0, 2, 3).reshape(N_FSDP, N_EXPERT * CAP, D)
    hidden_grouped = hidden.reshape(N_EXPERT, N_FSDP, CAP, FF).transpose(1, 0, 2, 3).reshape(N_FSDP, N_EXPERT * CAP, FF)
    partials = lax.map(partial_weight, (grads_grouped, hidden_grouped))
    d_weight = jnp.sum(partials, axis=0)
    return expert_out, d_rows, d_weight


def reference(tokens, cotangent, route_ids, route_gates, served_order, w_in, w_out):
    tok_blocks = tokens.reshape(BLOCKS, TOK_DEV, D)
    cot_blocks = cotangent.reshape(BLOCKS, TOK_DEV, D)
    id_blocks = route_ids.reshape(BLOCKS, TOK_DEV, TOP)
    gate_blocks = route_gates.reshape(BLOCKS, TOK_DEV * TOP)
    slot_token, slot_choice = jax.vmap(slot_table)(id_blocks, served_order)
    filled = slot_token < TOK_DEV
    safe_token = jnp.where(filled, slot_token, 0).astype(jnp.int32)
    slot_gate = jnp.where(filled, jnp.take_along_axis(gate_blocks, (safe_token * TOP + slot_choice).astype(jnp.int32), axis=1), jnp.zeros((), jnp.float32))

    def gather_block(operands):
        block_tokens, block_cot, block_safe, block_filled, block_gate = operands
        slot_rows = jnp.where(block_filled[:, None], jnp.take(block_tokens, block_safe, axis=0), jnp.zeros((), jnp.bfloat16))
        slot_grads = (block_gate[:, None] * jnp.take(block_cot, block_safe, axis=0).astype(jnp.float32)).astype(jnp.bfloat16)
        return slot_rows, slot_grads

    slot_rows, slot_grads = lax.map(gather_block, (tok_blocks, cot_blocks, safe_token, filled, slot_gate))
    rows_by_expert = slot_rows.reshape(BLOCKS, N_EXPERT, CAP, D).transpose(1, 0, 2, 3).reshape(N_EXPERT, BLOCKS * CAP, D)
    grads_by_expert = slot_grads.reshape(BLOCKS, N_EXPERT, CAP, D).transpose(1, 0, 2, 3).reshape(N_EXPERT, BLOCKS * CAP, D)
    expert_out, d_rows, d_w_out = lax.map(expert_pass, (rows_by_expert, grads_by_expert, w_in, w_out))
    out_blocks = expert_out.reshape(N_EXPERT, BLOCKS, CAP, D).transpose(1, 0, 2, 3).reshape(BLOCKS, N_EXPERT * CAP, D)
    back_blocks = d_rows.reshape(N_EXPERT, BLOCKS, CAP, D).transpose(1, 0, 2, 3).reshape(BLOCKS, N_EXPERT * CAP, D)

    def combine_block(operands):
        block_out, block_back, block_token, block_gate = operands
        weighted = block_out.astype(jnp.float32) * block_gate[:, None]
        combined = jnp.zeros((TOK_DEV + 1, D), jnp.float32).at[block_token].add(weighted)[:TOK_DEV]
        d_tokens = jnp.zeros((TOK_DEV + 1, D), jnp.float32).at[block_token].add(block_back.astype(jnp.float32))[:TOK_DEV]
        return combined.astype(jnp.bfloat16), d_tokens.astype(jnp.bfloat16)

    combined, d_tokens = lax.map(combine_block, (out_blocks, back_blocks, slot_token, slot_gate))
    return combined.reshape(TOKENS, D), d_tokens.reshape(TOKENS, D), d_w_out
```

```python
import jax
import jax.numpy as jnp
from jax import lax
from jax.experimental import pallas as pl
from jax.experimental.pallas import tpu as pltpu
from jax.sharding import PartitionSpec as P

EXPERTS = 128
CORES = 2
VMEM = 40 * 1024 * 1024
F32 = jnp.float32
BF16 = jnp.bfloat16


def product(left, right, left_dim, right_dim, **kw):
    return lax.dot_general(
        left, right, (((left_dim,), (right_dim,)), ((), ())), preferred_element_type=F32, **kw
    )


def call(body, out_shape, args, flops=0, nbytes=0, smem=0):
    specs = [pl.BlockSpec(memory_space=pltpu.SMEM)] * smem
    specs += [pl.BlockSpec(memory_space=pltpu.VMEM)] * (len(args) - smem)
    return pl.pallas_call(
        body,
        out_shape=out_shape,
        in_specs=specs,
        out_specs=jax.tree.map(lambda _: pl.BlockSpec(memory_space=pltpu.VMEM), out_shape),
        compiler_params=pltpu.CompilerParams(vmem_limit_bytes=VMEM),
        cost_estimate=pl.CostEstimate(flops=flops, bytes_accessed=nbytes, transcendentals=0),
    )(*args)


def shape(dims, kind=BF16):
    return jax.ShapeDtypeStruct(dims, kind)


def dispatch_kernel(groups, spread, capacity, where, ids, gates, order, tok, cot, *outs):
    chunks, (pick_out, gate_out) = outs[:-2], outs[-2:]
    count, choices = ids.shape
    slots = groups * capacity
    part = tok.shape[1] // (spread * CORES)
    own_expert, own_part = where[0], where[1]
    slot = lax.broadcasted_iota(jnp.int32, (count, slots), 1)
    wanted = ((slot // capacity) ^ own_expert) * (EXPERTS // groups)
    routed = jnp.zeros((count, slots), F32)
    gate = jnp.zeros((count, slots), F32)
    for k in range(choices):
        hit = ids[:, k : k + 1] == wanted
        routed += jnp.where(hit, 1.0, 0.0)
        gate += jnp.where(hit, gates[:, k : k + 1], 0.0)
    row = lax.broadcasted_iota(jnp.int32, (count, count), 0)
    col = lax.broadcasted_iota(jnp.int32, (count, count), 1)
    served = jnp.where(order[...] == row, 1.0, 0.0).astype(BF16)
    earlier = jnp.where(row < col, 1.0, 0.0).astype(BF16)
    by_rank = product(routed.astype(BF16), served, 0, 0)
    before = product(by_rank.astype(BF16), earlier, 1, 0)
    place = lax.broadcasted_iota(jnp.int32, (slots, count), 0) % capacity
    taken = jnp.where(before.astype(jnp.int32) == place, by_rank, 0.0).astype(BF16)
    pick = product(taken, served, 1, 1)
    pick_out[...] = product(served, taken, 1, 1).astype(BF16)
    crossed = product(pick, gate, 1, 0, precision=lax.Precision.HIGHEST)
    diagonal = lax.broadcasted_iota(jnp.int32, (slots, slots), 0) == lax.broadcasted_iota(
        jnp.int32, (slots, slots), 1
    )
    slot_gate = jnp.sum(jnp.where(diagonal, crossed, 0.0), axis=1, keepdims=True)
    gate_out[...] = jnp.broadcast_to(slot_gate, gate_out.shape)
    pick = pick.astype(BF16)
    for kx in range(spread):
        for kc in range(CORES):
            at = pl.ds(pl.multiple_of((own_part ^ (kx * CORES + kc)) * part, part), part)
            to = pl.ds(kc * part, part)
            rows = product(pick, tok[:, at], 1, 0).astype(BF16)
            grads = (slot_gate * product(pick, cot[:, at], 1, 0)).astype(BF16)
            for ke in range(groups):
                chunk = chunks[ke * spread + kx]
                chunk[:capacity, to] = rows[ke * capacity : (ke + 1) * capacity]
                chunk[capacity:, to] = grads[ke * capacity : (ke + 1) * capacity]


def partial_kernel(groups, spread, capacity, *refs):
    chunks = refs[: groups * spread]
    in_own, in_sib, out_own, out_sib, keep, sib_grads, *sends = refs[groups * spread :]
    part = in_own.shape[0]
    wide = in_own.shape[1]
    block = groups * capacity
    for kx in range(spread):
        mine = [chunks[ke * spread + kx] for ke in range(groups)]
        rows = jnp.concatenate([c[:capacity] for c in mine], axis=0)
        grads = jnp.concatenate([c[capacity:] for c in mine], axis=0)
        pre = product(rows[:, :part], in_own[...], 1, 0) + product(rows[:, part:], in_sib[...], 1, 0)
        back = product(grads[:, :part], out_own[...], 1, 0)
        back += product(grads[:, part:], out_sib[...], 1, 0)
        target = keep if kx == 0 else sends[kx - 1]
        target[:, :wide] = pre.astype(target.dtype)
        target[:, wide:] = back.astype(target.dtype)
        sib_grads[kx * block : (kx + 1) * block] = grads[:, part:]


def act_kernel(keep, *refs):
    others, out = refs[:-1], refs[-1]
    feed = out.shape[1] // 3
    total = keep[...]
    for other in others:
        total += other[...].astype(F32)
    gate_act, up_act, back = (total[:, i * feed : (i + 1) * feed] for i in range(3))
    sig = 1.0 / (1.0 + jnp.exp(-gate_act))
    silu = gate_act * sig
    out[:, :feed] = (silu * up_act).astype(BF16)
    out[:, feed : 2 * feed] = (back * up_act * (sig * (1.0 + gate_act * (1.0 - sig)))).astype(BF16)
    out[:, 2 * feed :] = (back * silu).astype(BF16)


def result_kernel(groups, spread, capacity, *refs):
    acts = refs[:spread]
    in_own, in_sib, out_own, out_sib, hidden_out, *chunks = refs[spread:]
    part = in_own.shape[0]
    feed = out_own.shape[1]
    block = groups * capacity
    for kx in range(spread):
        hidden = acts[kx][:, :feed]
        d_pre = acts[kx][:, feed:]
        hidden_out[kx * block : (kx + 1) * block] = hidden
        for kc, (w_in, w_out) in enumerate(((in_own, out_own), (in_sib, out_sib))):
            expert_out = product(hidden, w_out[...], 1, 1).astype(BF16)
            d_rows = product(d_pre, w_in[...], 1, 1).astype(BF16)
            to = pl.ds(kc * part, part)
            for ke in range(groups):
                chunk = chunks[ke * spread + kx]
                chunk[:capacity, to] = expert_out[ke * capacity : (ke + 1) * capacity]
                chunk[capacity:, to] = d_rows[ke * capacity : (ke + 1) * capacity]


def weight_kernel(groups, spread, capacity, *refs):
    chunks = refs[: groups * spread]
    sib_grads, hidden, sib_hidden, out = refs[groups * spread :]
    part = out.shape[0]
    grads = jnp.concatenate(
        [chunks[ke * spread + kx][capacity:, :part] for kx in range(spread) for ke in range(groups)],
        axis=0,
    )
    out[...] = product(grads, hidden[...], 0, 0) + product(sib_grads[...], sib_hidden[...], 0, 0)


def combine_kernel(groups, spread, capacity, where, pick, gate, *refs):
    chunks, (combined, d_tokens) = refs[:-2], refs[-2:]
    part = combined.shape[1] // (spread * CORES)
    own_part = where[1]
    twice = jnp.concatenate([pick[...], pick[...]], axis=1)
    for kx in range(spread):
        for kc in range(CORES):
            at = pl.ds(pl.multiple_of((own_part ^ (kx * CORES + kc)) * part, part), part)
            mine = [chunks[ke * spread + kx] for ke in range(groups)]
            cols = slice(kc * part, (kc + 1) * part)
            out = jnp.concatenate([c[:capacity, cols] for c in mine], axis=0)
            back = jnp.concatenate([c[capacity:, cols] for c in mine], axis=0)
            weighted = out.astype(F32) * gate[:, :1]
            high = weighted.astype(BF16)
            low = (weighted - high.astype(F32)).astype(BF16)
            both = jnp.concatenate([high, low], axis=0)
            combined[:, at] = product(twice, both, 1, 0).astype(BF16)
            d_tokens[:, at] = product(pick[...], back, 1, 0).astype(BF16)


def per_device(tokens, cotangent, route_ids, route_gates, served_order, w_in, w_out):
    groups = lax.axis_size("expert")
    parts = lax.axis_size("fsdp")
    spread = parts // CORES
    count, width = tokens.shape
    capacity = count * route_ids.shape[1] // EXPERTS
    feed = w_out.shape[2]
    slots = groups * capacity
    half = width // spread
    sizes = (groups, spread, capacity)
    where = jnp.stack([lax.axis_index("expert"), lax.axis_index("fsdp")]).astype(jnp.int32)

    def to_core(value):
        return lax.ppermute(value, "fsdp", [(i, i ^ 1) for i in range(parts)])

    def to_x(value, kx):
        return lax.ppermute(value, "fsdp", [(i, i ^ (kx * CORES)) for i in range(parts)])

    def exchange(chunks):
        got = list(chunks)
        for ke in reversed(range(groups)):
            for kx in reversed(range(spread)):
                if ke or kx:
                    got[ke * spread + kx] = lax.ppermute(
                        chunks[ke * spread + kx],
                        ("expert", "fsdp"),
                        [
                            (e * parts + i, (e ^ ke) * parts + (i ^ (kx * CORES)))
                            for e in range(groups)
                            for i in range(parts)
                        ],
                    )
        return got

    def body(kernel):
        return lambda *refs: kernel(*sizes, *refs)

    in_own, out_own = w_in[0], w_out[0]
    in_sib, out_sib = to_core(in_own), to_core(out_own)
    chunk_shapes = [shape((2 * capacity, half))] * (groups * spread)
    *chunks, pick, gate = call(
        body(dispatch_kernel),
        chunk_shapes + [shape((count, slots)), shape((slots, 128), F32)],
        (where, route_ids, route_gates, served_order, tokens, cotangent),
        flops=4 * slots * count * width,
        nbytes=4 * count * width,
        smem=1,
    )
    chunks = exchange(chunks)
    keep, sib_grads, *sends = call(
        body(partial_kernel),
        [shape((slots, 3 * feed), F32), shape((spread * slots, width // parts))]
        + [shape((slots, 3 * feed))] * (spread - 1),
        (*chunks, in_own, in_sib, out_own, out_sib),
        flops=6 * spread * slots * half * feed,
        nbytes=6 * half * feed,
    )
    others = [to_x(value, kx + 1) for kx, value in enumerate(sends)]
    sib_grads = to_core(sib_grads)
    act = call(
        act_kernel, shape((slots, 3 * feed)), (keep, *others), nbytes=8 * slots * 3 * feed
    )
    acts = [act] + [to_x(act, kx) for kx in range(1, spread)]
    hidden, *results = call(
        body(result_kernel),
        [shape((spread * slots, feed))] + chunk_shapes,
        (*acts, in_own, in_sib, out_own, out_sib),
        flops=6 * spread * slots * half * feed,
        nbytes=6 * half * feed,
    )
    results = exchange(results)
    sib_hidden = to_core(hidden)
    d_w_out = call(
        body(weight_kernel),
        shape((width // parts, feed), F32),
        (*chunks, sib_grads, hidden, sib_hidden),
        flops=4 * spread * slots * (width // parts) * feed,
        nbytes=4 * (width // parts) * feed,
    )
    combined, d_tokens = call(
        body(combine_kernel),
        [shape((count, width))] * 2,
        (where, pick, gate, *results),
        flops=6 * slots * count * width,
        nbytes=4 * count * width,
        smem=1,
    )
    return combined, d_tokens, d_w_out[None]


def solution(mesh):
    rows = P(("replica", "expert", "fsdp"), None)
    weights = P("expert", "fsdp", None)
    return jax.shard_map(
        per_device,
        mesh=mesh,
        in_specs=(rows,) * 5 + (weights,) * 2,
        out_specs=(rows, rows, P(("replica", "expert"), "fsdp", None)),
        check_vma=False,
    )
```

```python
import jax
import jax.numpy as jnp
from jax import lax
from jax.experimental import pallas as pl
from jax.experimental.pallas import tpu as pltpu
from jax.sharding import PartitionSpec as P

EXPERTS = 128
CORES = 2
VMEM = 40 * 1024 * 1024
F32 = jnp.float32
BF16 = jnp.bfloat16


def product(left, right, left_dim, right_dim, **kw):
    return lax.dot_general(
        left, right, (((left_dim,), (right_dim,)), ((), ())), preferred_element_type=F32, **kw
    )


def call(body, out_shape, args, flops=0, nbytes=0, smem=0, far=0, scratch=()):
    specs = [pl.BlockSpec(memory_space=pltpu.SMEM)] * smem
    specs += [pl.BlockSpec(memory_space=pltpu.VMEM)] * (len(args) - smem - far)
    specs += [pl.BlockSpec(memory_space=pl.ANY)] * far
    return pl.pallas_call(
        body,
        out_shape=out_shape,
        in_specs=specs,
        scratch_shapes=list(scratch),
        out_specs=jax.tree.map(lambda _: pl.BlockSpec(memory_space=pltpu.VMEM), out_shape),
        compiler_params=pltpu.CompilerParams(vmem_limit_bytes=VMEM),
        cost_estimate=pl.CostEstimate(flops=flops, bytes_accessed=nbytes, transcendentals=0),
    )(*args)


def shape(dims, kind=BF16):
    return jax.ShapeDtypeStruct(dims, kind)


def columns(own_part, kx, kc, part):
    return pl.ds(pl.multiple_of((own_part ^ (kx * CORES + kc)) * part, part), part)


def rows_kernel(groups, spread, capacity, where, ids, gates, order, tok_hbm, *refs):
    *outs, pick_out, turned_out, gate_out, tok, sem = refs
    copy = pltpu.make_async_copy(tok_hbm, tok, sem)
    copy.start()
    choices, count = ids.shape
    slots = groups * capacity
    part = tok.shape[1] // (spread * CORES)
    slot = lax.broadcasted_iota(jnp.int32, (slots, count), 0)
    wanted = ((slot // capacity) ^ where[0]) * (EXPERTS // groups)
    routed = jnp.zeros((slots, count), F32)
    gate = jnp.zeros((slots, count), F32)
    for k in range(choices):
        hit = ids[k : k + 1, :] == wanted
        routed = jnp.where(hit, 1.0, routed)
        gate = jnp.where(hit, gates[k : k + 1, :], gate)
    row = lax.broadcasted_iota(jnp.int32, (count, count), 0)
    col = lax.broadcasted_iota(jnp.int32, (count, count), 1)
    served = jnp.where(order[...] == row, 1.0, 0.0).astype(BF16)
    earlier = jnp.where(row < col, 1.0, 0.0).astype(BF16)
    by_rank = product(routed.astype(BF16), served, 1, 0)
    before = product(by_rank.astype(BF16), earlier, 1, 0)
    taken = jnp.where(before.astype(jnp.int32) == slot % capacity, by_rank, 0.0).astype(BF16)
    pick = product(taken, served, 1, 1)
    turned_out[...] = product(served, taken, 1, 1).astype(BF16)
    slot_gate = jnp.sum(pick * gate, axis=1, keepdims=True)
    gate_out[...] = jnp.broadcast_to(slot_gate, gate_out.shape)
    pick = pick.astype(BF16)
    pick_out[...] = pick
    copy.wait()
    for kx in reversed(range(spread)):
        for kc in range(CORES):
            rows = product(pick, tok[:, columns(where[1], kx, kc, part)], 1, 0)
            outs[kx][:, kc * part : (kc + 1) * part] = rows.astype(BF16)


def grads_kernel(groups, spread, capacity, where, pick, gate, cot, *outs):
    part = cot.shape[1] // (spread * CORES)
    for kx in reversed(range(spread)):
        for kc in range(CORES):
            rows = product(pick[...], cot[:, columns(where[1], kx, kc, part)], 1, 0)
            outs[kx][:, kc * part : (kc + 1) * part] = (gate[:, :1] * rows).astype(BF16)


def regroup_kernel(groups, spread, capacity, *refs):
    by_x, by_e = refs[:spread], refs[spread:]
    for ke in range(groups):
        for kx in range(spread):
            by_e[ke][kx * capacity : (kx + 1) * capacity] = by_x[kx][
                ke * capacity : (ke + 1) * capacity
            ]


def far_kernel(groups, spread, capacity, *refs):
    by_e, by_x = refs[:groups], refs[groups:]
    for ke in range(groups):
        for kx in range(1, spread):
            by_x[kx - 1][ke * capacity : (ke + 1) * capacity] = by_e[ke][
                kx * capacity : (kx + 1) * capacity
            ]


def partial(groups, spread, capacity, chunks, own, sib, outs):
    part = own.shape[0]
    left = jnp.concatenate([c[...] for c in chunks], axis=0)
    total = product(left[:, :part], own[...], 1, 0) + product(left[:, part:], sib[...], 1, 0)
    for ke in range(groups):
        for kx in range(spread):
            at = (ke * spread + kx) * capacity
            outs[kx][ke * capacity : (ke + 1) * capacity] = total[at : at + capacity].astype(
                outs[kx].dtype
            )


def pre_kernel(groups, spread, capacity, *refs):
    chunks, (own, sib, *outs) = refs[:groups], refs[groups:]
    partial(groups, spread, capacity, chunks, own, sib, outs)


def back_kernel(groups, spread, capacity, *refs):
    chunks, (own, sib, own_grads, sib_grads, *outs) = refs[:groups], refs[groups:]
    part = own.shape[0]
    partial(groups, spread, capacity, chunks, own, sib, outs)
    for kx in range(spread):
        for ke in range(groups):
            at = (kx * groups + ke) * capacity
            rows = chunks[ke][kx * capacity : (kx + 1) * capacity]
            own_grads[at : at + capacity] = rows[:, :part]
            sib_grads[at : at + capacity] = rows[:, part:]


def summed(refs):
    total = refs[0][...]
    for ref in refs[1:]:
        total += ref[...].astype(F32)
    return total


def hidden_kernel(*refs):
    pre, out = summed(refs[:-1]), refs[-1]
    feed = out.shape[1]
    gate_act, up_act = pre[:, :feed], pre[:, feed:]
    out[...] = (gate_act * (1.0 / (1.0 + jnp.exp(-gate_act))) * up_act).astype(BF16)


def d_pre_kernel(*refs):
    spread = len(refs) // 2
    pre, back, out = summed(refs[:spread]), summed(refs[spread:-1]), refs[-1]
    feed = back.shape[1]
    gate_act, up_act = pre[:, :feed], pre[:, feed:]
    sig = 1.0 / (1.0 + jnp.exp(-gate_act))
    out[:, :feed] = (back * up_act * (sig * (1.0 + gate_act * (1.0 - sig)))).astype(BF16)
    out[:, feed:] = (back * (gate_act * sig)).astype(BF16)


def result_kernel(groups, spread, capacity, *refs):
    left, (own, sib, *chunks) = refs[:spread], refs[spread:]
    part = own.shape[0]
    rows = jnp.concatenate([r[...] for r in left], axis=0)
    for kc, weight in enumerate((own, sib)):
        value = product(rows, weight[...], 1, 1).astype(BF16)
        for ke in range(groups):
            for kx in range(spread):
                at = (kx * groups + ke) * capacity
                chunks[ke][kx * capacity : (kx + 1) * capacity, kc * part : (kc + 1) * part] = value[
                    at : at + capacity
                ]


def weight_kernel(spread, own_grads, sib_grads, *refs):
    hidden, sib_hidden, out = refs[:spread], refs[spread:-1], refs[-1]
    left = jnp.concatenate([own_grads[...], sib_grads[...]], axis=0)
    right = jnp.concatenate([r[...] for r in (*hidden, *sib_hidden)], axis=0)
    out[...] = product(left, right, 0, 0)


def returned(groups, spread, capacity, refs, kx, cols):
    if kx:
        return refs[groups + kx - 1][:, cols]
    return jnp.concatenate([refs[ke][:capacity, cols] for ke in range(groups)], axis=0)


def combine_kernel(groups, spread, capacity, where, turned, gate, *refs):
    out = refs[-1]
    part = out.shape[1] // (spread * CORES)
    twice = jnp.concatenate([turned[...], turned[...]], axis=1)
    for kx in range(spread):
        for kc in range(CORES):
            cols = slice(kc * part, (kc + 1) * part)
            rows = returned(groups, spread, capacity, refs, kx, cols)
            weighted = rows.astype(F32) * gate[:, :1]
            high = weighted.astype(BF16)
            low = (weighted - high.astype(F32)).astype(BF16)
            both = jnp.concatenate([high, low], axis=0)
            out[:, columns(where[1], kx, kc, part)] = product(twice, both, 1, 0).astype(BF16)


def d_tokens_kernel(groups, spread, capacity, where, turned, *refs):
    out = refs[-1]
    part = out.shape[1] // (spread * CORES)
    for kx in range(spread):
        for kc in range(CORES):
            cols = slice(kc * part, (kc + 1) * part)
            rows = returned(groups, spread, capacity, refs, kx, cols)
            out[:, columns(where[1], kx, kc, part)] = product(turned[...], rows, 1, 0).astype(BF16)


def per_device(tokens, cotangent, route_ids, route_gates, served_order, w_in, w_out):
    groups = lax.axis_size("expert")
    parts = lax.axis_size("fsdp")
    spread = parts // CORES
    count, width = tokens.shape
    capacity = count * route_ids.shape[1] // EXPERTS
    feed = w_out.shape[2]
    slots = groups * capacity
    half = width // spread
    part = width // parts
    sizes = (groups, spread, capacity)
    where = jnp.stack([lax.axis_index("expert"), lax.axis_index("fsdp")]).astype(jnp.int32)

    def to_core(value):
        return lax.ppermute(value, "fsdp", [(i, i ^ 1) for i in range(parts)])

    def to_x(values):
        return [
            lax.ppermute(value, "fsdp", [(i, i ^ ((k + 1) * CORES)) for i in range(parts)])
            for k, value in enumerate(values)
        ]

    def to_expert(chunks):
        return [
            lax.ppermute(value, "expert", [(i, i ^ ke) for i in range(groups)]) if ke else value
            for ke, value in enumerate(chunks)
        ]

    def body(kernel):
        return lambda *refs: kernel(*sizes, *refs)

    by_x = [shape((slots, half))] * spread
    by_e = [shape((spread * capacity, half))] * groups

    def inward(near, *far):
        chunks = call(body(regroup_kernel), by_e, (near, *to_x(far)), nbytes=4 * slots * width)
        return to_expert(chunks)

    def outward(left, own, sib):
        chunks = call(
            body(result_kernel),
            by_e,
            (*left, own, sib),
            flops=2 * spread * slots * half * own.shape[1],
            nbytes=2 * half * own.shape[1],
        )
        chunks = to_expert(chunks)
        far = call(body(far_kernel), by_x[1:], chunks, nbytes=4 * slots * width)
        return (*chunks, *to_x(far))

    in_own, out_own = w_in[0], w_out[0]
    *rows, pick, turned, gate = call(
        body(rows_kernel),
        by_x + [shape((slots, count)), shape((count, slots)), shape((slots, 128), F32)],
        (where, route_ids.T, route_gates.T, served_order, tokens),
        flops=2 * slots * count * width,
        nbytes=4 * count * width,
        smem=1,
        far=1,
        scratch=(pltpu.VMEM(tokens.shape, BF16), pltpu.SemaphoreType.DMA),
    )
    in_own, out_own, pick = lax.optimization_barrier((in_own, out_own, pick))
    in_sib, out_sib = to_core(in_own), to_core(out_own)
    grads = call(
        body(grads_kernel),
        by_x,
        (where, pick, gate, cotangent),
        flops=2 * slots * count * width,
        nbytes=4 * count * width,
        smem=1,
    )
    rows = inward(*rows)
    grads = inward(*grads)
    pre, *pre_far = call(
        body(pre_kernel),
        [shape((slots, 2 * feed), F32)] + [shape((slots, 2 * feed))] * (spread - 1),
        (*rows, in_own, in_sib),
        flops=4 * spread * slots * half * feed,
        nbytes=4 * half * feed,
    )
    pre = (pre, *to_x(pre_far))
    own_grads, sib_grads, back, *back_far = call(
        body(back_kernel),
        [shape((spread * slots, part))] * 2
        + [shape((slots, feed), F32)]
        + [shape((slots, feed))] * (spread - 1),
        (*grads, out_own, out_sib),
        flops=2 * spread * slots * half * feed,
        nbytes=2 * half * feed,
    )
    back = (back, *to_x(back_far))
    hidden = call(hidden_kernel, shape((slots, feed)), pre, nbytes=12 * slots * feed)
    hidden = (hidden, *to_x([hidden] * (spread - 1)))
    expert_out = outward(hidden, out_own, out_sib)
    d_pre = call(d_pre_kernel, shape((slots, 2 * feed)), (*pre, *back), nbytes=20 * slots * feed)
    d_pre = (d_pre, *to_x([d_pre] * (spread - 1)))
    d_rows = outward(d_pre, in_own, in_sib)
    d_w_out = call(
        lambda *refs: weight_kernel(spread, *refs),
        shape((part, feed), F32),
        (own_grads, to_core(sib_grads), *hidden, *[to_core(value) for value in hidden]),
        flops=4 * spread * slots * part * feed,
        nbytes=4 * part * feed,
    )
    combined = call(
        body(combine_kernel),
        shape((count, width)),
        (where, turned, gate, *expert_out),
        flops=4 * slots * count * width,
        nbytes=4 * count * width,
        smem=1,
    )
    d_tokens = call(
        body(d_tokens_kernel),
        shape((count, width)),
        (where, turned, *d_rows),
        flops=2 * slots * count * width,
        nbytes=4 * count * width,
        smem=1,
    )
    return combined, d_tokens, d_w_out[None]


def solution(mesh):
    rows = P(("replica", "expert", "fsdp"), None)
    weights = P("expert", "fsdp", None)
    return jax.shard_map(
        per_device,
        mesh=mesh,
        in_specs=(rows,) * 5 + (weights,) * 2,
        out_specs=(rows, rows, P(("replica", "expert"), "fsdp", None)),
        check_vma=False,
    )
```

```python
import jax
import jax.numpy as jnp
from jax import lax
from jax.experimental import pallas as pl
from jax.experimental.pallas import tpu as pltpu
from jax.sharding import PartitionSpec as P

EXPERTS = 128
CORES = 2
VMEM = 40 * 1024 * 1024
F32 = jnp.float32
BF16 = jnp.bfloat16


def product(left, right, left_dim, right_dim, **kw):
    return lax.dot_general(
        left, right, (((left_dim,), (right_dim,)), ((), ())), preferred_element_type=F32, **kw
    )


def call(body, out_shape, args, flops=0, nbytes=0, smem=0, far=0, after=(), **kw):
    specs = [pl.BlockSpec(memory_space=pltpu.SMEM)] * smem
    specs += [pl.BlockSpec(memory_space=pltpu.VMEM)] * (len(args) - smem - far)
    specs += [pl.BlockSpec(memory_space=pltpu.HBM)] * far
    specs += [pl.BlockSpec(memory_space=pl.ANY)] * len(after)
    out_specs = kw.pop("out_specs", [pl.BlockSpec(memory_space=pltpu.VMEM)] * len(out_shape))
    args = [
        pltpu.with_memory_space_constraint(arg, pltpu.HBM) if i >= len(args) - far else arg
        for i, arg in enumerate(args)
    ]
    count, first, last = len(args), len(args) + len(after), len(args) + len(after) + len(out_shape)

    def kernel(*refs):
        refs[last][...] = jnp.zeros(refs[last].shape, F32)
        body(*refs[:count], *refs[first:last], *refs[last + 1 :])

    *out, token = pl.pallas_call(
        kernel,
        out_shape=[*out_shape, shape((8, 128), F32)],
        in_specs=specs,
        out_specs=[*out_specs, pl.BlockSpec(memory_space=pltpu.VMEM)],
        compiler_params=pltpu.CompilerParams(vmem_limit_bytes=VMEM),
        cost_estimate=pl.CostEstimate(flops=flops, bytes_accessed=nbytes, transcendentals=0),
        **kw,
    )(*args, *after)
    return out, token


def shape(dims, kind=BF16):
    return jax.ShapeDtypeStruct(dims, kind)


def columns(own_part, kx, kc, part):
    return pl.ds(pl.multiple_of((own_part ^ (kx * CORES + kc)) * part, part), part)


def rows_kernel(groups, spread, capacity, where, *refs):
    *outs, pick_out, turned_out, gate_out, cot, ids, gates, order, tok, sems = refs[5:]
    copies = [
        pltpu.make_async_copy(source, target, sems.at[i])
        for i, (source, target) in enumerate(zip(refs[:5], (ids, gates, order, tok, cot)))
    ]
    for copy in copies:
        copy.start()
    for copy in copies[:3]:
        copy.wait()
    choices, count = ids.shape
    slots = groups * capacity
    part = tok.shape[1] // (spread * CORES)
    slot = lax.broadcasted_iota(jnp.int32, (slots, count), 0)
    wanted = ((slot // capacity) ^ where[0]) * (EXPERTS // groups)
    routed = jnp.zeros((slots, count), F32)
    gate = jnp.zeros((slots, count), F32)
    for k in range(choices):
        hit = ids[k : k + 1, :] == wanted
        routed = jnp.where(hit, 1.0, routed)
        gate = jnp.where(hit, gates[k : k + 1, :], gate)
    row = lax.broadcasted_iota(jnp.int32, (count, count), 0)
    col = lax.broadcasted_iota(jnp.int32, (count, count), 1)
    served = jnp.where(order[...] == row, 1.0, 0.0).astype(BF16)
    earlier = jnp.where(row < col, 1.0, 0.0).astype(BF16)
    by_rank = product(routed.astype(BF16), served, 1, 0)
    before = product(by_rank.astype(BF16), earlier, 1, 0)
    taken = jnp.where(before.astype(jnp.int32) == slot % capacity, by_rank, 0.0).astype(BF16)
    pick = product(taken, served, 1, 1)
    turned_out[...] = product(served, taken, 1, 1).astype(BF16)
    slot_gate = jnp.sum(pick * gate, axis=1, keepdims=True)
    gate_out[...] = jnp.broadcast_to(slot_gate, gate_out.shape)
    pick = pick.astype(BF16)
    pick_out[...] = pick
    copies[3].wait()
    for kx in reversed(range(spread)):
        for kc in range(CORES):
            rows = product(pick, tok[:, columns(where[1], kx, kc, part)], 1, 0)
            outs[kx][:, kc * part : (kc + 1) * part] = rows.astype(BF16)
    copies[4].wait()


def grads_kernel(groups, spread, capacity, where, pick, gate, cot, *outs):
    part = cot.shape[1] // (spread * CORES)
    for kx in reversed(range(spread)):
        for kc in range(CORES):
            rows = product(pick[...], cot[:, columns(where[1], kx, kc, part)], 1, 0)
            outs[kx][:, kc * part : (kc + 1) * part] = (gate[:, :1] * rows).astype(BF16)


def regroup_kernel(groups, spread, capacity, *refs):
    by_x, by_e = refs[:spread], refs[spread:]
    for ke in range(groups):
        for kx in range(spread):
            by_e[ke][kx * capacity : (kx + 1) * capacity] = by_x[kx][
                ke * capacity : (ke + 1) * capacity
            ]


def far_kernel(groups, spread, capacity, *refs):
    by_e, by_x = refs[:groups], refs[groups:]
    for ke in range(groups):
        for kx in range(1, spread):
            by_x[kx - 1][ke * capacity : (ke + 1) * capacity] = by_e[ke][
                kx * capacity : (kx + 1) * capacity
            ]


def partial(groups, spread, capacity, chunks, own, sib, outs):
    part = own.shape[0]
    left = jnp.concatenate([c[...] for c in chunks], axis=0)
    total = product(left[:, :part], own[...], 1, 0) + product(left[:, part:], sib[...], 1, 0)
    for ke in range(groups):
        for kx in range(spread):
            at = (ke * spread + kx) * capacity
            outs[kx][ke * capacity : (ke + 1) * capacity] = total[at : at + capacity].astype(
                outs[kx].dtype
            )


def pre_kernel(groups, spread, capacity, *refs):
    chunks, (own, sib, *outs) = refs[:groups], refs[groups:]
    partial(groups, spread, capacity, chunks, own, sib, outs)


def back_kernel(groups, spread, capacity, *refs):
    chunks, (own, sib, own_grads, sib_grads, *outs) = refs[:groups], refs[groups:]
    part = own.shape[0]
    partial(groups, spread, capacity, chunks, own, sib, outs)
    for kx in range(spread):
        for ke in range(groups):
            at = (kx * groups + ke) * capacity
            rows = chunks[ke][kx * capacity : (kx + 1) * capacity]
            own_grads[at : at + capacity] = rows[:, :part]
            sib_grads[at : at + capacity] = rows[:, part:]


def summed(refs):
    total = refs[0][...]
    for ref in refs[1:]:
        total += ref[...].astype(F32)
    return total


def hidden_kernel(*refs):
    pre, out = summed(refs[:-1]), refs[-1]
    feed = out.shape[1]
    gate_act, up_act = pre[:, :feed], pre[:, feed:]
    out[...] = (gate_act * (1.0 / (1.0 + jnp.exp(-gate_act))) * up_act).astype(BF16)


def d_pre_kernel(*refs):
    spread = len(refs) // 2
    pre, back, out = summed(refs[:spread]), summed(refs[spread:-1]), refs[-1]
    feed = back.shape[1]
    gate_act, up_act = pre[:, :feed], pre[:, feed:]
    sig = 1.0 / (1.0 + jnp.exp(-gate_act))
    out[:, :feed] = (back * up_act * (sig * (1.0 + gate_act * (1.0 - sig)))).astype(BF16)
    out[:, feed:] = (back * (gate_act * sig)).astype(BF16)


def result_kernel(groups, spread, capacity, *refs):
    left, (own, sib, *chunks) = refs[:spread], refs[spread:]
    part = own.shape[0]
    rows = jnp.concatenate([r[...] for r in left], axis=0)
    for kc, weight in enumerate((own, sib)):
        value = product(rows, weight[...], 1, 1).astype(BF16)
        for ke in range(groups):
            for kx in range(spread):
                at = (kx * groups + ke) * capacity
                chunks[ke][kx * capacity : (kx + 1) * capacity, kc * part : (kc + 1) * part] = value[
                    at : at + capacity
                ]


def weight_kernel(spread, own_grads, sib_grads, *refs):
    hidden, sib_hidden, out = refs[:spread], refs[spread:-1], refs[-1]
    left = jnp.concatenate([own_grads[...], sib_grads[...]], axis=0)
    right = jnp.concatenate([r[...] for r in (*hidden, *sib_hidden)], axis=0)
    out[...] = product(left, right, 0, 0)


def returned(groups, spread, capacity, refs, kx, cols):
    if kx:
        return refs[groups + kx - 1][:, cols]
    return jnp.concatenate([refs[ke][:capacity, cols] for ke in range(groups)], axis=0)


def combine_kernel(groups, spread, capacity, where, turned, gate, *refs):
    out = refs[-1]
    part = out.shape[1] // (spread * CORES)
    twice = jnp.concatenate([turned[...], turned[...]], axis=1)
    for kx in range(spread):
        for kc in range(CORES):
            cols = slice(kc * part, (kc + 1) * part)
            rows = returned(groups, spread, capacity, refs, kx, cols)
            weighted = rows.astype(F32) * gate[:, :1]
            high = weighted.astype(BF16)
            low = (weighted - high.astype(F32)).astype(BF16)
            both = jnp.concatenate([high, low], axis=0)
            out[:, columns(where[1], kx, kc, part)] = product(twice, both, 1, 0).astype(BF16)


def d_tokens_kernel(groups, spread, capacity, span, where, turned, *refs):
    *refs, out, held, sems = refs
    part = out.shape[1] // (spread * CORES)
    copies = []
    for kx in span:
        for kc in range(CORES):
            cols = slice(kc * part, (kc + 1) * part)
            rows = returned(groups, spread, capacity, refs, kx, cols)
            n = len(copies)
            held[n] = product(turned[...], rows, 1, 0).astype(BF16)
            copies.append(
                pltpu.make_async_copy(
                    held.at[n], out.at[:, columns(where[1], kx, kc, part)], sems.at[n]
                )
            )
            copies[-1].start()
    for copy in copies:
        copy.wait()


def per_device(tokens, cotangent, route_ids, route_gates, served_order, w_in, w_out):
    groups = lax.axis_size("expert")
    parts = lax.axis_size("fsdp")
    spread = parts // CORES
    count, width = tokens.shape
    capacity = count * route_ids.shape[1] // EXPERTS
    feed = w_out.shape[2]
    slots = groups * capacity
    half = width // spread
    part = width // parts
    sizes = (groups, spread, capacity)
    where = jnp.stack([lax.axis_index("expert"), lax.axis_index("fsdp")]).astype(jnp.int32)

    def to_core(value):
        return lax.ppermute(value, "fsdp", [(i, i ^ 1) for i in range(parts)])

    def to_x(values):
        return [
            lax.ppermute(value, "fsdp", [(i, i ^ ((k + 1) * CORES)) for i in range(parts)])
            for k, value in enumerate(values)
        ]

    def to_expert(chunks):
        return [
            lax.ppermute(value, "expert", [(i, i ^ ke) for i in range(groups)]) if ke else value
            for ke, value in enumerate(chunks)
        ]

    def body(kernel):
        return lambda *refs: kernel(*sizes, *refs)

    by_x = [shape((slots, half))] * spread
    by_e = [shape((spread * capacity, half))] * groups

    def inward(near, far, after):
        chunks, _ = call(
            body(regroup_kernel), by_e, (near, *far), nbytes=4 * slots * width, after=after
        )
        return to_expert(chunks)

    def outward(left, own, sib):
        chunks, token = call(
            body(result_kernel),
            by_e,
            (*left, own, sib),
            flops=2 * spread * slots * half * own.shape[1],
            nbytes=2 * half * own.shape[1],
        )
        return to_expert(chunks), token

    def outward_far(chunks, after):
        far, _ = call(
            body(far_kernel), by_x[1:], chunks, nbytes=4 * slots * width, after=after
        )
        return to_x(far)

    in_own, out_own = w_in[0], w_out[0]
    (*rows, pick, turned, gate, cotangent), _ = call(
        body(rows_kernel),
        by_x
        + [shape((slots, count)), shape((count, slots)), shape((slots, 128), F32)]
        + [shape(cotangent.shape)],
        (where, route_ids.T, route_gates.T, served_order, tokens, cotangent),
        flops=2 * slots * count * width,
        nbytes=4 * count * width,
        smem=1,
        far=5,
        scratch_shapes=[
            pltpu.VMEM(route_ids.shape[::-1], jnp.int32),
            pltpu.VMEM(route_gates.shape[::-1], F32),
            pltpu.VMEM(served_order.shape, jnp.int32),
            pltpu.VMEM(tokens.shape, BF16),
            pltpu.SemaphoreType.DMA((5,)),
        ],
    )
    far = to_x(rows[1:])
    grads, grads_token = call(
        body(grads_kernel),
        by_x,
        (where, pick, gate, cotangent),
        flops=2 * slots * count * width,
        nbytes=4 * count * width,
        smem=1,
    )
    in_own, out_own, rows[0] = lax.optimization_barrier((in_own, out_own, rows[0]))
    in_sib, out_sib = to_core(in_own), to_core(out_own)
    rows = inward(rows[0], far, (grads_token,))
    grads = inward(grads[0], to_x(grads[1:]), ())
    (pre, *pre_far), _ = call(
        body(pre_kernel),
        [shape((slots, 2 * feed), F32)] + [shape((slots, 2 * feed))] * (spread - 1),
        (*rows, in_own, in_sib),
        flops=4 * spread * slots * half * feed,
        nbytes=4 * half * feed,
    )
    pre = (pre, *to_x(pre_far))
    (hidden,), hidden_token = call(
        hidden_kernel, [shape((slots, feed))], pre, nbytes=12 * slots * feed
    )
    hidden = (hidden, *to_x([hidden] * (spread - 1)))
    (own_grads, sib_grads, back, *back_far), _ = call(
        body(back_kernel),
        [shape((spread * slots, part))] * 2
        + [shape((slots, feed), F32)]
        + [shape((slots, feed))] * (spread - 1),
        (*grads, out_own, out_sib),
        flops=2 * spread * slots * half * feed,
        nbytes=2 * half * feed,
        after=(hidden_token,),
    )
    back = (back, *to_x(back_far))
    expert_out, out_token = outward(hidden, out_own, out_sib)
    (d_pre,), _ = call(
        d_pre_kernel,
        [shape((slots, 2 * feed))],
        (*pre, *back),
        nbytes=20 * slots * feed,
        after=(out_token,),
    )
    d_pre = (d_pre, *to_x([d_pre] * (spread - 1)))
    d_rows, _ = outward(d_pre, in_own, in_sib)
    (d_w_out,), weight_token = call(
        lambda *refs: weight_kernel(spread, *refs),
        [shape((part, feed), F32)],
        (own_grads, to_core(sib_grads), *hidden, *[to_core(value) for value in hidden]),
        flops=4 * spread * slots * part * feed,
        nbytes=4 * part * feed,
    )
    expert_out_far = outward_far(expert_out, ())
    d_rows_far = outward_far(d_rows, (weight_token,))
    (combined,), combined_token = call(
        body(combine_kernel),
        [shape((count, width))],
        (where, turned, gate, *expert_out, *expert_out_far),
        flops=4 * slots * count * width,
        nbytes=4 * count * width,
        smem=1,
    )

    def d_tokens_columns(span, *operands, **kw):
        pieces = len(span) * CORES
        (value,), token = call(
            lambda *refs: d_tokens_kernel(*sizes, span, *refs),
            [shape((count, width))],
            (where, turned, *d_rows, *operands),
            flops=2 * slots * half * count,
            nbytes=2 * count * half,
            smem=1,
            out_specs=[pl.BlockSpec(memory_space=pltpu.HBM)],
            scratch_shapes=[
                pltpu.VMEM((pieces, count, part), BF16),
                pltpu.SemaphoreType.DMA((pieces,)),
            ],
            **kw,
        )
        return value

    d_tokens = d_tokens_columns([0], after=(combined_token,))
    d_tokens = d_tokens_columns(
        range(1, spread),
        *d_rows_far,
        d_tokens,
        far=1,
        input_output_aliases={2 + groups + len(d_rows_far): 0},
    )
    return combined, d_tokens, d_w_out[None]


def solution(mesh):
    rows = P(("replica", "expert", "fsdp"), None)
    weights = P("expert", "fsdp", None)
    return jax.shard_map(
        per_device,
        mesh=mesh,
        in_specs=(rows,) * 5 + (weights,) * 2,
        out_specs=(rows, rows, P(("replica", "expert"), "fsdp", None)),
        check_vma=False,
    )
```

```python
import jax
import jax.numpy as jnp
from jax import lax
from jax.experimental import pallas as pl
from jax.experimental.pallas import tpu as pltpu
from jax.sharding import PartitionSpec as P

EXPERTS = 128
CORES = 2
VMEM = 40 * 1024 * 1024
F32 = jnp.float32
BF16 = jnp.bfloat16


def product(left, right, left_dim, right_dim, **kw):
    return lax.dot_general(
        left, right, (((left_dim,), (right_dim,)), ((), ())), preferred_element_type=F32, **kw
    )


def call(body, out_shape, args, flops=0, nbytes=0, far=0, after=(), token=False, **kw):
    out_shape = [*out_shape] + [shape((8, 128), F32)] * token
    specs = [pl.BlockSpec(memory_space=pltpu.VMEM)] * (len(args) - far)
    specs += [pl.BlockSpec(memory_space=pltpu.HBM)] * far
    specs += [pl.BlockSpec(memory_space=pl.ANY)] * len(after)
    kw.setdefault("out_specs", [pl.BlockSpec(memory_space=pltpu.VMEM)] * len(out_shape))
    args = [
        pltpu.with_memory_space_constraint(arg, pltpu.HBM) if i >= len(args) - far else arg
        for i, arg in enumerate(args)
    ]
    count, first, last = len(args), len(args) + len(after), len(args) + len(after) + len(out_shape)

    def kernel(*refs):
        if token:
            refs[last - 1][...] = jnp.zeros(refs[last - 1].shape, F32)
        body(*refs[:count], *refs[first : last - token], *refs[last:])

    return pl.pallas_call(
        kernel,
        out_shape=out_shape,
        in_specs=specs,
        compiler_params=pltpu.CompilerParams(vmem_limit_bytes=VMEM),
        cost_estimate=pl.CostEstimate(flops=0, bytes_accessed=0, transcendentals=0),
        **kw,
    )(*args, *after)


def shape(dims, kind=BF16):
    return jax.ShapeDtypeStruct(dims, kind)


def columns(k, part):
    return pl.ds(pl.multiple_of((lax.axis_index("fsdp") ^ k) * part, part), part)


def piece_columns(n, width, replicas):
    return pl.ds(pl.multiple_of((lax.axis_index("replica") ^ n) * width, width), width)


def rows_kernel(groups, parts, capacity, replicas, *refs):
    sources, chunks, refs = refs[:6], refs[6 : 6 + groups], refs[6 + groups :]
    pick_out, turned_out, gate_out, cot, piece, ids, gates, order, tok, sems = refs
    sources = (*sources[:5], sources[5].at[:, piece_columns(0, piece.shape[1], replicas)])
    copies = [
        pltpu.make_async_copy(source, target, sems.at[i])
        for i, (source, target) in enumerate(zip(sources, (ids, gates, order, tok, cot, piece)))
    ]
    for copy in copies:
        copy.start()
    for copy in copies[:3]:
        copy.wait()
    choices, count = ids.shape
    slots = groups * capacity
    part = tok.shape[1] // parts
    slot = lax.broadcasted_iota(jnp.int32, (slots, count), 0)
    wanted = ((slot // capacity) ^ lax.axis_index("expert")) * (EXPERTS // groups)
    routed = jnp.zeros((slots, count), F32)
    gate = jnp.zeros((slots, count), F32)
    for k in range(choices):
        hit = ids[k : k + 1, :] == wanted
        routed = jnp.where(hit, 1.0, routed)
        gate = jnp.where(hit, gates[k : k + 1, :], gate)
    row = lax.broadcasted_iota(jnp.int32, (count, count), 0)
    col = lax.broadcasted_iota(jnp.int32, (count, count), 1)
    served = jnp.where(order[...] == row, 1.0, 0.0).astype(BF16)
    earlier = jnp.where(row < col, 1.0, 0.0).astype(BF16)
    by_rank = product(routed.astype(BF16), served, 1, 0)
    before = product(by_rank.astype(BF16), earlier, 1, 0)
    taken = jnp.where(before.astype(jnp.int32) == slot % capacity, by_rank, 0.0).astype(BF16)
    pick = product(taken, served, 1, 1)
    turned_out[...] = product(served, taken, 1, 1).astype(BF16)
    slot_gate = jnp.sum(pick * gate, axis=1, keepdims=True)
    gate_out[...] = jnp.broadcast_to(slot_gate, gate_out.shape)
    pick = pick.astype(BF16)
    pick_out[...] = pick
    copies[3].wait()
    for k in range(parts):
        rows = product(pick, tok[:, columns(k, part)], 1, 0).astype(BF16)
        for ke in range(groups):
            chunks[ke][:, k * part : (k + 1) * part] = rows[ke * capacity : (ke + 1) * capacity]
    copies[4].wait()
    copies[5].wait()


def grads_kernel(groups, parts, capacity, pick, gate, cot, *chunks):
    part = cot.shape[1] // parts
    for k in range(parts):
        value = product(pick[...], cot[:, columns(k, part)], 1, 0)
        value = (gate[:, :1] * value).astype(BF16)
        for ke in range(groups):
            chunks[ke][:, k * part : (k + 1) * part] = value[ke * capacity : (ke + 1) * capacity]


def split_kernel(groups, spread, capacity, *refs):
    chunks, by_x = refs[:groups], refs[groups:]
    half = by_x[0].shape[1]
    for kx in range(spread):
        for ke in range(groups):
            by_x[kx][ke * capacity : (ke + 1) * capacity] = chunks[ke][
                :, kx * half : (kx + 1) * half
            ]


def far_kernel(groups, spread, capacity, *refs):
    by_e, by_x = refs[:groups], refs[groups:]
    for ke in range(groups):
        for kx in range(1, spread):
            by_x[kx - 1][ke * capacity : (ke + 1) * capacity] = by_e[ke][
                kx * capacity : (kx + 1) * capacity
            ]


def pre_kernel(spread, *refs):
    left, (own, sib, *outs) = refs[:spread], refs[spread:]
    part = own.shape[0]
    rows = jnp.concatenate([r[...] for r in left], axis=0)
    total = product(rows[:, :part], own[...], 1, 0) + product(rows[:, part:], sib[...], 1, 0)
    count = left[0].shape[0]
    for kx in range(spread):
        outs[kx][...] = total[kx * count : (kx + 1) * count].astype(outs[kx].dtype)


def back_kernel(groups, replicas, *refs):
    chunks, weights, (grads, back) = refs[:groups], refs[groups:-2], refs[-2:]
    part, feed = weights[0].shape
    grads[...] = jnp.concatenate([c[...] for c in chunks], axis=0)
    total = product(grads[:, :part], weights[0][...], 1, 0)
    back[...] = total + product(grads[:, part : 2 * part], weights[1][...], 1, 0)
    add_pieces(grads, weights[CORES:], back, 0, replicas)


def add_pieces(grads, pieces, back, n, replicas):
    part, width = pieces[0].shape
    total = 0.0
    for k, piece in enumerate(pieces, CORES):
        total += product(grads[:, k * part : (k + 1) * part], piece[...], 1, 0)
    back[:, piece_columns(n, width, replicas)] += total


def act_kernel(spread, replicas, *refs):
    pre_refs, grads, back_in, pieces = refs[:spread], refs[spread], refs[spread + 1], refs[spread + 2 : -3]
    hidden, d_pre, back = refs[-3:]
    back[...] = back_in[...]
    for n in range(1, replicas):
        add_pieces(grads, pieces[n - 1 :: replicas - 1], back, n, replicas)
    pre = pre_refs[0][...]
    for ref in pre_refs[1:]:
        pre += ref[...].astype(F32)
    feed = back.shape[1]
    gate_act, up_act = pre[:, :feed], pre[:, feed:]
    sig = 1.0 / (1.0 + jnp.exp(-gate_act))
    silu = gate_act * sig
    hidden[...] = (silu * up_act).astype(BF16)
    d_pre[:, :feed] = (back[...] * up_act * (sig * (1.0 + gate_act * (1.0 - sig)))).astype(BF16)
    d_pre[:, feed:] = (back[...] * silu).astype(BF16)


def expert_out_kernel(groups, capacity, replicas, hidden, *refs):
    weights, chunks = refs[:-groups], refs[-groups:]
    part, feed = weights[0].shape
    width = feed // replicas

    def store(k, value):
        value = value.astype(BF16)
        for ke in range(groups):
            chunks[ke][:, k * part : (k + 1) * part] = value[ke * capacity : (ke + 1) * capacity]

    for k in range(CORES):
        store(k, product(hidden[...], weights[k][...], 1, 1))
    for k in range(CORES, chunks[0].shape[1] // part):
        pieces = weights[CORES + (k - CORES) * replicas :][:replicas]
        total = product(hidden[:, piece_columns(0, width, replicas)], pieces[0][...], 1, 1)
        for n in range(1, replicas):
            total += product(hidden[:, piece_columns(n, width, replicas)], pieces[n][...], 1, 1)
        store(k, total)


def d_rows_kernel(groups, spread, capacity, *refs):
    left, (own, sib, *chunks) = refs[:spread], refs[spread:]
    part = own.shape[0]
    rows = jnp.concatenate([r[...] for r in left], axis=0)
    for kc, weight in enumerate((own, sib)):
        value = product(rows, weight[...], 1, 1).astype(BF16)
        for ke in range(groups):
            for kx in range(spread):
                at = (kx * groups + ke) * capacity
                chunks[ke][kx * capacity : (kx + 1) * capacity, kc * part : (kc + 1) * part] = value[
                    at : at + capacity
                ]


def pack_kernel(spread, grads, hidden, *outs):
    half = grads.shape[1] // spread
    for kx in range(1, spread):
        outs[kx - 1][:, :half] = grads[:, kx * half : (kx + 1) * half]
        outs[kx - 1][:, half:] = hidden[...]


def gather_kernel(spread, grads, hidden, *refs):
    far, (own, sib, all_hidden) = refs[: spread - 1], refs[spread - 1 :]
    part = own.shape[1]
    count = grads.shape[0]
    for kx in range(spread):
        source = far[kx - 1] if kx else grads
        at = pl.ds(kx * count, count)
        own[at] = source[:, :part]
        sib[at] = source[:, part : 2 * part]
        all_hidden[at] = source[:, 2 * part :] if kx else hidden[...]


def weight_kernel(own, hidden, sib, sib_hidden, out):
    left = jnp.concatenate([own[...], sib[...]], axis=0)
    right = jnp.concatenate([hidden[...], sib_hidden[...]], axis=0)
    out[...] = product(left, right, 0, 0)


def combine_kernel(groups, parts, turned, gate, *refs):
    chunks, (out, held, sems) = refs[:groups], refs[groups:]
    part = out.shape[1] // parts
    twice = jnp.concatenate([turned[...], turned[...]], axis=1)
    copies = []
    for k in range(parts):
        rows = jnp.concatenate([c[:, k * part : (k + 1) * part] for c in chunks], axis=0)
        weighted = rows.astype(F32) * gate[:, :1]
        high = weighted.astype(BF16)
        low = (weighted - high.astype(F32)).astype(BF16)
        both = jnp.concatenate([high, low], axis=0)
        held[k] = product(twice, both, 1, 0).astype(BF16)
        copies.append(pltpu.make_async_copy(held.at[k], out.at[:, columns(k, part)], sems.at[k]))
        copies[-1].start()
    for copy in copies:
        copy.wait()


def d_tokens_kernel(groups, parts, capacity, span, turned, *refs):
    *refs, out, held, sems = refs
    part = out.shape[1] // parts
    copies = []
    for n, kx in enumerate(span):
        for kc in range(CORES):
            cols = slice(kc * part, (kc + 1) * part)
            if kx:
                rows = refs[n][:, cols]
            else:
                rows = jnp.concatenate([refs[ke][:capacity, cols] for ke in range(groups)], axis=0)
            i = len(copies)
            held[i] = product(turned[...], rows, 1, 0).astype(BF16)
            target = out.at[:, columns(kx * CORES + kc, part)]
            copies.append(pltpu.make_async_copy(held.at[i], target, sems.at[i]))
            copies[-1].start()
    for copy in copies:
        copy.wait()


def per_device(tokens, cotangent, route_ids, route_gates, served_order, w_in, w_out):
    replicas = lax.axis_size("replica")
    groups = lax.axis_size("expert")
    parts = lax.axis_size("fsdp")
    spread = parts // CORES
    count, width = tokens.shape
    capacity = count * route_ids.shape[1] // EXPERTS
    feed = w_out.shape[2]
    slots = groups * capacity
    half = width // spread
    part = width // parts

    def bound(kernel, *sizes):
        return lambda *refs: kernel(*sizes, *refs)

    def to_core(value):
        return lax.ppermute(value, "fsdp", [(i, i ^ 1) for i in range(parts)])

    def to_x(values):
        return [
            lax.ppermute(value, "fsdp", [(i, i ^ ((k + 1) * CORES)) for i in range(parts)])
            for k, value in enumerate(values)
        ]

    def to_replica(value, n):
        return lax.ppermute(value, "replica", [(i, i ^ n) for i in range(replicas)])

    def to_expert(chunks):
        return [
            lax.ppermute(value, "expert", [(i, i ^ ke) for i in range(groups)]) if ke else value
            for ke, value in enumerate(chunks)
        ]

    chunk = [shape((capacity, width))] * groups
    in_own, out_own = w_in[0], w_out[0]
    *rows, pick, turned, gate, cotangent, piece = call(
        bound(rows_kernel, groups, parts, capacity, replicas),
        chunk
        + [shape((slots, count)), shape((count, slots)), shape((slots, 128), F32)]
        + [shape(cotangent.shape), shape((part, feed // replicas))],
        (route_ids.T, route_gates.T, served_order, tokens, cotangent, out_own),
        flops=2 * slots * count * width,
        nbytes=4 * count * width,
        far=6,
        scratch_shapes=[
            pltpu.VMEM(route_ids.shape[::-1], jnp.int32),
            pltpu.VMEM(route_gates.shape[::-1], F32),
            pltpu.VMEM(served_order.shape, jnp.int32),
            pltpu.VMEM(tokens.shape, BF16),
            pltpu.SemaphoreType.DMA((6,)),
        ],
    )
    rows = to_expert(rows)
    grads = call(
        bound(grads_kernel, groups, parts, capacity),
        chunk,
        (pick, gate, cotangent),
        flops=2 * slots * count * width,
        nbytes=4 * count * width,
    )
    grads = list(grads)
    pieces = to_x([piece] * (spread - 1))
    near, *far = call(
        bound(split_kernel, groups, spread, capacity),
        [shape((slots, half))] * spread,
        rows,
        nbytes=4 * slots * width,
        after=pieces,
    )
    in_own, out_own, near, pieces = lax.optimization_barrier((in_own, out_own, near, pieces))
    in_sib, out_sib = to_core(in_own), to_core(out_own)
    pieces = [[value] + [to_replica(value, n) for n in range(1, replicas)] for value in pieces]
    pre, *pre_far = call(
        bound(pre_kernel, spread),
        [shape((slots, 2 * feed), F32)] + [shape((slots, 2 * feed))] * (spread - 1),
        (near, *to_x(far), in_own, in_sib),
        flops=4 * spread * slots * half * feed,
        nbytes=4 * half * feed,
    )
    *grads, pre = lax.optimization_barrier((*grads, pre))
    grads = to_expert(grads)
    first = [value for values in pieces for value in (values[0], to_core(values[0]))]
    grads, back = call(
        bound(back_kernel, groups, replicas),
        [shape((slots, width)), shape((slots, feed), F32)],
        (*grads, out_own, out_sib, *first),
    )
    pre_far = to_x(pre_far)
    rest = [values[1:] for values in pieces]
    rest, *_ = lax.optimization_barrier((rest, pre_far, back))
    rest = [(values, [to_core(value) for value in values]) for values in rest]
    w_outs = [out_own, out_sib]
    for i, pair in enumerate(rest):
        for core in range(CORES):
            w_outs += [first[i * CORES + core], *pair[core]]
    hidden, d_pre = call(
        bound(act_kernel, spread, replicas),
        [shape((slots, feed)), shape((slots, 2 * feed))],
        (pre, *pre_far, grads, back, *[value for pair in rest for values in pair for value in values]),
        scratch_shapes=[pltpu.VMEM((slots, feed), F32)],
    )
    d_pre = [d_pre, *to_x([d_pre] * (spread - 1))]
    expert_out = call(
        bound(expert_out_kernel, groups, capacity, replicas),
        chunk,
        (hidden, *w_outs),
        flops=2 * slots * width * feed,
        nbytes=2 * width * feed,
    )
    expert_out = to_expert(expert_out)
    d_rows = call(
        bound(d_rows_kernel, groups, spread, capacity),
        [shape((spread * capacity, half))] * groups,
        (*d_pre, in_own, in_sib),
        flops=4 * spread * slots * half * feed,
        nbytes=4 * half * feed,
        after=expert_out[1:],
    )
    d_rows = to_expert(d_rows)
    packed = call(
        bound(pack_kernel, spread),
        [shape((slots, half + feed))] * (spread - 1),
        (grads, hidden),
        after=(d_rows[0],),
    )
    own, sib, all_hidden = call(
        bound(gather_kernel, spread),
        [shape((spread * slots, part))] * 2 + [shape((spread * slots, feed))],
        (grads, hidden, *to_x(packed)),
    )
    (d_w_out,) = call(
        weight_kernel,
        [shape((part, feed), F32)],
        (own, all_hidden, to_core(sib), to_core(all_hidden)),
        flops=4 * spread * slots * part * feed,
        nbytes=4 * part * feed,
    )
    combined, combined_token = call(
        bound(combine_kernel, groups, parts),
        [shape((count, width))],
        (turned, gate, *expert_out),
        flops=4 * slots * count * width,
        nbytes=4 * count * width,
        token=True,
        out_specs=[pl.BlockSpec(memory_space=pltpu.HBM), pl.BlockSpec(memory_space=pltpu.VMEM)],
        scratch_shapes=[
            pltpu.VMEM((parts, count, part), BF16),
            pltpu.SemaphoreType.DMA((parts,)),
        ],
    )

    def d_tokens_columns(span, *operands, **kw):
        pieces = len(span) * CORES
        return call(
            bound(d_tokens_kernel, groups, parts, capacity, span),
            [shape((count, width))],
            (turned, *operands),
            flops=2 * slots * half * count,
            nbytes=2 * count * half,
            out_specs=[pl.BlockSpec(memory_space=pltpu.HBM)],
            scratch_shapes=[
                pltpu.VMEM((pieces, count, part), BF16),
                pltpu.SemaphoreType.DMA((pieces,)),
            ],
            **kw,
        )[0]

    far = call(
        bound(far_kernel, groups, spread, capacity),
        [shape((slots, half))] * (spread - 1),
        d_rows,
        nbytes=4 * slots * width,
    )
    far = to_x(far)
    d_tokens = d_tokens_columns([0], *d_rows, after=(combined_token,))
    d_tokens = d_tokens_columns(
        range(1, spread), *far, d_tokens, far=1, input_output_aliases={1 + len(far): 0}
    )
    return combined, d_tokens, d_w_out[None]


def solution(mesh):
    rows = P(("replica", "expert", "fsdp"), None)
    weights = P("expert", "fsdp", None)
    return jax.shard_map(
        per_device,
        mesh=mesh,
        in_specs=(rows,) * 5 + (weights,) * 2,
        out_specs=(rows, rows, P(("replica", "expert"), "fsdp", None)),
        check_vma=False,
    )
```

```python
import jax
import jax.numpy as jnp
from jax import lax
from jax.experimental import pallas as pl
from jax.experimental.pallas import tpu as pltpu
from jax.sharding import PartitionSpec as P

EXPERTS = 128
CORES = 2
VMEM = 40 * 1024 * 1024
F32 = jnp.float32
BF16 = jnp.bfloat16


def product(left, right, left_dim, right_dim, **kw):
    return lax.dot_general(
        left, right, (((left_dim,), (right_dim,)), ((), ())), preferred_element_type=F32, **kw
    )


def call(body, out_shape, args, far=0, after=(), token=False, **kw):
    out_shape = [*out_shape] + [shape((8, 128), F32)] * token
    specs = [pl.BlockSpec(memory_space=pltpu.VMEM)] * (len(args) - far)
    specs += [pl.BlockSpec(memory_space=pltpu.HBM)] * far
    specs += [pl.BlockSpec(memory_space=pl.ANY)] * len(after)
    kw.setdefault("out_specs", [pl.BlockSpec(memory_space=pltpu.VMEM)] * len(out_shape))
    args = [
        pltpu.with_memory_space_constraint(arg, pltpu.HBM) if i >= len(args) - far else arg
        for i, arg in enumerate(args)
    ]
    count, first, last = len(args), len(args) + len(after), len(args) + len(after) + len(out_shape)

    def kernel(*refs):
        if token:
            refs[last - 1][...] = jnp.zeros(refs[last - 1].shape, F32)
        body(*refs[:count], *refs[first : last - token], *refs[last:])

    return pl.pallas_call(
        kernel,
        out_shape=out_shape,
        in_specs=specs,
        compiler_params=pltpu.CompilerParams(vmem_limit_bytes=VMEM),
        cost_estimate=pl.CostEstimate(flops=0, bytes_accessed=0, transcendentals=0),
        **kw,
    )(*args, *after)


def shape(dims, kind=BF16):
    return jax.ShapeDtypeStruct(dims, kind)


def columns(k, part):
    return pl.ds(pl.multiple_of((lax.axis_index("fsdp") ^ k) * part, part), part)


def slot_kernel(groups, parts, capacity, *refs):
    sources, chunks, refs = refs[:5], refs[5 : 5 + groups], refs[5 + groups :]
    turned_out, gate_out, ids, gates, order, tok, cot, sems = refs
    copies = [
        pltpu.make_async_copy(source, target, sems.at[i])
        for i, (source, target) in enumerate(zip(sources, (ids, gates, order, tok, cot)))
    ]
    for copy in copies:
        copy.start()
    for copy in copies[:3]:
        copy.wait()
    choices, count = ids.shape
    slots = groups * capacity
    part = tok.shape[1] // parts
    slot = lax.broadcasted_iota(jnp.int32, (slots, count), 0)
    wanted = ((slot // capacity) ^ lax.axis_index("expert")) * (EXPERTS // groups)
    routed = jnp.zeros((slots, count), F32)
    gate = jnp.zeros((slots, count), F32)
    for k in range(choices):
        hit = ids[k : k + 1, :] == wanted
        routed = jnp.where(hit, 1.0, routed)
        gate = jnp.where(hit, gates[k : k + 1, :], gate)
    row = lax.broadcasted_iota(jnp.int32, (count, count), 0)
    col = lax.broadcasted_iota(jnp.int32, (count, count), 1)
    served = jnp.where(order[...] == row, 1.0, 0.0).astype(BF16)
    earlier = jnp.where(row < col, 1.0, 0.0).astype(BF16)
    by_rank = product(routed.astype(BF16), served, 1, 0)
    before = product(by_rank.astype(BF16), earlier, 1, 0)
    taken = jnp.where(before.astype(jnp.int32) == slot % capacity, by_rank, 0.0).astype(BF16)
    pick = product(taken, served, 1, 1)
    turned_out[...] = product(served, taken, 1, 1).astype(BF16)
    slot_gate = jnp.sum(pick * gate, axis=1, keepdims=True)
    gate_out[...] = jnp.broadcast_to(slot_gate, gate_out.shape)
    pick = pick.astype(BF16)
    for copy, source, scale, top in ((copies[3], tok, None, 0), (copies[4], cot, slot_gate, capacity)):
        copy.wait()
        for k in range(parts):
            rows = product(pick, source[:, columns(k, part)], 1, 0)
            rows = (rows if scale is None else scale * rows).astype(BF16)
            for ke in range(groups):
                chunks[ke][top : top + capacity, k * part : (k + 1) * part] = rows[
                    ke * capacity : (ke + 1) * capacity
                ]


def split_kernel(groups, spread, capacity, *refs):
    chunks, by_x = refs[:groups], refs[groups:]
    half = by_x[0].shape[1]
    for kx in range(spread):
        for ke in range(groups):
            by_x[kx][ke * capacity : (ke + 1) * capacity] = chunks[ke][
                :capacity, kx * half : (kx + 1) * half
            ]


def far_kernel(groups, spread, capacity, *refs):
    by_e, by_x = refs[:groups], refs[groups:]
    for ke in range(groups):
        for kx in range(1, spread):
            by_x[kx - 1][ke * capacity : (ke + 1) * capacity] = by_e[ke][
                kx * capacity : (kx + 1) * capacity
            ]


def pre_kernel(spread, *refs):
    left, (own, sib, *outs) = refs[:spread], refs[spread:]
    part = own.shape[0]
    rows = jnp.concatenate([r[...] for r in left], axis=0)
    total = product(rows[:, :part], own[...], 1, 0) + product(rows[:, part:], sib[...], 1, 0)
    count = left[0].shape[0]
    for kx in range(spread):
        outs[kx][...] = total[kx * count : (kx + 1) * count].astype(outs[kx].dtype)


def back_kernel(groups, capacity, *refs):
    chunks, weights, (grads, back) = refs[:groups], refs[groups:-2], refs[-2:]
    part = weights[0].shape[0]
    grads[...] = jnp.concatenate([c[capacity:] for c in chunks], axis=0)
    total = product(grads[:, :part], weights[0][...], 1, 0)
    for k, weight in enumerate(weights[1:], 1):
        total += product(grads[:, k * part : (k + 1) * part], weight[...], 1, 0)
    back[...] = total


def act_kernel(spread, *refs):
    back, hidden, d_pre = refs[spread:]
    pre = refs[0][...]
    for ref in refs[1:spread]:
        pre += ref[...].astype(F32)
    feed = back.shape[1]
    gate_act, up_act = pre[:, :feed], pre[:, feed:]
    sig = 1.0 / (1.0 + jnp.exp(-gate_act))
    silu = gate_act * sig
    hidden[...] = (silu * up_act).astype(BF16)
    d_pre[:, :feed] = (back[...] * up_act * (sig * (1.0 + gate_act * (1.0 - sig)))).astype(BF16)
    d_pre[:, feed:] = (back[...] * silu).astype(BF16)


def expert_out_kernel(groups, capacity, hidden, *refs):
    weights, chunks = refs[:-groups], refs[-groups:]
    part = weights[0].shape[0]
    for k, weight in enumerate(weights):
        value = product(hidden[...], weight[...], 1, 1).astype(BF16)
        for ke in range(groups):
            chunks[ke][:, k * part : (k + 1) * part] = value[ke * capacity : (ke + 1) * capacity]


def d_rows_kernel(groups, spread, capacity, *refs):
    left, (own, sib, *chunks) = refs[:spread], refs[spread:]
    part = own.shape[0]
    rows = jnp.concatenate([r[...] for r in left], axis=0)
    for kc, weight in enumerate((own, sib)):
        value = product(rows, weight[...], 1, 1).astype(BF16)
        for ke in range(groups):
            for kx in range(spread):
                at = (kx * groups + ke) * capacity
                chunks[ke][kx * capacity : (kx + 1) * capacity, kc * part : (kc + 1) * part] = value[
                    at : at + capacity
                ]


def pack_kernel(spread, grads, hidden, *outs):
    half = grads.shape[1] // spread
    for kx in range(1, spread):
        outs[kx - 1][:, :half] = grads[:, kx * half : (kx + 1) * half]
        outs[kx - 1][:, half:] = hidden[...]


def gather_kernel(spread, grads, hidden, *refs):
    far, (own, sib, all_hidden) = refs[: spread - 1], refs[spread - 1 :]
    part = own.shape[1]
    count = grads.shape[0]
    for kx in range(spread):
        source = far[kx - 1] if kx else grads
        at = pl.ds(kx * count, count)
        own[at] = source[:, :part]
        sib[at] = source[:, part : 2 * part]
        all_hidden[at] = source[:, 2 * part :] if kx else hidden[...]


def weight_kernel(own, hidden, sib, sib_hidden, out):
    left = jnp.concatenate([own[...], sib[...]], axis=0)
    right = jnp.concatenate([hidden[...], sib_hidden[...]], axis=0)
    out[...] = product(left, right, 0, 0)


def combine_kernel(groups, parts, turned, gate, *refs):
    chunks, (out, held, sems) = refs[:groups], refs[groups:]
    part = out.shape[1] // parts
    twice = jnp.concatenate([turned[...], turned[...]], axis=1)
    copies = []
    for k in range(parts):
        rows = jnp.concatenate([c[:, k * part : (k + 1) * part] for c in chunks], axis=0)
        weighted = rows.astype(F32) * gate[:, :1]
        high = weighted.astype(BF16)
        low = (weighted - high.astype(F32)).astype(BF16)
        both = jnp.concatenate([high, low], axis=0)
        held[k] = product(twice, both, 1, 0).astype(BF16)
        copies.append(pltpu.make_async_copy(held.at[k], out.at[:, columns(k, part)], sems.at[k]))
        copies[-1].start()
    for copy in copies:
        copy.wait()


def d_tokens_kernel(groups, parts, capacity, span, turned, *refs):
    *refs, out, held, sems = refs
    part = out.shape[1] // parts
    copies = []
    for n, kx in enumerate(span):
        for kc in range(CORES):
            cols = slice(kc * part, (kc + 1) * part)
            if kx:
                rows = refs[n][:, cols]
            else:
                rows = jnp.concatenate([refs[ke][:capacity, cols] for ke in range(groups)], axis=0)
            i = len(copies)
            held[i] = product(turned[...], rows, 1, 0).astype(BF16)
            target = out.at[:, columns(kx * CORES + kc, part)]
            copies.append(pltpu.make_async_copy(held.at[i], target, sems.at[i]))
            copies[-1].start()
    for copy in copies:
        copy.wait()


def per_device(tokens, cotangent, route_ids, route_gates, served_order, w_in, w_out):
    groups = lax.axis_size("expert")
    parts = lax.axis_size("fsdp")
    spread = parts // CORES
    count, width = tokens.shape
    capacity = count * route_ids.shape[1] // EXPERTS
    feed = w_out.shape[2]
    slots = groups * capacity
    half = width // spread
    part = width // parts

    def bound(kernel, *sizes):
        return lambda *refs: kernel(*sizes, *refs)

    def to_core(value):
        return lax.ppermute(value, "fsdp", [(i, i ^ 1) for i in range(parts)])

    def to_x(values):
        return [
            lax.ppermute(value, "fsdp", [(i, i ^ ((k + 1) * CORES)) for i in range(parts)])
            for k, value in enumerate(values)
        ]

    def to_expert(chunks):
        return [
            lax.ppermute(value, "expert", [(i, i ^ ke) for i in range(groups)]) if ke else value
            for ke, value in enumerate(chunks)
        ]

    chunk = [shape((capacity, width))] * groups
    in_own, out_own = w_in[0], w_out[0]
    *chunks, turned, gate = call(
        bound(slot_kernel, groups, parts, capacity),
        [shape((2 * capacity, width))] * groups
        + [shape((count, slots)), shape((slots, 128), F32)],
        (route_ids.T, route_gates.T, served_order, tokens, cotangent),
        far=5,
        scratch_shapes=[
            pltpu.VMEM(route_ids.shape[::-1], jnp.int32),
            pltpu.VMEM(route_gates.shape[::-1], F32),
            pltpu.VMEM(served_order.shape, jnp.int32),
            pltpu.VMEM(tokens.shape, BF16),
            pltpu.VMEM(cotangent.shape, BF16),
            pltpu.SemaphoreType.DMA((5,)),
        ],
    )
    in_own, out_own, chunks[0] = lax.optimization_barrier((in_own, out_own, chunks[0]))
    chunks = to_expert(chunks)
    out_far = to_x([out_own] * (spread - 1))
    in_sib, out_sib = to_core(in_own), to_core(out_own)
    near, *far = call(
        bound(split_kernel, groups, spread, capacity), [shape((slots, half))] * spread, chunks
    )
    pre, *pre_far = call(
        bound(pre_kernel, spread),
        [shape((slots, 2 * feed), F32)] + [shape((slots, 2 * feed))] * (spread - 1),
        (near, *to_x(far), in_own, in_sib),
    )
    out_far, pre = lax.optimization_barrier((out_far, pre))
    w_outs = [out_own, out_sib] + [w for value in out_far for w in (value, to_core(value))]
    grads, back = call(
        bound(back_kernel, groups, capacity),
        [shape((slots, width)), shape((slots, feed), F32)],
        (*chunks, *w_outs),
    )
    hidden, d_pre = call(
        bound(act_kernel, spread),
        [shape((slots, feed)), shape((slots, 2 * feed))],
        (pre, *to_x(pre_far), back),
    )
    expert_out = to_expert(
        call(bound(expert_out_kernel, groups, capacity), chunk, (hidden, *w_outs))
    )
    d_rows = call(
        bound(d_rows_kernel, groups, spread, capacity),
        [shape((spread * capacity, half))] * groups,
        (d_pre, *to_x([d_pre] * (spread - 1)), in_own, in_sib),
        after=expert_out[1:3],
    )
    packed = call(
        bound(pack_kernel, spread),
        [shape((slots, half + feed))] * (spread - 1),
        (grads, hidden),
        after=d_rows[:1],
    )
    d_rows = to_expert(d_rows)
    far = call(
        bound(far_kernel, groups, spread, capacity),
        [shape((slots, half))] * (spread - 1),
        d_rows,
        after=expert_out[3:],
    )
    own, sib, all_hidden = call(
        bound(gather_kernel, spread),
        [shape((spread * slots, part))] * 2 + [shape((spread * slots, feed))],
        (grads, hidden, *to_x(packed)),
        after=far[:1],
    )
    d_w_out, token = call(
        weight_kernel,
        [shape((part, feed), F32)],
        (own, all_hidden, to_core(sib), to_core(all_hidden)),
        token=True,
    )

    def scattered(kernel, pieces, operands, **kw):
        out, *token = call(
            kernel,
            [shape((count, width))],
            operands,
            out_specs=[pl.BlockSpec(memory_space=pltpu.HBM)]
            + [pl.BlockSpec(memory_space=pltpu.VMEM)] * kw.get("token", False),
            scratch_shapes=[
                pltpu.VMEM((pieces, count, part), BF16),
                pltpu.SemaphoreType.DMA((pieces,)),
            ],
            **kw,
        )
        return out, token

    combined, token = scattered(
        bound(combine_kernel, groups, parts),
        parts,
        (turned, gate, *expert_out),
        after=(token,),
        token=True,
    )
    d_tokens, _ = scattered(
        bound(d_tokens_kernel, groups, parts, capacity, [0]),
        CORES,
        (turned, *d_rows),
        after=token,
    )
    far = to_x(far)
    d_tokens, _ = scattered(
        bound(d_tokens_kernel, groups, parts, capacity, range(1, spread)),
        len(far) * CORES,
        (turned, *far, d_tokens),
        far=1,
        input_output_aliases={1 + len(far): 0},
    )
    return combined, d_tokens, d_w_out[None]


def solution(mesh):
    rows = P(("replica", "expert", "fsdp"), None)
    weights = P("expert", "fsdp", None)
    return jax.shard_map(
        per_device,
        mesh=mesh,
        in_specs=(rows,) * 5 + (weights,) * 2,
        out_specs=(rows, rows, P(("replica", "expert"), "fsdp", None)),
        check_vma=False,
    )
```

```python
import jax
import jax.numpy as jnp
from jax import lax
from jax.experimental import pallas as pl
from jax.experimental.pallas import tpu as pltpu
from jax.sharding import PartitionSpec as P

EXPERTS = 128
CORES = 2
VMEM = 40 * 1024 * 1024
F32 = jnp.float32
BF16 = jnp.bfloat16


def product(left, right, left_dim, right_dim, **kw):
    return lax.dot_general(
        left, right, (((left_dim,), (right_dim,)), ((), ())), preferred_element_type=F32, **kw
    )


def call(body, out_shape, args, far=0, after=(), token=False, **kw):
    out_shape = [*out_shape] + [shape((8, 128), F32)] * token
    specs = [pl.BlockSpec(memory_space=pltpu.VMEM)] * (len(args) - far)
    specs += [pl.BlockSpec(memory_space=pltpu.HBM)] * far
    specs += [pl.BlockSpec(memory_space=pl.ANY)] * len(after)
    kw.setdefault("out_specs", [pl.BlockSpec(memory_space=pltpu.VMEM)] * len(out_shape))
    args = [
        pltpu.with_memory_space_constraint(arg, pltpu.HBM) if i >= len(args) - far else arg
        for i, arg in enumerate(args)
    ]
    count, first, last = len(args), len(args) + len(after), len(args) + len(after) + len(out_shape)

    def kernel(*refs):
        if token:
            refs[last - 1][...] = jnp.zeros(refs[last - 1].shape, F32)
        body(*refs[:count], *refs[first : last - token], *refs[last:])

    return pl.pallas_call(
        kernel,
        out_shape=out_shape,
        in_specs=specs,
        compiler_params=pltpu.CompilerParams(vmem_limit_bytes=VMEM),
        cost_estimate=pl.CostEstimate(flops=0, bytes_accessed=0, transcendentals=0),
        **kw,
    )(*args, *after)


def shape(dims, kind=BF16):
    return jax.ShapeDtypeStruct(dims, kind)


def columns(k, part):
    return pl.ds(pl.multiple_of((lax.axis_index("fsdp") ^ k) * part, part), part)


def slot_kernel(groups, spread, capacity, *refs):
    sources, by_x, refs = refs[:5], refs[5 : 5 + spread], refs[5 + spread :]
    chunks, (turned_out, gate_out, ids, gates, order, tok, cot, sems) = refs[:groups], refs[groups:]
    parts = spread * CORES
    copies = [
        pltpu.make_async_copy(source, target, sems.at[i])
        for i, (source, target) in enumerate(zip(sources, (ids, gates, order, tok, cot)))
    ]
    for copy in copies:
        copy.start()
    for copy in copies[:3]:
        copy.wait()
    choices, count = ids.shape
    slots = groups * capacity
    part = tok.shape[1] // parts
    slot = lax.broadcasted_iota(jnp.int32, (slots, count), 0)
    wanted = ((slot // capacity) ^ lax.axis_index("expert")) * (EXPERTS // groups)
    routed = jnp.zeros((slots, count), F32)
    gate = jnp.zeros((slots, count), F32)
    for k in range(choices):
        hit = ids[k : k + 1, :] == wanted
        routed = jnp.where(hit, 1.0, routed)
        gate = jnp.where(hit, gates[k : k + 1, :], gate)
    row = lax.broadcasted_iota(jnp.int32, (count, count), 0)
    col = lax.broadcasted_iota(jnp.int32, (count, count), 1)
    served = jnp.where(order[...] == row, 1.0, 0.0).astype(BF16)
    earlier = jnp.where(row < col, 1.0, 0.0).astype(BF16)
    by_rank = product(routed.astype(BF16), served, 1, 0)
    before = product(by_rank.astype(BF16), earlier, 1, 0)
    taken = jnp.where(before.astype(jnp.int32) == slot % capacity, by_rank, 0.0).astype(BF16)
    pick = product(taken, served, 1, 1)
    turned_out[...] = product(served, taken, 1, 1).astype(BF16)
    slot_gate = jnp.sum(pick * gate, axis=1, keepdims=True)
    gate_out[...] = jnp.broadcast_to(slot_gate, gate_out.shape)
    pick = pick.astype(BF16)
    copies[3].wait()
    for k in range(parts):
        rows = product(pick, tok[:, columns(k, part)], 1, 0).astype(BF16)
        by_x[k // CORES][:, (k % CORES) * part : (k % CORES + 1) * part] = rows
    copies[4].wait()
    for k in range(parts):
        grads = product(pick, cot[:, columns(k, part)], 1, 0)
        grads = (slot_gate * grads).astype(BF16)
        for ke in range(groups):
            chunks[ke][:, k * part : (k + 1) * part] = grads[ke * capacity : (ke + 1) * capacity]


def join_kernel(groups, spread, capacity, *refs):
    by_x, riders, chunks = refs[:spread], refs[spread:-groups], refs[-groups:]
    half = by_x[0].shape[1]
    for ke in range(groups):
        for kx in range(spread):
            chunks[ke][:capacity, kx * half : (kx + 1) * half] = by_x[kx][
                ke * capacity : (ke + 1) * capacity
            ]
    for ke, rider in enumerate(riders, 1):
        chunks[ke][capacity:] = rider[...]


def pre_kernel(groups, spread, capacity, *refs):
    chunks, (own, sib, *outs) = refs[:groups], refs[groups:]
    part = own.shape[0]
    half = CORES * part
    slots = groups * capacity
    rows = jnp.concatenate(
        [c[:capacity, kx * half : (kx + 1) * half] for kx in range(spread) for c in chunks], axis=0
    )
    total = product(rows[:, :part], own[...], 1, 0) + product(rows[:, part:], sib[...], 1, 0)
    for kx in range(spread):
        outs[kx][...] = total[kx * slots : (kx + 1) * slots].astype(outs[kx].dtype)


def back_kernel(groups, capacity, *refs):
    chunks, weights, (grads, back) = refs[:groups], refs[groups:-2], refs[-2:]
    part = weights[0].shape[0]
    grads[...] = jnp.concatenate([c[-capacity:] for c in chunks], axis=0)
    total = product(grads[:, :part], weights[0][...], 1, 0)
    for k, weight in enumerate(weights[1:], 1):
        total += product(grads[:, k * part : (k + 1) * part], weight[...], 1, 0)
    back[...] = total


def act_kernel(spread, *refs):
    back, hidden, d_pre = refs[spread:]
    pre = refs[0][...]
    for ref in refs[1:spread]:
        pre += ref[...].astype(F32)
    feed = back.shape[1]
    gate_act, up_act = pre[:, :feed], pre[:, feed:]
    sig = 1.0 / (1.0 + jnp.exp(-gate_act))
    silu = gate_act * sig
    hidden[...] = (silu * up_act).astype(BF16)
    d_pre[:, :feed] = (back[...] * up_act * (sig * (1.0 + gate_act * (1.0 - sig)))).astype(BF16)
    d_pre[:, feed:] = (back[...] * silu).astype(BF16)


def expert_out_kernel(groups, capacity, hidden, *refs):
    weights, chunks = refs[:-groups], refs[-groups:]
    part = weights[0].shape[0]
    for k, weight in enumerate(weights):
        value = product(hidden[...], weight[...], 1, 1).astype(BF16)
        for ke in range(groups):
            chunks[ke][:, k * part : (k + 1) * part] = value[ke * capacity : (ke + 1) * capacity]


def d_rows_kernel(spread, *refs):
    left, (own, sib, *outs) = refs[:spread], refs[spread:]
    part = own.shape[0]
    count = left[0].shape[0]
    rows = jnp.concatenate([r[...] for r in left], axis=0)
    for kc, weight in enumerate((own, sib)):
        value = product(rows, weight[...], 1, 1).astype(BF16)
        for kx in range(spread):
            outs[kx][:, kc * part : (kc + 1) * part] = value[kx * count : (kx + 1) * count]


def pack_kernel(spread, grads, hidden, *outs):
    half = grads.shape[1] // spread
    for kx in range(1, spread):
        outs[kx - 1][:, :half] = grads[:, kx * half : (kx + 1) * half]
        outs[kx - 1][:, half:] = hidden[...]


def gather_kernel(spread, grads, hidden, *refs):
    far, (own, sib, all_hidden) = refs[: spread - 1], refs[spread - 1 :]
    part = own.shape[1]
    count = grads.shape[0]
    for kx in range(spread):
        source = far[kx - 1] if kx else grads
        at = pl.ds(kx * count, count)
        own[at] = source[:, :part]
        sib[at] = source[:, part : 2 * part]
        all_hidden[at] = source[:, 2 * part :] if kx else hidden[...]


def weight_kernel(own, hidden, sib, sib_hidden, out):
    left = jnp.concatenate([own[...], sib[...]], axis=0)
    right = jnp.concatenate([hidden[...], sib_hidden[...]], axis=0)
    out[...] = product(left, right, 0, 0)


def combine_kernel(groups, parts, turned, gate, *refs):
    chunks, (out, held, sems) = refs[:groups], refs[groups:]
    part = out.shape[1] // parts
    twice = jnp.concatenate([turned[...], turned[...]], axis=1)
    copies = []
    for k in range(parts):
        rows = jnp.concatenate([c[:, k * part : (k + 1) * part] for c in chunks], axis=0)
        if gate is None:
            held[k] = product(turned[...], rows, 1, 0).astype(BF16)
        else:
            weighted = rows.astype(F32) * gate[:, :1]
            high = weighted.astype(BF16)
            low = (weighted - high.astype(F32)).astype(BF16)
            both = jnp.concatenate([high, low], axis=0)
            held[k] = product(twice, both, 1, 0).astype(BF16)
        copies.append(pltpu.make_async_copy(held.at[k], out.at[:, columns(k, part)], sems.at[k]))
        copies[-1].start()
    for copy in copies:
        copy.wait()


def per_device(tokens, cotangent, route_ids, route_gates, served_order, w_in, w_out):
    groups = lax.axis_size("expert")
    parts = lax.axis_size("fsdp")
    spread = parts // CORES
    count, width = tokens.shape
    capacity = count * route_ids.shape[1] // EXPERTS
    feed = w_out.shape[2]
    slots = groups * capacity
    half = width // spread
    part = width // parts

    def bound(kernel, *sizes):
        return lambda *refs: kernel(*sizes, *refs)

    def to_core(value):
        return lax.ppermute(value, "fsdp", [(i, i ^ 1) for i in range(parts)])

    def to_x(values):
        return [
            lax.ppermute(value, "fsdp", [(i, i ^ ((k + 1) * CORES)) for i in range(parts)])
            for k, value in enumerate(values)
        ]

    def to_expert(chunks):
        return [
            lax.ppermute(value, "expert", [(i, i ^ ke) for i in range(groups)]) if ke else value
            for ke, value in enumerate(chunks)
        ]

    chunk = [shape((capacity, width))] * groups
    by_x = [shape((slots, half))] * spread
    in_own, out_own = w_in[0], w_out[0]
    outs = call(
        bound(slot_kernel, groups, spread, capacity),
        by_x + chunk + [shape((count, slots)), shape((slots, 128), F32)],
        (route_ids.T, route_gates.T, served_order, tokens, cotangent),
        far=5,
        scratch_shapes=[
            pltpu.VMEM(route_ids.shape[::-1], jnp.int32),
            pltpu.VMEM(route_gates.shape[::-1], F32),
            pltpu.VMEM(served_order.shape, jnp.int32),
            pltpu.VMEM(tokens.shape, BF16),
            pltpu.VMEM(cotangent.shape, BF16),
            pltpu.SemaphoreType.DMA((5,)),
        ],
    )
    (near, *far), grads, (turned, gate) = outs[:spread], outs[spread:-2], outs[-2:]
    in_own, out_own, near = lax.optimization_barrier((in_own, out_own, near))
    in_sib, out_sib = to_core(in_own), to_core(out_own)
    out_far = to_x([out_own] * (spread - 1))
    rows = call(
        bound(join_kernel, groups, spread, capacity),
        [shape(((1 + (ke == 1)) * capacity, width)) for ke in range(groups)],
        (near, *to_x(far), grads[1]),
    )
    rows = to_expert(rows)
    pre, *pre_far = call(
        bound(pre_kernel, groups, spread, capacity),
        [shape((slots, 2 * feed), F32)] + [shape((slots, 2 * feed))] * (spread - 1),
        (*rows, in_own, in_sib),
    )
    out_far, pre, *grads = lax.optimization_barrier((out_far, pre, *grads))
    w_outs = [out_own, out_sib] + [w for value in out_far for w in (value, to_core(value))]
    grads = to_expert(grads)
    grads[1] = rows[1]
    grads, back = call(
        bound(back_kernel, groups, capacity),
        [shape((slots, width)), shape((slots, feed), F32)],
        (*grads, *w_outs),
    )
    hidden, d_pre = call(
        bound(act_kernel, spread),
        [shape((slots, feed)), shape((slots, 2 * feed))],
        (pre, *to_x(pre_far), back),
    )
    expert_out = to_expert(
        call(bound(expert_out_kernel, groups, capacity), chunk, (hidden, *w_outs))
    )
    near, *far = call(
        bound(d_rows_kernel, spread),
        by_x,
        (d_pre, *to_x([d_pre] * (spread - 1)), in_own, in_sib),
        after=expert_out[2:3],
    )
    d_rows = call(
        bound(join_kernel, groups, spread, capacity),
        chunk,
        (near, *to_x(far)),
        after=(expert_out[1], *expert_out[3:]),
    )
    packed = call(
        bound(pack_kernel, spread),
        [shape((slots, half + feed))] * (spread - 1),
        (grads, hidden),
        after=d_rows[:1],
    )
    d_rows = to_expert(d_rows)
    own, sib, all_hidden = call(
        bound(gather_kernel, spread),
        [shape((spread * slots, part))] * 2 + [shape((spread * slots, feed))],
        (grads, hidden, *to_x(packed)),
        after=d_rows[1:],
    )
    (d_w_out,) = call(
        weight_kernel,
        [shape((part, feed), F32)],
        (own, all_hidden, to_core(sib), to_core(all_hidden)),
    )

    def scattered(kernel, operands, **kw):
        return call(
            kernel,
            [shape((count, width))],
            operands,
            out_specs=[pl.BlockSpec(memory_space=pltpu.HBM)]
            + [pl.BlockSpec(memory_space=pltpu.VMEM)] * kw.get("token", False),
            scratch_shapes=[
                pltpu.VMEM((parts, count, part), BF16),
                pltpu.SemaphoreType.DMA((parts,)),
            ],
            **kw,
        )

    combined, token = scattered(
        bound(combine_kernel, groups, parts), (turned, gate, *expert_out), token=True
    )
    (d_tokens,) = scattered(
        lambda turned, *refs: combine_kernel(groups, parts, turned, None, *refs),
        (turned, *d_rows),
        after=(token,),
    )
    return combined, d_tokens, d_w_out[None]


def solution(mesh):
    rows = P(("replica", "expert", "fsdp"), None)
    weights = P("expert", "fsdp", None)
    return jax.shard_map(
        per_device,
        mesh=mesh,
        in_specs=(rows,) * 5 + (weights,) * 2,
        out_specs=(rows, rows, P(("replica", "expert"), "fsdp", None)),
        check_vma=False,
    )
```

```python
import jax
import jax.numpy as jnp
from jax import lax
from jax.experimental import pallas as pl
from jax.experimental.pallas import tpu as pltpu
from jax.sharding import PartitionSpec as P

EXPERTS = 128
CORES = 2
PIECES = 3
VMEM = 40 * 1024 * 1024
F32 = jnp.float32
BF16 = jnp.bfloat16


def product(left, right, left_dim, right_dim, **kw):
    return lax.dot_general(
        left, right, (((left_dim,), (right_dim,)), ((), ())), preferred_element_type=F32, **kw
    )


def call(body, out_shape, args, far=0, cost=0, after=(), token=False, **kw):
    out_shape = [*out_shape] + [shape((8, 128), F32)] * token
    specs = [pl.BlockSpec(memory_space=pltpu.VMEM)] * (len(args) - far)
    specs += [pl.BlockSpec(memory_space=pltpu.HBM)] * far
    specs += [pl.BlockSpec(memory_space=pl.ANY)] * len(after)
    kw.setdefault("out_specs", [pl.BlockSpec(memory_space=pltpu.VMEM)] * len(out_shape))
    args = [
        pltpu.with_memory_space_constraint(arg, pltpu.HBM) if i >= len(args) - far else arg
        for i, arg in enumerate(args)
    ]
    count, first, last = len(args), len(args) + len(after), len(args) + len(after) + len(out_shape)

    def kernel(*refs):
        if token:
            refs[last - 1][...] = jnp.zeros(refs[last - 1].shape, F32)
        body(*refs[:count], *refs[first : last - token], *refs[last:])

    return pl.pallas_call(
        kernel,
        out_shape=out_shape,
        in_specs=specs,
        compiler_params=pltpu.CompilerParams(vmem_limit_bytes=VMEM),
        cost_estimate=pl.CostEstimate(flops=cost, bytes_accessed=0, transcendentals=0),
        **kw,
    )(*args, *after)


def shape(dims, kind=BF16):
    return jax.ShapeDtypeStruct(dims, kind)


def columns(k, part):
    return pl.ds(pl.multiple_of((lax.axis_index("fsdp") ^ k) * part, part), part)


def slot_kernel(groups, parts, capacity, *refs):
    sources, chunks, refs = refs[:5], refs[5 : 5 + groups], refs[5 + groups :]
    turned_out, gate_out, ids, gates, order, tok, cot, sems = refs
    copies = [
        pltpu.make_async_copy(source, target, sems.at[i])
        for i, (source, target) in enumerate(zip(sources, (ids, gates, order, tok, cot)))
    ]
    for copy in copies:
        copy.start()
    for copy in copies[:3]:
        copy.wait()
    choices, count = ids.shape
    slots = groups * capacity
    part = tok.shape[1] // parts
    slot = lax.broadcasted_iota(jnp.int32, (slots, count), 0)
    wanted = ((slot // capacity) ^ lax.axis_index("expert")) * (EXPERTS // groups)
    routed = jnp.zeros((slots, count), F32)
    gate = jnp.zeros((slots, count), F32)
    for k in range(choices):
        hit = ids[k : k + 1, :] == wanted
        routed = jnp.where(hit, 1.0, routed)
        gate = jnp.where(hit, gates[k : k + 1, :], gate)
    row = lax.broadcasted_iota(jnp.int32, (count, count), 0)
    col = lax.broadcasted_iota(jnp.int32, (count, count), 1)
    served = jnp.where(order[...] == row, 1.0, 0.0).astype(BF16)
    earlier = jnp.where(row < col, 1.0, 0.0).astype(BF16)
    by_rank = product(routed.astype(BF16), served, 1, 0)
    before = product(by_rank.astype(BF16), earlier, 1, 0)
    taken = jnp.where(before.astype(jnp.int32) == slot % capacity, by_rank, 0.0).astype(BF16)
    pick = product(taken, served, 1, 1)
    turned_out[...] = product(served, taken, 1, 1).astype(BF16)
    slot_gate = jnp.sum(pick * gate, axis=1, keepdims=True)
    gate_out[...] = jnp.broadcast_to(slot_gate, gate_out.shape)
    pick = pick.astype(BF16)
    for copy, source, scale, top in ((copies[3], tok, None, 0), (copies[4], cot, slot_gate, capacity)):
        copy.wait()
        for k in range(parts):
            rows = product(pick, source[:, columns(k, part)], 1, 0)
            rows = (rows if scale is None else scale * rows).astype(BF16)
            for ke in range(groups):
                chunks[ke][top : top + capacity, k * part : (k + 1) * part] = rows[
                    ke * capacity : (ke + 1) * capacity
                ]


def piece_columns(n, s, width, replicas):
    at = ((lax.axis_index("replica") ^ n) * PIECES + s) * width
    return pl.ds(pl.multiple_of(at, 128), width)


def piece_kernel(replicas, w_in, *refs):
    *outs, sems = refs
    copies = []
    for s, out in enumerate(outs):
        cols = piece_columns(0, s, out.shape[1], replicas)
        copies.append(pltpu.make_async_copy(w_in.at[:, cols], out, sems.at[s]))
        copies[-1].start()
    for copy in copies:
        copy.wait()


def near_kernel(groups, spread, capacity, *refs):
    chunks, (own, sib, rows, pre, *grads) = refs[:groups], refs[groups:]
    part = own.shape[0]
    half = CORES * part
    rows[...] = jnp.concatenate([c[:capacity] for c in chunks], axis=0)
    for kx in range(spread):
        cols = slice(kx * half, (kx + 1) * half)
        grads[kx][...] = jnp.concatenate([c[capacity:, cols] for c in chunks], axis=0)
    total = product(rows[:, :part], own[...], 1, 0)
    pre[...] = total + product(rows[:, part : 2 * part], sib[...], 1, 0)


def back_kernel(spread, *refs):
    left, (own, sib, *outs) = refs[:spread], refs[spread:]
    part = own.shape[0]
    count = left[0].shape[0]
    rows = jnp.concatenate([r[...] for r in left], axis=0)
    total = product(rows[:, :part], own[...], 1, 0) + product(rows[:, part:], sib[...], 1, 0)
    for kx in range(spread):
        outs[kx][...] = total[kx * count : (kx + 1) * count].astype(outs[kx].dtype)


def hidden_kernel(replicas, rows, pre_in, *refs):
    pieces, (hidden, pre) = refs[:-2], refs[-2:]
    part, width = pieces[0].shape
    feed = hidden.shape[1]
    each = PIECES * replicas
    pre[...] = pre_in[...]
    for i in range(each):
        total = 0.0
        for k, piece in enumerate(pieces[i::each], CORES):
            total += product(rows[:, k * part : (k + 1) * part], piece[...], 1, 0)
        pre[:, piece_columns(i // PIECES, i % PIECES, width, replicas)] += total
    gate_act, up_act = pre[:, :feed], pre[:, feed:]
    hidden[...] = (gate_act * (1.0 / (1.0 + jnp.exp(-gate_act))) * up_act).astype(BF16)


def d_rows_kernel(groups, spread, capacity, replicas, pre, *refs):
    backs, (own, sib), refs = refs[:spread], refs[spread : spread + 2], refs[spread + 2 :]
    pieces, chunks, d_pre = refs[: -groups - 1], refs[-groups - 1 : -1], refs[-1]
    part = own.shape[0]
    width = pieces[0].shape[1]
    each = PIECES * replicas
    back = backs[0][...]
    for ref in backs[1:]:
        back += ref[...].astype(F32)
    feed = back.shape[1]
    gate_act, up_act = pre[:, :feed], pre[:, feed:]
    sig = 1.0 / (1.0 + jnp.exp(-gate_act))
    d_pre[:, :feed] = (back * up_act * (sig * (1.0 + gate_act * (1.0 - sig)))).astype(BF16)
    d_pre[:, feed:] = (back * (gate_act * sig)).astype(BF16)

    def store(k, value):
        value = value.astype(BF16)
        for ke in range(groups):
            chunks[ke][:, k * part : (k + 1) * part] = value[ke * capacity : (ke + 1) * capacity]

    store(0, product(d_pre[...], own[...], 1, 1))
    store(1, product(d_pre[...], sib[...], 1, 1))
    for k in range(len(pieces) // each):
        total = 0.0
        for i, piece in enumerate(pieces[k * each : (k + 1) * each]):
            cols = piece_columns(i // PIECES, i % PIECES, width, replicas)
            total += product(d_pre[:, cols], piece[...], 1, 1)
        store(CORES + k, total)


def expert_out_kernel(spread, *refs):
    left, (own, sib, *outs) = refs[:spread], refs[spread:]
    part = own.shape[0]
    count = left[0].shape[0]
    rows = jnp.concatenate([r[...] for r in left], axis=0)
    for kc, weight in enumerate((own, sib)):
        value = product(rows, weight[...], 1, 1).astype(BF16)
        for kx in range(spread):
            outs[kx][:, kc * part : (kc + 1) * part] = value[kx * count : (kx + 1) * count]


def join_kernel(groups, spread, capacity, *refs):
    by_x, chunks = refs[:spread], refs[spread:]
    half = by_x[0].shape[1]
    for ke in range(groups):
        for kx in range(spread):
            chunks[ke][:, kx * half : (kx + 1) * half] = by_x[kx][
                ke * capacity : (ke + 1) * capacity
            ]


def gather_kernel(spread, *refs):
    grads, hidden, (own, sib, all_hidden) = refs[:spread], refs[spread : 2 * spread], refs[2 * spread :]
    part = own.shape[1]
    count = grads[0].shape[0]
    for kx in range(spread):
        at = pl.ds(kx * count, count)
        own[at] = grads[kx][:, :part]
        sib[at] = grads[kx][:, part:]
        all_hidden[at] = hidden[kx][...]


def weight_kernel(own, hidden, sib, sib_hidden, out):
    left = jnp.concatenate([own[...], sib[...]], axis=0)
    right = jnp.concatenate([hidden[...], sib_hidden[...]], axis=0)
    out[...] = product(left, right, 0, 0)


def combine_kernel(groups, parts, turned, gate, *refs):
    chunks, (out, held, sems) = refs[:groups], refs[groups:]
    part = out.shape[1] // parts
    twice = jnp.concatenate([turned[...], turned[...]], axis=1)
    copies = []
    for k in range(parts):
        rows = jnp.concatenate([c[:, k * part : (k + 1) * part] for c in chunks], axis=0)
        if gate is None:
            held[k] = product(turned[...], rows, 1, 0).astype(BF16)
        else:
            weighted = rows.astype(F32) * gate[:, :1]
            high = weighted.astype(BF16)
            low = (weighted - high.astype(F32)).astype(BF16)
            both = jnp.concatenate([high, low], axis=0)
            held[k] = product(twice, both, 1, 0).astype(BF16)
        copies.append(pltpu.make_async_copy(held.at[k], out.at[:, columns(k, part)], sems.at[k]))
        copies[-1].start()
    for copy in copies:
        copy.wait()


def per_device(tokens, cotangent, route_ids, route_gates, served_order, w_in, w_out):
    replicas = lax.axis_size("replica")
    groups = lax.axis_size("expert")
    parts = lax.axis_size("fsdp")
    spread = parts // CORES
    count, width = tokens.shape
    capacity = count * route_ids.shape[1] // EXPERTS
    feed = w_out.shape[2]
    slots = groups * capacity
    half = width // spread
    part = width // parts

    def bound(kernel, *sizes):
        return lambda *refs: kernel(*sizes, *refs)

    def to_core(value):
        return lax.ppermute(value, "fsdp", [(i, i ^ 1) for i in range(parts)])

    def to_x(values):
        return [
            lax.ppermute(value, "fsdp", [(i, i ^ ((k + 1) * CORES)) for i in range(parts)])
            for k, value in enumerate(values)
        ]

    def to_replica(value, n):
        return lax.ppermute(value, "replica", [(i, i ^ n) for i in range(replicas)])

    def to_expert(chunks):
        return [
            lax.ppermute(value, "expert", [(i, i ^ ke) for i in range(groups)]) if ke else value
            for ke, value in enumerate(chunks)
        ]

    chunk = [shape((capacity, width))] * groups
    by_x = [shape((slots, half))] * spread
    in_own, out_own = w_in[0], w_out[0]
    pieces = call(
        bound(piece_kernel, replicas),
        [shape((part, 2 * feed // (replicas * PIECES)))] * PIECES,
        (in_own,),
        far=1,
        scratch_shapes=[pltpu.SemaphoreType.DMA((PIECES,))],
    )
    *chunks, turned, gate = call(
        bound(slot_kernel, groups, parts, capacity),
        [shape((2 * capacity, width))] * groups
        + [shape((count, slots)), shape((slots, 128), F32)],
        (route_ids.T, route_gates.T, served_order, tokens, cotangent),
        far=5,
        after=pieces[:1],
        scratch_shapes=[
            pltpu.VMEM(route_ids.shape[::-1], jnp.int32),
            pltpu.VMEM(route_gates.shape[::-1], F32),
            pltpu.VMEM(served_order.shape, jnp.int32),
            pltpu.VMEM(tokens.shape, BF16),
            pltpu.VMEM(cotangent.shape, BF16),
            pltpu.SemaphoreType.DMA((5,)),
        ],
    )
    in_sib, out_sib = to_core(in_own), to_core(out_own)
    *chunks, in_sib, out_sib = lax.optimization_barrier((*chunks, in_sib, out_sib))
    chunks = to_expert(chunks)
    shares = [to_x([piece] * (spread - 1)) for piece in pieces]
    shares = [lax.optimization_barrier((vs, chunks[1 + i]))[0] for i, vs in enumerate(shares)]
    shares = [[[v] + [to_replica(v, n) for n in range(1, replicas)] for v in vs] for vs in shares]
    early = shares[0][0][1:]
    rows, pre, *grads = call(
        bound(near_kernel, groups, spread, capacity),
        [shape((slots, width)), shape((slots, 2 * feed), F32)] + by_x,
        (*chunks, in_own, in_sib),
        after=early,
    )
    grads[1:] = to_x(grads[1:])
    back, *back_far = call(
        bound(back_kernel, spread),
        [shape((slots, feed), F32)] + [shape((slots, feed))] * (spread - 1),
        (*grads, out_own, out_sib),
    )
    backs = (back, *to_x(back_far))
    shares[-1], back = lax.optimization_barrier((shares[-1], back))
    pieces = []
    for kx in range(spread - 1):
        here = [shares[s][kx][n] for n in range(replicas) for s in range(PIECES)]
        pieces += here + [to_core(value) for value in here]
    hidden, pre = call(
        bound(hidden_kernel, replicas),
        [shape((slots, feed)), shape((slots, 2 * feed), F32)],
        (rows, pre, *pieces),
    )
    hidden = (hidden, *to_x([hidden] * (spread - 1)))
    d_rows = call(
        bound(d_rows_kernel, groups, spread, capacity, replicas),
        chunk,
        (pre, *backs, in_own, in_sib, *pieces),
        scratch_shapes=[pltpu.VMEM((slots, 2 * feed), BF16)],
    )
    d_rows = to_expert(d_rows)
    near, *far = call(bound(expert_out_kernel, spread), by_x, (*hidden, out_own, out_sib))
    expert_out = call(
        bound(join_kernel, groups, spread, capacity), chunk, (near, *to_x(far))
    )
    expert_out = to_expert(expert_out)
    own, sib, all_hidden = call(
        bound(gather_kernel, spread),
        [shape((spread * slots, part))] * 2 + [shape((spread * slots, feed))],
        (*grads, *hidden),
    )
    d_w_out, token = call(
        weight_kernel,
        [shape((part, feed), F32)],
        (own, all_hidden, to_core(sib), to_core(all_hidden)),
        token=True,
    )

    def scattered(kernel, operands, **kw):
        return call(
            kernel,
            [shape((count, width))],
            operands,
            out_specs=[pl.BlockSpec(memory_space=pltpu.HBM)]
            + [pl.BlockSpec(memory_space=pltpu.VMEM)] * kw.get("token", False),
            scratch_shapes=[
                pltpu.VMEM((parts, count, part), BF16),
                pltpu.SemaphoreType.DMA((parts,)),
            ],
            **kw,
        )

    d_tokens, token = scattered(
        lambda turned, *refs: combine_kernel(groups, parts, turned, None, *refs),
        (turned, *d_rows),
        after=(token,),
        token=True,
    )
    (combined,) = scattered(
        bound(combine_kernel, groups, parts), (turned, gate, *expert_out), after=(token,)
    )
    return combined, d_tokens, d_w_out[None]


def solution(mesh):
    rows = P(("replica", "expert", "fsdp"), None)
    weights = P("expert", "fsdp", None)
    return jax.shard_map(
        per_device,
        mesh=mesh,
        in_specs=(rows,) * 5 + (weights,) * 2,
        out_specs=(rows, rows, P(("replica", "expert"), "fsdp", None)),
        check_vma=False,
    )
```

```python
import jax
import jax.numpy as jnp
from jax import lax
from jax.experimental import pallas as pl
from jax.experimental.pallas import tpu as pltpu
from jax.sharding import PartitionSpec as P

EXPERTS = 128
CORES = 2
PIECES = 3
VMEM = 40 * 1024 * 1024
F32 = jnp.float32
BF16 = jnp.bfloat16


def product(left, right, left_dim, right_dim, **kw):
    return lax.dot_general(
        left, right, (((left_dim,), (right_dim,)), ((), ())), preferred_element_type=F32, **kw
    )


def call(body, out_shape, args, far=0, cost=0, after=(), token=False, **kw):
    out_shape = [*out_shape] + [shape((8, 128), F32)] * token
    specs = [pl.BlockSpec(memory_space=pltpu.VMEM)] * (len(args) - far)
    specs += [pl.BlockSpec(memory_space=pltpu.HBM)] * far
    specs += [pl.BlockSpec(memory_space=pl.ANY)] * len(after)
    kw.setdefault("out_specs", [pl.BlockSpec(memory_space=pltpu.VMEM)] * len(out_shape))
    args = [
        pltpu.with_memory_space_constraint(arg, pltpu.HBM) if i >= len(args) - far else arg
        for i, arg in enumerate(args)
    ]
    count, first, last = len(args), len(args) + len(after), len(args) + len(after) + len(out_shape)

    def kernel(*refs):
        if token:
            refs[last - 1][...] = jnp.zeros(refs[last - 1].shape, F32)
        body(*refs[:count], *refs[first : last - token], *refs[last:])

    return pl.pallas_call(
        kernel,
        out_shape=out_shape,
        in_specs=specs,
        compiler_params=pltpu.CompilerParams(vmem_limit_bytes=VMEM),
        cost_estimate=pl.CostEstimate(flops=cost, bytes_accessed=0, transcendentals=0),
        **kw,
    )(*args, *after)


def shape(dims, kind=BF16):
    return jax.ShapeDtypeStruct(dims, kind)


def columns(k, part):
    return pl.ds(pl.multiple_of((lax.axis_index("fsdp") ^ k) * part, part), part)


def slot_kernel(groups, parts, capacity, *refs):
    sources, chunks, refs = refs[:5], refs[5 : 5 + groups], refs[5 + groups :]
    turned_out, gate_out, ids, gates, order, tok, cot, sems = refs
    copies = [
        pltpu.make_async_copy(source, target, sems.at[i])
        for i, (source, target) in enumerate(zip(sources, (ids, gates, order, tok, cot)))
    ]
    for copy in copies:
        copy.start()
    for copy in copies[:3]:
        copy.wait()
    choices, count = ids.shape
    slots = groups * capacity
    part = tok.shape[1] // parts
    slot = lax.broadcasted_iota(jnp.int32, (slots, count), 0)
    wanted = ((slot // capacity) ^ lax.axis_index("expert")) * (EXPERTS // groups)
    routed = jnp.zeros((slots, count), F32)
    gate = jnp.zeros((slots, count), F32)
    for k in range(choices):
        hit = ids[k : k + 1, :] == wanted
        routed = jnp.where(hit, 1.0, routed)
        gate = jnp.where(hit, gates[k : k + 1, :], gate)
    row = lax.broadcasted_iota(jnp.int32, (count, count), 0)
    col = lax.broadcasted_iota(jnp.int32, (count, count), 1)
    served = jnp.where(order[...] == row, 1.0, 0.0).astype(BF16)
    earlier = jnp.where(row < col, 1.0, 0.0).astype(BF16)
    by_rank = product(routed.astype(BF16), served, 1, 0)
    before = product(by_rank.astype(BF16), earlier, 1, 0)
    taken = jnp.where(before.astype(jnp.int32) == slot % capacity, by_rank, 0.0).astype(BF16)
    pick = product(taken, served, 1, 1)
    turned_out[...] = product(served, taken, 1, 1).astype(BF16)
    slot_gate = jnp.sum(pick * gate, axis=1, keepdims=True)
    gate_out[...] = jnp.broadcast_to(slot_gate, gate_out.shape)
    pick = pick.astype(BF16)
    for copy, source, scale, top in ((copies[3], tok, None, 0), (copies[4], cot, slot_gate, capacity)):
        copy.wait()
        for k in range(parts):
            rows = product(pick, source[:, columns(k, part)], 1, 0)
            rows = (rows if scale is None else scale * rows).astype(BF16)
            for ke in range(groups):
                chunks[ke][top : top + capacity, k * part : (k + 1) * part] = rows[
                    ke * capacity : (ke + 1) * capacity
                ]


def piece_columns(n, s, width, replicas):
    at = ((lax.axis_index("replica") ^ n) * PIECES + s) * width
    return pl.ds(pl.multiple_of(at, 128), width)


def piece_kernel(replicas, w_in, *refs):
    *outs, sems = refs
    copies = []
    for s, out in enumerate(outs):
        cols = piece_columns(0, s, out.shape[1], replicas)
        copies.append(pltpu.make_async_copy(w_in.at[:, cols], out, sems.at[s]))
        copies[-1].start()
    for copy in copies:
        copy.wait()


def near_kernel(groups, spread, capacity, *refs):
    chunks, (own, sib, rows, pre, *grads) = refs[:groups], refs[groups:]
    part = own.shape[0]
    half = CORES * part
    rows[...] = jnp.concatenate([c[:capacity] for c in chunks], axis=0)
    for kx in range(spread):
        cols = slice(kx * half, (kx + 1) * half)
        grads[kx][...] = jnp.concatenate([c[capacity:, cols] for c in chunks], axis=0)
    total = product(rows[:, :part], own[...], 1, 0)
    pre[...] = total + product(rows[:, part : 2 * part], sib[...], 1, 0)


def back_kernel(spread, *refs):
    left, (own, sib, *outs) = refs[:spread], refs[spread:]
    part = own.shape[0]
    count = left[0].shape[0]
    rows = jnp.concatenate([r[...] for r in left], axis=0)
    total = product(rows[:, :part], own[...], 1, 0) + product(rows[:, part:], sib[...], 1, 0)
    for kx in range(spread):
        outs[kx][...] = total[kx * count : (kx + 1) * count].astype(outs[kx].dtype)


def hidden_kernel(replicas, rows, pre_in, *refs):
    pieces, (hidden, pre) = refs[:-2], refs[-2:]
    part, width = pieces[0].shape
    feed = hidden.shape[1]
    each = PIECES * replicas
    pre[...] = pre_in[...]
    for i in range(each):
        total = 0.0
        for k, piece in enumerate(pieces[i::each], CORES):
            total += product(rows[:, k * part : (k + 1) * part], piece[...], 1, 0)
        pre[:, piece_columns(i // PIECES, i % PIECES, width, replicas)] += total
    gate_act, up_act = pre[:, :feed], pre[:, feed:]
    hidden[...] = (gate_act * (1.0 / (1.0 + jnp.exp(-gate_act))) * up_act).astype(BF16)


def d_rows_kernel(groups, spread, capacity, replicas, pre, *refs):
    backs, (own, sib), refs = refs[:spread], refs[spread : spread + 2], refs[spread + 2 :]
    pieces, chunks, d_pre = refs[: -groups - 1], refs[-groups - 1 : -1], refs[-1]
    part = own.shape[0]
    width = pieces[0].shape[1]
    each = PIECES * replicas
    back = backs[0][...]
    for ref in backs[1:]:
        back += ref[...].astype(F32)
    feed = back.shape[1]
    gate_act, up_act = pre[:, :feed], pre[:, feed:]
    sig = 1.0 / (1.0 + jnp.exp(-gate_act))
    d_pre[:, :feed] = (back * up_act * (sig * (1.0 + gate_act * (1.0 - sig)))).astype(BF16)
    d_pre[:, feed:] = (back * (gate_act * sig)).astype(BF16)

    def store(k, value):
        value = value.astype(BF16)
        for ke in range(groups):
            chunks[ke][:, k * part : (k + 1) * part] = value[ke * capacity : (ke + 1) * capacity]

    store(0, product(d_pre[...], own[...], 1, 1))
    store(1, product(d_pre[...], sib[...], 1, 1))
    for k in range(len(pieces) // each):
        total = 0.0
        for i, piece in enumerate(pieces[k * each : (k + 1) * each]):
            cols = piece_columns(i // PIECES, i % PIECES, width, replicas)
            total += product(d_pre[:, cols], piece[...], 1, 1)
        store(CORES + k, total)


def expert_out_kernel(spread, *refs):
    left, (own, sib, *outs) = refs[:spread], refs[spread:]
    part = own.shape[0]
    count = left[0].shape[0]
    rows = jnp.concatenate([r[...] for r in left], axis=0)
    for kc, weight in enumerate((own, sib)):
        value = product(rows, weight[...], 1, 1).astype(BF16)
        for kx in range(spread):
            outs[kx][:, kc * part : (kc + 1) * part] = value[kx * count : (kx + 1) * count]


def join_kernel(groups, spread, capacity, *refs):
    by_x, chunks = refs[:spread], refs[spread:]
    half = by_x[0].shape[1]
    for ke in range(groups):
        for kx in range(spread):
            chunks[ke][:, kx * half : (kx + 1) * half] = by_x[kx][
                ke * capacity : (ke + 1) * capacity
            ]


def gather_kernel(spread, *refs):
    grads, hidden, (own, sib, all_hidden) = refs[:spread], refs[spread : 2 * spread], refs[2 * spread :]
    part = own.shape[1]
    count = grads[0].shape[0]
    for kx in range(spread):
        at = pl.ds(kx * count, count)
        own[at] = grads[kx][:, :part]
        sib[at] = grads[kx][:, part:]
        all_hidden[at] = hidden[kx][...]


def weight_kernel(own, hidden, sib, sib_hidden, out):
    left = jnp.concatenate([own[...], sib[...]], axis=0)
    right = jnp.concatenate([hidden[...], sib_hidden[...]], axis=0)
    out[...] = product(left, right, 0, 0)


def combine_kernel(groups, parts, turned, gate, *refs):
    chunks, (out, held, sems) = refs[:groups], refs[groups:]
    part = out.shape[1] // parts
    twice = jnp.concatenate([turned[...], turned[...]], axis=1)
    copies = []
    for k in range(parts):
        rows = jnp.concatenate([c[:, k * part : (k + 1) * part] for c in chunks], axis=0)
        if gate is None:
            held[k] = product(turned[...], rows, 1, 0).astype(BF16)
        else:
            weighted = rows.astype(F32) * gate[:, :1]
            high = weighted.astype(BF16)
            low = (weighted - high.astype(F32)).astype(BF16)
            both = jnp.concatenate([high, low], axis=0)
            held[k] = product(twice, both, 1, 0).astype(BF16)
        copies.append(pltpu.make_async_copy(held.at[k], out.at[:, columns(k, part)], sems.at[k]))
        copies[-1].start()
    for copy in copies:
        copy.wait()


def per_device(tokens, cotangent, route_ids, route_gates, served_order, w_in, w_out):
    replicas = lax.axis_size("replica")
    groups = lax.axis_size("expert")
    parts = lax.axis_size("fsdp")
    spread = parts // CORES
    count, width = tokens.shape
    capacity = count * route_ids.shape[1] // EXPERTS
    feed = w_out.shape[2]
    slots = groups * capacity
    half = width // spread
    part = width // parts

    def bound(kernel, *sizes):
        return lambda *refs: kernel(*sizes, *refs)

    def to_core(value):
        return lax.ppermute(value, "fsdp", [(i, i ^ 1) for i in range(parts)])

    def to_x(values):
        return [
            lax.ppermute(value, "fsdp", [(i, i ^ ((k + 1) * CORES)) for i in range(parts)])
            for k, value in enumerate(values)
        ]

    def to_replica(value, n):
        return lax.ppermute(value, "replica", [(i, i ^ n) for i in range(replicas)])

    def to_expert(chunks):
        return [
            lax.ppermute(value, "expert", [(i, i ^ ke) for i in range(groups)]) if ke else value
            for ke, value in enumerate(chunks)
        ]

    chunk = [shape((capacity, width))] * groups
    by_x = [shape((slots, half))] * spread
    in_own, out_own = w_in[0], w_out[0]
    pieces = call(
        bound(piece_kernel, replicas),
        [shape((part, 2 * feed // (replicas * PIECES)))] * PIECES,
        (in_own,),
        far=1,
        scratch_shapes=[pltpu.SemaphoreType.DMA((PIECES,))],
    )
    *chunks, turned, gate = call(
        bound(slot_kernel, groups, parts, capacity),
        [shape((2 * capacity, width))] * groups
        + [shape((count, slots)), shape((slots, 128), F32)],
        (route_ids.T, route_gates.T, served_order, tokens, cotangent),
        far=5,
        after=pieces[:1],
        scratch_shapes=[
            pltpu.VMEM(route_ids.shape[::-1], jnp.int32),
            pltpu.VMEM(route_gates.shape[::-1], F32),
            pltpu.VMEM(served_order.shape, jnp.int32),
            pltpu.VMEM(tokens.shape, BF16),
            pltpu.VMEM(cotangent.shape, BF16),
            pltpu.SemaphoreType.DMA((5,)),
        ],
    )
    in_sib, out_sib = to_core(in_own), to_core(out_own)
    *chunks, in_sib, out_sib = lax.optimization_barrier((*chunks, in_sib, out_sib))
    chunks = to_expert(chunks)
    shares = [to_x([piece] * (spread - 1)) for piece in pieces]
    shares[0] = lax.optimization_barrier((shares[0], chunks[1]))[0]
    shares = [[[v] + [to_replica(v, n) for n in range(1, replicas)] for v in vs] for vs in shares]
    early = shares[0][0][1:]
    rows, pre, *grads = call(
        bound(near_kernel, groups, spread, capacity),
        [shape((slots, width)), shape((slots, 2 * feed), F32)] + by_x,
        (*chunks, in_own, in_sib),
        after=early,
    )
    grads[1:] = to_x(grads[1:])
    back, *back_far = call(
        bound(back_kernel, spread),
        [shape((slots, feed), F32)] + [shape((slots, feed))] * (spread - 1),
        (*grads, out_own, out_sib),
    )
    backs = (back, *to_x(back_far))
    shares[-1] = lax.optimization_barrier((shares[-1], *backs[1:]))[0]
    pieces = []
    for kx in range(spread - 1):
        here = [shares[s][kx][n] for n in range(replicas) for s in range(PIECES)]
        pieces += here + [to_core(value) for value in here]
    hidden, pre = call(
        bound(hidden_kernel, replicas),
        [shape((slots, feed)), shape((slots, 2 * feed), F32)],
        (rows, pre, *pieces),
    )
    hidden = (hidden, *to_x([hidden] * (spread - 1)))
    d_rows = call(
        bound(d_rows_kernel, groups, spread, capacity, replicas),
        chunk,
        (pre, *backs, in_own, in_sib, *pieces),
        scratch_shapes=[pltpu.VMEM((slots, 2 * feed), BF16)],
    )
    d_rows = to_expert(d_rows)
    near, *far = call(
        bound(expert_out_kernel, spread), by_x, (*hidden, out_own, out_sib), after=d_rows[1:2]
    )
    expert_out = call(
        bound(join_kernel, groups, spread, capacity), chunk, (near, *to_x(far))
    )
    expert_out = to_expert(expert_out)
    own, sib, all_hidden = call(
        bound(gather_kernel, spread),
        [shape((spread * slots, part))] * 2 + [shape((spread * slots, feed))],
        (*grads, *hidden),
    )
    d_w_out, token = call(
        weight_kernel,
        [shape((part, feed), F32)],
        (own, all_hidden, to_core(sib), to_core(all_hidden)),
        token=True,
    )

    def scattered(kernel, operands, **kw):
        return call(
            kernel,
            [shape((count, width))],
            operands,
            out_specs=[pl.BlockSpec(memory_space=pltpu.HBM)]
            + [pl.BlockSpec(memory_space=pltpu.VMEM)] * kw.get("token", False),
            scratch_shapes=[
                pltpu.VMEM((parts, count, part), BF16),
                pltpu.SemaphoreType.DMA((parts,)),
            ],
            **kw,
        )

    d_tokens, token = scattered(
        lambda turned, *refs: combine_kernel(groups, parts, turned, None, *refs),
        (turned, *d_rows),
        after=(token,),
        token=True,
    )
    (combined,) = scattered(
        bound(combine_kernel, groups, parts), (turned, gate, *expert_out), after=(token,)
    )
    return combined, d_tokens, d_w_out[None]


def solution(mesh):
    rows = P(("replica", "expert", "fsdp"), None)
    weights = P("expert", "fsdp", None)
    return jax.shard_map(
        per_device,
        mesh=mesh,
        in_specs=(rows,) * 5 + (weights,) * 2,
        out_specs=(rows, rows, P(("replica", "expert"), "fsdp", None)),
        check_vma=False,
    )
```

```python
import jax
import jax.numpy as jnp
from jax import lax
from jax.experimental import pallas as pl
from jax.experimental.pallas import tpu as pltpu
from jax.sharding import PartitionSpec as P

EXPERTS = 128
CORES = 2
VMEM = 40 * 1024 * 1024
F32 = jnp.float32
BF16 = jnp.bfloat16


def product(left, right, left_dim, right_dim, **kw):
    return lax.dot_general(
        left, right, (((left_dim,), (right_dim,)), ((), ())), preferred_element_type=F32, **kw
    )


def call(body, out_shape, args, far=0, cost=0, after=(), token=False, **kw):
    out_shape = [*out_shape] + [shape((8, 128), F32)] * token
    specs = [pl.BlockSpec(memory_space=pltpu.VMEM)] * (len(args) - far)
    specs += [pl.BlockSpec(memory_space=pltpu.HBM)] * far
    specs += [pl.BlockSpec(memory_space=pl.ANY)] * len(after)
    kw.setdefault("out_specs", [pl.BlockSpec(memory_space=pltpu.VMEM)] * len(out_shape))
    args = [
        pltpu.with_memory_space_constraint(arg, pltpu.HBM) if i >= len(args) - far else arg
        for i, arg in enumerate(args)
    ]
    count, first, last = len(args), len(args) + len(after), len(args) + len(after) + len(out_shape)

    def kernel(*refs):
        if token:
            refs[last - 1][...] = jnp.zeros(refs[last - 1].shape, F32)
        body(*refs[:count], *refs[first : last - token], *refs[last:])

    return pl.pallas_call(
        kernel,
        out_shape=out_shape,
        in_specs=specs,
        compiler_params=pltpu.CompilerParams(vmem_limit_bytes=VMEM),
        cost_estimate=pl.CostEstimate(flops=cost, bytes_accessed=0, transcendentals=0),
        **kw,
    )(*args, *after)


def shape(dims, kind=BF16):
    return jax.ShapeDtypeStruct(dims, kind)


def columns(k, part):
    return pl.ds(pl.multiple_of((lax.axis_index("fsdp") ^ k) * part, part), part)


def slot_kernel(spread, *refs):
    sources, rows_out, grads_out, refs = refs[:5], refs[5 : 5 + spread], refs[5 + spread : 5 + 2 * spread], refs[5 + 2 * spread :]
    turned_out, gate_out, ids, gates, order, tok, cot, sems = refs
    parts = spread * CORES
    copies = [
        pltpu.make_async_copy(source, target, sems.at[i])
        for i, (source, target) in enumerate(zip(sources, (ids, gates, order, tok, cot)))
    ]
    for copy in copies:
        copy.start()
    for copy in copies[:3]:
        copy.wait()
    choices, count = ids.shape
    slots = gate_out.shape[0]
    groups = lax.axis_size("expert")
    capacity = slots // groups
    part = tok.shape[1] // parts
    slot = lax.broadcasted_iota(jnp.int32, (slots, count), 0)
    wanted = ((slot // capacity) ^ lax.axis_index("expert")) * (EXPERTS // groups)
    routed = jnp.zeros((slots, count), F32)
    gate = jnp.zeros((slots, count), F32)
    for k in range(choices):
        hit = ids[k : k + 1, :] == wanted
        routed = jnp.where(hit, 1.0, routed)
        gate = jnp.where(hit, gates[k : k + 1, :], gate)
    row = lax.broadcasted_iota(jnp.int32, (count, count), 0)
    col = lax.broadcasted_iota(jnp.int32, (count, count), 1)
    served = jnp.where(order[...] == row, 1.0, 0.0).astype(BF16)
    earlier = jnp.where(row < col, 1.0, 0.0).astype(BF16)
    by_rank = product(routed.astype(BF16), served, 1, 0)
    before = product(by_rank.astype(BF16), earlier, 1, 0)
    taken = jnp.where(before.astype(jnp.int32) == slot % capacity, by_rank, 0.0).astype(BF16)
    pick = product(taken, served, 1, 1)
    turned_out[...] = product(served, taken, 1, 1).astype(BF16)
    slot_gate = jnp.sum(pick * gate, axis=1, keepdims=True)
    gate_out[...] = jnp.broadcast_to(slot_gate, gate_out.shape)
    pick = pick.astype(BF16)
    for copy, source, scale, outs in (
        (copies[3], tok, None, rows_out),
        (copies[4], cot, slot_gate, grads_out),
    ):
        copy.wait()
        for k in reversed(range(parts)):
            value = product(pick, source[:, columns(k, part)], 1, 0)
            value = value if scale is None else scale * value
            to = pl.ds((k % CORES) * part, part)
            outs[k // CORES][:, to] = value.astype(BF16)


def join_kernel(groups, spread, capacity, *refs):
    by_x, chunks = refs[:spread], refs[spread:]
    half = by_x[0].shape[1]
    for ke in range(groups):
        for kx in range(spread):
            chunks[ke][:, kx * half : (kx + 1) * half] = by_x[kx][
                ke * capacity : (ke + 1) * capacity
            ]


def far_kernel(groups, spread, capacity, *refs):
    by_e, by_x = refs[:groups], refs[groups:]
    for ke in range(groups):
        for kx in range(1, spread):
            by_x[kx - 1][ke * capacity : (ke + 1) * capacity] = by_e[ke][
                kx * capacity : (kx + 1) * capacity
            ]


def partial(groups, spread, refs, outs):
    chunks, (own, sib) = refs[:groups], refs[groups:]
    part = own.shape[0]
    half = CORES * part
    rows = jnp.concatenate(
        [c[:, kx * half : (kx + 1) * half] for kx in range(spread) for c in chunks], axis=0
    )
    total = product(rows[:, :part], own[...], 1, 0) + product(rows[:, part:], sib[...], 1, 0)
    slots = rows.shape[0] // spread
    for kx in range(spread):
        outs[kx][...] = total[kx * slots : (kx + 1) * slots].astype(outs[kx].dtype)
    return rows


def pre_kernel(groups, spread, *refs):
    partial(groups, spread, refs[: groups + 2], refs[groups + 2 :])


def back_kernel(groups, spread, *refs):
    own, sib, *outs = refs[groups + 2 :]
    rows = partial(groups, spread, refs[: groups + 2], outs)
    part = own.shape[1]
    own[...] = rows[:, :part]
    sib[...] = rows[:, part:]


def summed(refs):
    total = refs[0][...]
    for ref in refs[1:]:
        total += ref[...].astype(F32)
    return total


def hidden_kernel(*refs):
    pre, out = summed(refs[:-1]), refs[-1]
    feed = out.shape[1]
    gate_act, up_act = pre[:, :feed], pre[:, feed:]
    out[...] = (gate_act * (1.0 / (1.0 + jnp.exp(-gate_act))) * up_act).astype(BF16)


def d_pre_kernel(*refs):
    spread = len(refs) // 2
    pre, back, out = summed(refs[:spread]), summed(refs[spread:-1]), refs[-1]
    feed = back.shape[1]
    gate_act, up_act = pre[:, :feed], pre[:, feed:]
    sig = 1.0 / (1.0 + jnp.exp(-gate_act))
    out[:, :feed] = (back * up_act * (sig * (1.0 + gate_act * (1.0 - sig)))).astype(BF16)
    out[:, feed:] = (back * (gate_act * sig)).astype(BF16)


def width_product(left, weights, store):
    rows = jnp.concatenate([r[...] for r in left], axis=0)
    for kc, weight in enumerate(weights):
        store(kc, product(rows, weight[...], 1, 1).astype(BF16))


def expert_out_kernel(groups, spread, capacity, *refs):
    chunks = refs[-groups:]
    part = refs[spread].shape[0]

    def store(kc, value):
        for ke in range(groups):
            for kx in range(spread):
                at = (kx * groups + ke) * capacity
                chunks[ke][kx * capacity : (kx + 1) * capacity, kc * part : (kc + 1) * part] = value[
                    at : at + capacity
                ]

    width_product(refs[:spread], refs[spread : spread + CORES], store)


def d_rows_kernel(spread, *refs):
    outs = refs[-spread:]
    part = refs[spread].shape[0]
    slots = outs[0].shape[0]

    def store(kc, value):
        for kx in range(spread):
            outs[kx][:, kc * part : (kc + 1) * part] = value[kx * slots : (kx + 1) * slots]

    width_product(refs[:spread], refs[spread : spread + CORES], store)


def weight_kernel(spread, own, sib, *refs):
    hidden, sib_hidden, out = refs[:spread], refs[spread:-1], refs[-1]
    left = jnp.concatenate([own[...], sib[...]], axis=0)
    right = jnp.concatenate([r[...] for r in (*hidden, *sib_hidden)], axis=0)
    out[...] = product(left, right, 0, 0)


def scatter(turned, groups_of_rows, out, held, sems):
    part = held.shape[2]
    copies = []
    for k, rows in enumerate(groups_of_rows):
        held[k] = product(turned, rows, 1, 0).astype(BF16)
        copies.append(pltpu.make_async_copy(held.at[k], out.at[:, columns(k, part)], sems.at[k]))
        copies[-1].start()
    for copy in copies:
        copy.wait()


def combine_kernel(groups, parts, capacity, turned, gate, *refs):
    chunks, far, (out, held, sems) = refs[:groups], refs[groups:-3], refs[-3:]
    part = held.shape[2]

    def weighted(k):
        cols = slice((k % CORES) * part, (k % CORES + 1) * part)
        if k < CORES:
            rows = jnp.concatenate([c[:capacity, cols] for c in chunks], axis=0)
        else:
            rows = far[k // CORES - 1][:, cols]
        rows = rows.astype(F32) * gate[:, :1]
        high = rows.astype(BF16)
        return jnp.concatenate([high, (rows - high.astype(F32)).astype(BF16)], axis=0)

    twice = jnp.concatenate([turned[...], turned[...]], axis=1)
    scatter(twice, map(weighted, range(parts)), out, held, sems)


def d_tokens_kernel(groups, parts, turned, *refs):
    chunks, (out, held, sems) = refs[:groups], refs[groups:]
    part = held.shape[2]
    rows = (
        jnp.concatenate([c[:, k * part : (k + 1) * part] for c in chunks], axis=0)
        for k in range(parts)
    )
    scatter(turned[...], rows, out, held, sems)


def per_device(tokens, cotangent, route_ids, route_gates, served_order, w_in, w_out):
    groups = lax.axis_size("expert")
    parts = lax.axis_size("fsdp")
    spread = parts // CORES
    count, width = tokens.shape
    capacity = count * route_ids.shape[1] // EXPERTS
    feed = w_out.shape[2]
    slots = groups * capacity
    half = width // spread
    part = width // parts

    def bound(kernel, *sizes):
        return lambda *refs: kernel(*sizes, *refs)

    def to_core(value):
        return lax.ppermute(value, "fsdp", [(i, i ^ 1) for i in range(parts)])

    def to_x(values):
        return [
            lax.ppermute(value, "fsdp", [(i, i ^ ((k + 1) * CORES)) for i in range(parts)])
            for k, value in enumerate(values)
        ]

    def to_expert(chunks):
        return [
            lax.ppermute(value, "expert", [(i, i ^ ke) for i in range(groups)]) if ke else value
            for ke, value in enumerate(chunks)
        ]

    chunk = [shape((capacity, width))] * groups
    by_x = [shape((slots, half))] * spread
    in_own, out_own = w_in[0], w_out[0]
    in_sib, out_sib = to_core(in_own), to_core(out_own)
    outs = call(
        bound(slot_kernel, spread),
        by_x * 2 + [shape((count, slots)), shape((slots, 128), F32)],
        (route_ids.T, route_gates.T, served_order, tokens, cotangent),
        far=5,
        scratch_shapes=[
            pltpu.VMEM(route_ids.shape[::-1], jnp.int32),
            pltpu.VMEM(route_gates.shape[::-1], F32),
            pltpu.VMEM(served_order.shape, jnp.int32),
            pltpu.VMEM(tokens.shape, BF16),
            pltpu.VMEM(cotangent.shape, BF16),
            pltpu.SemaphoreType.DMA((5,)),
        ],
    )
    turned, gate = outs[-2:]
    rows = [outs[0], *to_x(outs[1:spread])]
    grads = [outs[spread], *to_x(outs[spread + 1 : 2 * spread])]
    rows, in_sib, out_sib = lax.optimization_barrier((rows, in_sib, out_sib))
    join = bound(join_kernel, groups, spread, capacity)
    rows = to_expert(call(join, chunk, rows))
    grads = to_expert(call(join, chunk, grads))
    pre, *pre_far = call(
        bound(pre_kernel, groups, spread),
        [shape((slots, 2 * feed), F32)] + [shape((slots, 2 * feed))] * (spread - 1),
        (*rows, in_own, in_sib),
    )
    pre = (pre, *to_x(pre_far))
    (hidden,) = call(hidden_kernel, [shape((slots, feed))], pre)
    hidden = (hidden, *to_x([hidden] * (spread - 1)))
    own_grads, sib_grads, back, *back_far = call(
        bound(back_kernel, groups, spread),
        [shape((spread * slots, part))] * 2
        + [shape((slots, feed), F32)]
        + [shape((slots, feed))] * (spread - 1),
        (*grads, out_own, out_sib),
        after=hidden[:1],
    )
    back = (back, *to_x(back_far))
    expert_out = to_expert(
        call(
            bound(expert_out_kernel, groups, spread, capacity),
            [shape((spread * capacity, half))] * groups,
            (*hidden, out_own, out_sib),
        )
    )
    (d_pre,) = call(
        d_pre_kernel, [shape((slots, 2 * feed))], (*pre, *back), after=expert_out[:1]
    )
    d_pre = (d_pre, *to_x([d_pre] * (spread - 1)))
    near, *far = call(bound(d_rows_kernel, spread), by_x, (*d_pre, in_own, in_sib))
    d_rows = to_expert(call(join, chunk, (near, *to_x(far))))
    far = to_x(
        call(bound(far_kernel, groups, spread, capacity), by_x[1:], expert_out)
    )
    d_w_out, token = call(
        bound(weight_kernel, spread),
        [shape((part, feed), F32)],
        (own_grads, to_core(sib_grads), *hidden, *[to_core(value) for value in hidden]),
        token=True,
    )

    def scattered(kernel, operands, **kw):
        return call(
            kernel,
            [shape((count, width))],
            operands,
            out_specs=[pl.BlockSpec(memory_space=pltpu.HBM)]
            + [pl.BlockSpec(memory_space=pltpu.VMEM)] * kw.get("token", False),
            scratch_shapes=[
                pltpu.VMEM((parts, count, part), BF16),
                pltpu.SemaphoreType.DMA((parts,)),
            ],
            **kw,
        )

    combined, token = scattered(
        bound(combine_kernel, groups, parts, capacity),
        (turned, gate, *expert_out, *far),
        after=(token,),
        token=True,
    )
    (d_tokens,) = scattered(
        bound(d_tokens_kernel, groups, parts), (turned, *d_rows), after=(token,)
    )
    return combined, d_tokens, d_w_out[None]


def solution(mesh):
    rows = P(("replica", "expert", "fsdp"), None)
    weights = P("expert", "fsdp", None)
    return jax.shard_map(
        per_device,
        mesh=mesh,
        in_specs=(rows,) * 5 + (weights,) * 2,
        out_specs=(rows, rows, P(("replica", "expert"), "fsdp", None)),
        check_vma=False,
    )
```

```python
import jax
import jax.numpy as jnp
from jax import lax
from jax.experimental import pallas as pl
from jax.experimental.pallas import tpu as pltpu
from jax.sharding import PartitionSpec as P

EXPERTS = 128
CORES = 2
BACK_COST = 12000000000
VMEM = 40 * 1024 * 1024
F32 = jnp.float32
BF16 = jnp.bfloat16


def product(left, right, left_dim, right_dim, **kw):
    return lax.dot_general(
        left, right, (((left_dim,), (right_dim,)), ((), ())), preferred_element_type=F32, **kw
    )


def call(body, out_shape, args, far=0, cost=0, after=(), token=False, **kw):
    out_shape = [*out_shape] + [shape((8, 128), F32)] * token
    specs = [pl.BlockSpec(memory_space=pltpu.VMEM)] * (len(args) - far)
    specs += [pl.BlockSpec(memory_space=pltpu.HBM)] * far
    specs += [pl.BlockSpec(memory_space=pl.ANY)] * len(after)
    kw.setdefault("out_specs", [pl.BlockSpec(memory_space=pltpu.VMEM)] * len(out_shape))
    args = [
        pltpu.with_memory_space_constraint(arg, pltpu.HBM) if i >= len(args) - far else arg
        for i, arg in enumerate(args)
    ]
    count, first, last = len(args), len(args) + len(after), len(args) + len(after) + len(out_shape)

    def kernel(*refs):
        if token:
            refs[last - 1][...] = jnp.zeros(refs[last - 1].shape, F32)
        body(*refs[:count], *refs[first : last - token], *refs[last:])

    return pl.pallas_call(
        kernel,
        out_shape=out_shape,
        in_specs=specs,
        compiler_params=pltpu.CompilerParams(vmem_limit_bytes=VMEM),
        cost_estimate=pl.CostEstimate(flops=cost, bytes_accessed=0, transcendentals=0),
        **kw,
    )(*args, *after)


def shape(dims, kind=BF16):
    return jax.ShapeDtypeStruct(dims, kind)


def columns(k, part):
    return pl.ds(pl.multiple_of((lax.axis_index("fsdp") ^ k) * part, part), part)


def slot_kernel(spread, *refs):
    sources, rows_out, grads_out, refs = refs[:5], refs[5 : 5 + spread], refs[5 + spread : 5 + 2 * spread], refs[5 + 2 * spread :]
    turned_out, gate_out, ids, gates, order, tok, cot, sems = refs
    parts = spread * CORES
    copies = [
        pltpu.make_async_copy(source, target, sems.at[i])
        for i, (source, target) in enumerate(zip(sources, (ids, gates, order, tok, cot)))
    ]
    for copy in copies:
        copy.start()
    for copy in copies[:3]:
        copy.wait()
    choices, count = ids.shape
    slots = gate_out.shape[0]
    groups = lax.axis_size("expert")
    capacity = slots // groups
    part = tok.shape[1] // parts
    slot = lax.broadcasted_iota(jnp.int32, (slots, count), 0)
    wanted = ((slot // capacity) ^ lax.axis_index("expert")) * (EXPERTS // groups)
    routed = jnp.zeros((slots, count), F32)
    gate = jnp.zeros((slots, count), F32)
    for k in range(choices):
        hit = ids[k : k + 1, :] == wanted
        routed = jnp.where(hit, 1.0, routed)
        gate = jnp.where(hit, gates[k : k + 1, :], gate)
    row = lax.broadcasted_iota(jnp.int32, (count, count), 0)
    col = lax.broadcasted_iota(jnp.int32, (count, count), 1)
    served = jnp.where(order[...] == row, 1.0, 0.0).astype(BF16)
    earlier = jnp.where(row < col, 1.0, 0.0).astype(BF16)
    by_rank = product(routed.astype(BF16), served, 1, 0)
    before = product(by_rank.astype(BF16), earlier, 1, 0)
    taken = jnp.where(before.astype(jnp.int32) == slot % capacity, by_rank, 0.0).astype(BF16)
    pick = product(taken, served, 1, 1)
    turned_out[...] = product(served, taken, 1, 1).astype(BF16)
    slot_gate = jnp.sum(pick * gate, axis=1, keepdims=True)
    gate_out[...] = jnp.broadcast_to(slot_gate, gate_out.shape)
    pick = pick.astype(BF16)
    for copy, source, scale, outs in (
        (copies[3], tok, None, rows_out),
        (copies[4], cot, slot_gate, grads_out),
    ):
        copy.wait()
        for k in reversed(range(parts)):
            value = product(pick, source[:, columns(k, part)], 1, 0)
            value = value if scale is None else scale * value
            to = pl.ds((k % CORES) * part, part)
            outs[k // CORES][:, to] = value.astype(BF16)


def join_kernel(groups, spread, capacity, *refs):
    by_x, chunks = refs[:spread], refs[spread:]
    half = by_x[0].shape[1]
    for ke in range(groups):
        for kx in range(spread):
            chunks[ke][:, kx * half : (kx + 1) * half] = by_x[kx][
                ke * capacity : (ke + 1) * capacity
            ]


def far_kernel(groups, spread, capacity, *refs):
    by_e, by_x = refs[:groups], refs[groups:]
    for ke in range(groups):
        for kx in range(1, spread):
            by_x[kx - 1][ke * capacity : (ke + 1) * capacity] = by_e[ke][
                kx * capacity : (kx + 1) * capacity
            ]


def partial(groups, spread, refs, outs):
    chunks, (own, sib) = refs[:groups], refs[groups:]
    part = own.shape[0]
    half = CORES * part
    rows = jnp.concatenate(
        [c[:, kx * half : (kx + 1) * half] for kx in range(spread) for c in chunks], axis=0
    )
    total = product(rows[:, :part], own[...], 1, 0) + product(rows[:, part:], sib[...], 1, 0)
    slots = rows.shape[0] // spread
    for kx in range(spread):
        outs[kx][...] = total[kx * slots : (kx + 1) * slots].astype(outs[kx].dtype)
    return rows


def pre_kernel(groups, spread, *refs):
    partial(groups, spread, refs[: groups + 2], refs[groups + 2 :])


def back_kernel(groups, spread, *refs):
    own, sib, *outs = refs[groups + 2 :]
    rows = partial(groups, spread, refs[: groups + 2], outs)
    part = own.shape[1]
    own[...] = rows[:, :part]
    sib[...] = rows[:, part:]


def summed(refs):
    total = refs[0][...]
    for ref in refs[1:]:
        total += ref[...].astype(F32)
    return total


def hidden_kernel(*refs):
    pre, out = summed(refs[:-1]), refs[-1]
    feed = out.shape[1]
    gate_act, up_act = pre[:, :feed], pre[:, feed:]
    out[...] = (gate_act * (1.0 / (1.0 + jnp.exp(-gate_act))) * up_act).astype(BF16)


def d_pre_kernel(*refs):
    spread = len(refs) // 2
    pre, back, out = summed(refs[:spread]), summed(refs[spread:-1]), refs[-1]
    feed = back.shape[1]
    gate_act, up_act = pre[:, :feed], pre[:, feed:]
    sig = 1.0 / (1.0 + jnp.exp(-gate_act))
    out[:, :feed] = (back * up_act * (sig * (1.0 + gate_act * (1.0 - sig)))).astype(BF16)
    out[:, feed:] = (back * (gate_act * sig)).astype(BF16)


def width_product(left, weights, store):
    rows = jnp.concatenate([r[...] for r in left], axis=0)
    for kc, weight in enumerate(weights):
        store(kc, product(rows, weight[...], 1, 1).astype(BF16))


def expert_out_kernel(groups, spread, capacity, *refs):
    chunks = refs[-groups:]
    part = refs[spread].shape[0]

    def store(kc, value):
        for ke in range(groups):
            for kx in range(spread):
                at = (kx * groups + ke) * capacity
                chunks[ke][kx * capacity : (kx + 1) * capacity, kc * part : (kc + 1) * part] = value[
                    at : at + capacity
                ]

    width_product(refs[:spread], refs[spread : spread + CORES], store)


def d_rows_kernel(spread, *refs):
    outs = refs[-spread:]
    part = refs[spread].shape[0]
    slots = outs[0].shape[0]

    def store(kc, value):
        for kx in range(spread):
            outs[kx][:, kc * part : (kc + 1) * part] = value[kx * slots : (kx + 1) * slots]

    width_product(refs[:spread], refs[spread : spread + CORES], store)


def weight_kernel(spread, own, sib, *refs):
    hidden, sib_hidden, out = refs[:spread], refs[spread:-1], refs[-1]
    left = jnp.concatenate([own[...], sib[...]], axis=0)
    right = jnp.concatenate([r[...] for r in (*hidden, *sib_hidden)], axis=0)
    out[...] = product(left, right, 0, 0)


def scatter(turned, groups_of_rows, out, held, sems):
    part = held.shape[2]
    copies = []
    for k, rows in enumerate(groups_of_rows):
        held[k] = product(turned, rows, 1, 0).astype(BF16)
        copies.append(pltpu.make_async_copy(held.at[k], out.at[:, columns(k, part)], sems.at[k]))
        copies[-1].start()
    for copy in copies:
        copy.wait()


def combine_kernel(groups, parts, capacity, turned, gate, *refs):
    chunks, far, (out, held, sems) = refs[:groups], refs[groups:-3], refs[-3:]
    part = held.shape[2]

    def weighted(k):
        cols = slice((k % CORES) * part, (k % CORES + 1) * part)
        if k < CORES:
            rows = jnp.concatenate([c[:capacity, cols] for c in chunks], axis=0)
        else:
            rows = far[k // CORES - 1][:, cols]
        rows = rows.astype(F32) * gate[:, :1]
        high = rows.astype(BF16)
        return jnp.concatenate([high, (rows - high.astype(F32)).astype(BF16)], axis=0)

    twice = jnp.concatenate([turned[...], turned[...]], axis=1)
    scatter(twice, map(weighted, range(parts)), out, held, sems)


def d_tokens_kernel(groups, parts, turned, *refs):
    chunks, (out, held, sems) = refs[:groups], refs[groups:]
    part = held.shape[2]
    rows = (
        jnp.concatenate([c[:, k * part : (k + 1) * part] for c in chunks], axis=0)
        for k in range(parts)
    )
    scatter(turned[...], rows, out, held, sems)


def per_device(tokens, cotangent, route_ids, route_gates, served_order, w_in, w_out):
    groups = lax.axis_size("expert")
    parts = lax.axis_size("fsdp")
    spread = parts // CORES
    count, width = tokens.shape
    capacity = count * route_ids.shape[1] // EXPERTS
    feed = w_out.shape[2]
    slots = groups * capacity
    half = width // spread
    part = width // parts

    def bound(kernel, *sizes):
        return lambda *refs: kernel(*sizes, *refs)

    def to_core(value):
        return lax.ppermute(value, "fsdp", [(i, i ^ 1) for i in range(parts)])

    def to_x(values):
        return [
            lax.ppermute(value, "fsdp", [(i, i ^ ((k + 1) * CORES)) for i in range(parts)])
            for k, value in enumerate(values)
        ]

    def to_expert(chunks):
        return [
            lax.ppermute(value, "expert", [(i, i ^ ke) for i in range(groups)]) if ke else value
            for ke, value in enumerate(chunks)
        ]

    chunk = [shape((capacity, width))] * groups
    by_x = [shape((slots, half))] * spread
    in_own, out_own = w_in[0], w_out[0]
    in_sib, out_sib = to_core(in_own), to_core(out_own)
    outs = call(
        bound(slot_kernel, spread),
        by_x * 2 + [shape((count, slots)), shape((slots, 128), F32)],
        (route_ids.T, route_gates.T, served_order, tokens, cotangent),
        far=5,
        scratch_shapes=[
            pltpu.VMEM(route_ids.shape[::-1], jnp.int32),
            pltpu.VMEM(route_gates.shape[::-1], F32),
            pltpu.VMEM(served_order.shape, jnp.int32),
            pltpu.VMEM(tokens.shape, BF16),
            pltpu.VMEM(cotangent.shape, BF16),
            pltpu.SemaphoreType.DMA((5,)),
        ],
    )
    turned, gate = outs[-2:]
    rows = [outs[0], *to_x(outs[1:spread])]
    grads = [outs[spread], *to_x(outs[spread + 1 : 2 * spread])]
    rows, in_sib, out_sib = lax.optimization_barrier((rows, in_sib, out_sib))
    join = bound(join_kernel, groups, spread, capacity)
    rows = to_expert(call(join, chunk, rows))
    grads = to_expert(call(join, chunk, grads))
    pre, *pre_far = call(
        bound(pre_kernel, groups, spread),
        [shape((slots, 2 * feed), F32)] + [shape((slots, 2 * feed))] * (spread - 1),
        (*rows, in_own, in_sib),
    )
    pre = (pre, *to_x(pre_far))
    (hidden,) = call(hidden_kernel, [shape((slots, feed))], pre)
    hidden = (hidden, *to_x([hidden] * (spread - 1)))
    own_grads, sib_grads, back, *back_far = call(
        bound(back_kernel, groups, spread),
        [shape((spread * slots, part))] * 2
        + [shape((slots, feed), F32)]
        + [shape((slots, feed))] * (spread - 1),
        (*grads, out_own, out_sib),
        cost=BACK_COST,
    )
    back = (back, *to_x(back_far))
    expert_out = to_expert(
        call(
            bound(expert_out_kernel, groups, spread, capacity),
            [shape((spread * capacity, half))] * groups,
            (*hidden, out_own, out_sib),
        )
    )
    (d_pre,) = call(d_pre_kernel, [shape((slots, 2 * feed))], (*pre, *back))
    d_pre = (d_pre, *to_x([d_pre] * (spread - 1)))
    near, *far = call(
        bound(d_rows_kernel, spread), by_x, (*d_pre, in_own, in_sib), after=expert_out[1:2]
    )
    d_rows = to_expert(call(join, chunk, (near, *to_x(far))))
    far = to_x(
        call(bound(far_kernel, groups, spread, capacity), by_x[1:], expert_out)
    )
    d_w_out, token = call(
        bound(weight_kernel, spread),
        [shape((part, feed), F32)],
        (own_grads, to_core(sib_grads), *hidden, *[to_core(value) for value in hidden]),
        token=True,
    )

    def scattered(kernel, operands, **kw):
        return call(
            kernel,
            [shape((count, width))],
            operands,
            out_specs=[pl.BlockSpec(memory_space=pltpu.HBM)]
            + [pl.BlockSpec(memory_space=pltpu.VMEM)] * kw.get("token", False),
            scratch_shapes=[
                pltpu.VMEM((parts, count, part), BF16),
                pltpu.SemaphoreType.DMA((parts,)),
            ],
            **kw,
        )

    combined, token = scattered(
        bound(combine_kernel, groups, parts, capacity),
        (turned, gate, *expert_out, *far),
        after=(token,),
        token=True,
    )
    (d_tokens,) = scattered(
        bound(d_tokens_kernel, groups, parts), (turned, *d_rows), after=(token,)
    )
    return combined, d_tokens, d_w_out[None]


def solution(mesh):
    rows = P(("replica", "expert", "fsdp"), None)
    weights = P("expert", "fsdp", None)
    return jax.shard_map(
        per_device,
        mesh=mesh,
        in_specs=(rows,) * 5 + (weights,) * 2,
        out_specs=(rows, rows, P(("replica", "expert"), "fsdp", None)),
        check_vma=False,
    )
```

```python
import jax
import jax.numpy as jnp
from jax import lax
from jax.experimental import pallas as pl
from jax.experimental.pallas import tpu as pltpu
from jax.sharding import PartitionSpec as P

EXPERTS = 128
CORES = 2
BACK_COST = 12000000000
VMEM = 40 * 1024 * 1024
F32 = jnp.float32
BF16 = jnp.bfloat16


def product(left, right, left_dim, right_dim, **kw):
    return lax.dot_general(
        left, right, (((left_dim,), (right_dim,)), ((), ())), preferred_element_type=F32, **kw
    )


def call(body, out_shape, args, far=0, cost=0, after=(), token=False, **kw):
    out_shape = [*out_shape] + [shape((8, 128), F32)] * token
    specs = [pl.BlockSpec(memory_space=pltpu.VMEM)] * (len(args) - far)
    specs += [pl.BlockSpec(memory_space=pltpu.HBM)] * far
    specs += [pl.BlockSpec(memory_space=pl.ANY)] * len(after)
    kw.setdefault("out_specs", [pl.BlockSpec(memory_space=pltpu.VMEM)] * len(out_shape))
    args = [
        pltpu.with_memory_space_constraint(arg, pltpu.HBM) if i >= len(args) - far else arg
        for i, arg in enumerate(args)
    ]
    count, first, last = len(args), len(args) + len(after), len(args) + len(after) + len(out_shape)

    def kernel(*refs):
        if token:
            refs[last - 1][...] = jnp.zeros(refs[last - 1].shape, F32)
        body(*refs[:count], *refs[first : last - token], *refs[last:])

    return pl.pallas_call(
        kernel,
        out_shape=out_shape,
        in_specs=specs,
        compiler_params=pltpu.CompilerParams(vmem_limit_bytes=VMEM),
        cost_estimate=pl.CostEstimate(flops=cost, bytes_accessed=0, transcendentals=0),
        **kw,
    )(*args, *after)


def shape(dims, kind=BF16):
    return jax.ShapeDtypeStruct(dims, kind)


def columns(k, part):
    return pl.ds(pl.multiple_of((lax.axis_index("fsdp") ^ k) * part, part), part)


def slot_kernel(spread, *refs):
    sources, rows_out, grads_out, refs = refs[:5], refs[5 : 5 + spread], refs[5 + spread : 5 + 2 * spread], refs[5 + 2 * spread :]
    turned_out, gate_out, ids, gates, order, tok, cot, sems = refs
    parts = spread * CORES
    copies = [
        pltpu.make_async_copy(source, target, sems.at[i])
        for i, (source, target) in enumerate(zip(sources, (ids, gates, order, tok, cot)))
    ]
    for copy in copies:
        copy.start()
    for copy in copies[:3]:
        copy.wait()
    choices, count = ids.shape
    slots = gate_out.shape[0]
    groups = lax.axis_size("expert")
    capacity = slots // groups
    part = tok.shape[1] // parts
    slot = lax.broadcasted_iota(jnp.int32, (slots, count), 0)
    wanted = ((slot // capacity) ^ lax.axis_index("expert")) * (EXPERTS // groups)
    routed = jnp.zeros((slots, count), F32)
    gate = jnp.zeros((slots, count), F32)
    for k in range(choices):
        hit = ids[k : k + 1, :] == wanted
        routed = jnp.where(hit, 1.0, routed)
        gate = jnp.where(hit, gates[k : k + 1, :], gate)
    row = lax.broadcasted_iota(jnp.int32, (count, count), 0)
    col = lax.broadcasted_iota(jnp.int32, (count, count), 1)
    served = jnp.where(order[...] == row, 1.0, 0.0).astype(BF16)
    earlier = jnp.where(row < col, 1.0, 0.0).astype(BF16)
    by_rank = product(routed.astype(BF16), served, 1, 0)
    before = product(by_rank.astype(BF16), earlier, 1, 0)
    taken = jnp.where(before.astype(jnp.int32) == slot % capacity, by_rank, 0.0).astype(BF16)
    pick = product(taken, served, 1, 1)
    turned_out[...] = product(served, taken, 1, 1).astype(BF16)
    slot_gate = jnp.sum(pick * gate, axis=1, keepdims=True)
    gate_out[...] = jnp.broadcast_to(slot_gate, gate_out.shape)
    pick = pick.astype(BF16)
    for copy, source, scale, outs in (
        (copies[3], tok, None, rows_out),
        (copies[4], cot, slot_gate, grads_out),
    ):
        copy.wait()
        for k in reversed(range(parts)):
            value = product(pick, source[:, columns(k, part)], 1, 0)
            value = value if scale is None else scale * value
            to = pl.ds((k % CORES) * part, part)
            outs[k // CORES][:, to] = value.astype(BF16)


def join_kernel(groups, spread, capacity, *refs):
    by_x, chunks = refs[:spread], refs[spread:]
    half = by_x[0].shape[1]
    for ke in range(groups):
        for kx in range(spread):
            chunks[ke][:, kx * half : (kx + 1) * half] = by_x[kx][
                ke * capacity : (ke + 1) * capacity
            ]


def far_kernel(groups, spread, capacity, *refs):
    by_e, by_x = refs[:groups], refs[groups:]
    for ke in range(groups):
        for kx in range(1, spread):
            by_x[kx - 1][ke * capacity : (ke + 1) * capacity] = by_e[ke][
                kx * capacity : (kx + 1) * capacity
            ]


def partial(groups, spread, refs, outs):
    chunks, (own, sib) = refs[:groups], refs[groups:]
    part = own.shape[0]
    half = CORES * part
    rows = jnp.concatenate(
        [c[:, kx * half : (kx + 1) * half] for kx in range(spread) for c in chunks], axis=0
    )
    total = product(rows[:, :part], own[...], 1, 0) + product(rows[:, part:], sib[...], 1, 0)
    slots = rows.shape[0] // spread
    for kx in range(spread):
        outs[kx][...] = total[kx * slots : (kx + 1) * slots].astype(outs[kx].dtype)
    return rows


def pre_kernel(groups, spread, *refs):
    partial(groups, spread, refs[: groups + 2], refs[groups + 2 :])


def back_kernel(groups, spread, *refs):
    own, sib, *outs = refs[groups + 2 :]
    rows = partial(groups, spread, refs[: groups + 2], outs)
    part = own.shape[1]
    own[...] = rows[:, :part]
    sib[...] = rows[:, part:]


def summed(refs):
    total = refs[0][...]
    for ref in refs[1:]:
        total += ref[...].astype(F32)
    return total


def hidden_kernel(*refs):
    pre, out = summed(refs[:-1]), refs[-1]
    feed = out.shape[1]
    gate_act, up_act = pre[:, :feed], pre[:, feed:]
    out[...] = (gate_act * (1.0 / (1.0 + jnp.exp(-gate_act))) * up_act).astype(BF16)


def d_pre_kernel(*refs):
    spread = len(refs) // 2
    pre, back, out = summed(refs[:spread]), summed(refs[spread:-1]), refs[-1]
    feed = back.shape[1]
    gate_act, up_act = pre[:, :feed], pre[:, feed:]
    sig = 1.0 / (1.0 + jnp.exp(-gate_act))
    out[:, :feed] = (back * up_act * (sig * (1.0 + gate_act * (1.0 - sig)))).astype(BF16)
    out[:, feed:] = (back * (gate_act * sig)).astype(BF16)


def width_product(left, weights, store):
    rows = jnp.concatenate([r[...] for r in left], axis=0)
    for kc, weight in enumerate(weights):
        store(kc, product(rows, weight[...], 1, 1).astype(BF16))


def expert_out_kernel(groups, spread, capacity, *refs):
    chunks = refs[-groups:]
    part = refs[spread].shape[0]

    def store(kc, value):
        for ke in range(groups):
            for kx in range(spread):
                at = (kx * groups + ke) * capacity
                chunks[ke][kx * capacity : (kx + 1) * capacity, kc * part : (kc + 1) * part] = value[
                    at : at + capacity
                ]

    width_product(refs[:spread], refs[spread : spread + CORES], store)


def d_rows_kernel(spread, *refs):
    outs = refs[-spread:]
    part = refs[spread].shape[0]
    slots = outs[0].shape[0]

    def store(kc, value):
        for kx in range(spread):
            outs[kx][:, kc * part : (kc + 1) * part] = value[kx * slots : (kx + 1) * slots]

    width_product(refs[:spread], refs[spread : spread + CORES], store)


def weight_kernel(spread, own, sib, *refs):
    hidden, sib_hidden, out = refs[:spread], refs[spread:-1], refs[-1]
    left = jnp.concatenate([own[...], sib[...]], axis=0)
    right = jnp.concatenate([r[...] for r in (*hidden, *sib_hidden)], axis=0)
    out[...] = product(left, right, 0, 0)


def scatter(turned, groups_of_rows, out, held, sems):
    part = held.shape[2]
    copies = []
    for k, rows in enumerate(groups_of_rows):
        held[k] = product(turned, rows, 1, 0).astype(BF16)
        copies.append(pltpu.make_async_copy(held.at[k], out.at[:, columns(k, part)], sems.at[k]))
        copies[-1].start()
    for copy in copies:
        copy.wait()


def combine_kernel(groups, parts, capacity, turned, gate, *refs):
    chunks, far, (out, held, sems) = refs[:groups], refs[groups:-3], refs[-3:]
    part = held.shape[2]

    def weighted(k):
        cols = slice((k % CORES) * part, (k % CORES + 1) * part)
        if k < CORES:
            rows = jnp.concatenate([c[:capacity, cols] for c in chunks], axis=0)
        else:
            rows = far[k // CORES - 1][:, cols]
        rows = rows.astype(F32) * gate[:, :1]
        high = rows.astype(BF16)
        return jnp.concatenate([high, (rows - high.astype(F32)).astype(BF16)], axis=0)

    twice = jnp.concatenate([turned[...], turned[...]], axis=1)
    scatter(twice, map(weighted, range(parts)), out, held, sems)


def d_tokens_kernel(groups, parts, turned, *refs):
    chunks, (out, held, sems) = refs[:groups], refs[groups:]
    part = held.shape[2]
    rows = (
        jnp.concatenate([c[:, k * part : (k + 1) * part] for c in chunks], axis=0)
        for k in range(parts)
    )
    scatter(turned[...], rows, out, held, sems)


def per_device(tokens, cotangent, route_ids, route_gates, served_order, w_in, w_out):
    groups = lax.axis_size("expert")
    parts = lax.axis_size("fsdp")
    spread = parts // CORES
    count, width = tokens.shape
    capacity = count * route_ids.shape[1] // EXPERTS
    feed = w_out.shape[2]
    slots = groups * capacity
    half = width // spread
    part = width // parts

    def bound(kernel, *sizes):
        return lambda *refs: kernel(*sizes, *refs)

    def to_core(value):
        return lax.ppermute(value, "fsdp", [(i, i ^ 1) for i in range(parts)])

    def to_x(values):
        return [
            lax.ppermute(value, "fsdp", [(i, i ^ ((k + 1) * CORES)) for i in range(parts)])
            for k, value in enumerate(values)
        ]

    def to_expert(chunks):
        return [
            lax.ppermute(value, "expert", [(i, i ^ ke) for i in range(groups)]) if ke else value
            for ke, value in enumerate(chunks)
        ]

    chunk = [shape((capacity, width))] * groups
    by_x = [shape((slots, half))] * spread
    in_own, out_own = w_in[0], w_out[0]
    in_sib, out_sib = to_core(in_own), to_core(out_own)
    outs = call(
        bound(slot_kernel, spread),
        by_x * 2 + [shape((count, slots)), shape((slots, 128), F32)],
        (route_ids.T, route_gates.T, served_order, tokens, cotangent),
        far=5,
        scratch_shapes=[
            pltpu.VMEM(route_ids.shape[::-1], jnp.int32),
            pltpu.VMEM(route_gates.shape[::-1], F32),
            pltpu.VMEM(served_order.shape, jnp.int32),
            pltpu.VMEM(tokens.shape, BF16),
            pltpu.VMEM(cotangent.shape, BF16),
            pltpu.SemaphoreType.DMA((5,)),
        ],
    )
    turned, gate = outs[-2:]
    rows = [outs[0], *to_x(outs[1:spread])]
    grads = [outs[spread], *to_x(outs[spread + 1 : 2 * spread])]
    rows, in_sib, out_sib = lax.optimization_barrier((rows, in_sib, out_sib))
    join = bound(join_kernel, groups, spread, capacity)
    rows = to_expert(call(join, chunk, rows))
    grads = to_expert(call(join, chunk, grads))
    pre, *pre_far = call(
        bound(pre_kernel, groups, spread),
        [shape((slots, 2 * feed), F32)] + [shape((slots, 2 * feed))] * (spread - 1),
        (*rows, in_own, in_sib),
    )
    pre = (pre, *to_x(pre_far))
    (hidden,) = call(hidden_kernel, [shape((slots, feed))], pre)
    hidden = (hidden, *to_x([hidden] * (spread - 1)))
    own_grads, sib_grads, back, *back_far = call(
        bound(back_kernel, groups, spread),
        [shape((spread * slots, part))] * 2
        + [shape((slots, feed), F32)]
        + [shape((slots, feed))] * (spread - 1),
        (*grads, out_own, out_sib),
        cost=BACK_COST,
    )
    back = (back, *to_x(back_far))
    expert_out = to_expert(
        call(
            bound(expert_out_kernel, groups, spread, capacity),
            [shape((spread * capacity, half))] * groups,
            (*hidden, out_own, out_sib),
        )
    )
    (d_pre,) = call(
        d_pre_kernel, [shape((slots, 2 * feed))], (*pre, *back), after=hidden[1:]
    )
    d_pre = (d_pre, *to_x([d_pre] * (spread - 1)))
    near, *far = call(
        bound(d_rows_kernel, spread), by_x, (*d_pre, in_own, in_sib), after=expert_out[1:2]
    )
    d_rows = to_expert(call(join, chunk, (near, *to_x(far))))
    far = to_x(
        call(bound(far_kernel, groups, spread, capacity), by_x[1:], expert_out)
    )
    d_w_out, token = call(
        bound(weight_kernel, spread),
        [shape((part, feed), F32)],
        (own_grads, to_core(sib_grads), *hidden, *[to_core(value) for value in hidden]),
        token=True,
    )

    def scattered(kernel, operands, **kw):
        return call(
            kernel,
            [shape((count, width))],
            operands,
            out_specs=[pl.BlockSpec(memory_space=pltpu.HBM)]
            + [pl.BlockSpec(memory_space=pltpu.VMEM)] * kw.get("token", False),
            scratch_shapes=[
                pltpu.VMEM((parts, count, part), BF16),
                pltpu.SemaphoreType.DMA((parts,)),
            ],
            **kw,
        )

    combined, token = scattered(
        bound(combine_kernel, groups, parts, capacity),
        (turned, gate, *expert_out, *far),
        after=(token,),
        token=True,
    )
    (d_tokens,) = scattered(
        bound(d_tokens_kernel, groups, parts), (turned, *d_rows), after=(token,)
    )
    return combined, d_tokens, d_w_out[None]


def solution(mesh):
    rows = P(("replica", "expert", "fsdp"), None)
    weights = P("expert", "fsdp", None)
    return jax.shard_map(
        per_device,
        mesh=mesh,
        in_specs=(rows,) * 5 + (weights,) * 2,
        out_specs=(rows, rows, P(("replica", "expert"), "fsdp", None)),
        check_vma=False,
    )
```

```python
import jax
import jax.numpy as jnp
from jax import lax
from jax.experimental import pallas as pl
from jax.experimental.pallas import tpu as pltpu
from jax.sharding import PartitionSpec as P

EXPERTS = 128
CORES = 2
PRE_COST = 4500000000
BACK_COST = 3000000000
VMEM = 40 * 1024 * 1024
F32 = jnp.float32
BF16 = jnp.bfloat16


def product(left, right, left_dim, right_dim, **kw):
    return lax.dot_general(
        left, right, (((left_dim,), (right_dim,)), ((), ())), preferred_element_type=F32, **kw
    )


def call(body, out_shape, args, far=0, cost=0, after=(), token=False, **kw):
    out_shape = [*out_shape] + [shape((8, 128), F32)] * token
    specs = [pl.BlockSpec(memory_space=pltpu.VMEM)] * (len(args) - far)
    specs += [pl.BlockSpec(memory_space=pltpu.HBM)] * far
    specs += [pl.BlockSpec(memory_space=pl.ANY)] * len(after)
    kw.setdefault("out_specs", [pl.BlockSpec(memory_space=pltpu.VMEM)] * len(out_shape))
    args = [
        pltpu.with_memory_space_constraint(arg, pltpu.HBM) if i >= len(args) - far else arg
        for i, arg in enumerate(args)
    ]
    count, first, last = len(args), len(args) + len(after), len(args) + len(after) + len(out_shape)

    def kernel(*refs):
        if token:
            refs[last - 1][...] = jnp.zeros(refs[last - 1].shape, F32)
        body(*refs[:count], *refs[first : last - token], *refs[last:])

    return pl.pallas_call(
        kernel,
        out_shape=out_shape,
        in_specs=specs,
        compiler_params=pltpu.CompilerParams(vmem_limit_bytes=VMEM),
        cost_estimate=pl.CostEstimate(flops=cost, bytes_accessed=0, transcendentals=0),
        **kw,
    )(*args, *after)


def shape(dims, kind=BF16):
    return jax.ShapeDtypeStruct(dims, kind)


def columns(k, part):
    return pl.ds(pl.multiple_of((lax.axis_index("fsdp") ^ k) * part, part), part)


def slot_kernel(groups, spread, *refs):
    sources, chunks, refs = refs[:5], refs[5 : 5 + groups], refs[5 + groups :]
    rows_far, grads_out, refs = refs[: spread - 1], refs[spread - 1 : 2 * spread - 1], refs[2 * spread - 1 :]
    turned_out, gate_out, ids, gates, order, tok, cot, sems = refs
    parts = spread * CORES
    copies = [
        pltpu.make_async_copy(source, target, sems.at[i])
        for i, (source, target) in enumerate(zip(sources, (ids, gates, order, tok, cot)))
    ]
    for copy in copies:
        copy.start()
    for copy in copies[:3]:
        copy.wait()
    choices, count = ids.shape
    slots = gate_out.shape[0]
    capacity = slots // groups
    part = tok.shape[1] // parts
    slot = lax.broadcasted_iota(jnp.int32, (slots, count), 0)
    wanted = ((slot // capacity) ^ lax.axis_index("expert")) * (EXPERTS // groups)
    routed = jnp.zeros((slots, count), F32)
    gate = jnp.zeros((slots, count), F32)
    for k in range(choices):
        hit = ids[k : k + 1, :] == wanted
        routed = jnp.where(hit, 1.0, routed)
        gate = jnp.where(hit, gates[k : k + 1, :], gate)
    row = lax.broadcasted_iota(jnp.int32, (count, count), 0)
    col = lax.broadcasted_iota(jnp.int32, (count, count), 1)
    served = jnp.where(order[...] == row, 1.0, 0.0).astype(BF16)
    earlier = jnp.where(row < col, 1.0, 0.0).astype(BF16)
    by_rank = product(routed.astype(BF16), served, 1, 0)
    before = product(by_rank.astype(BF16), earlier, 1, 0)
    taken = jnp.where(before.astype(jnp.int32) == slot % capacity, by_rank, 0.0).astype(BF16)
    pick = product(taken, served, 1, 1)
    turned_out[...] = product(served, taken, 1, 1).astype(BF16)
    slot_gate = jnp.sum(pick * gate, axis=1, keepdims=True)
    gate_out[...] = jnp.broadcast_to(slot_gate, gate_out.shape)
    pick = pick.astype(BF16)
    copies[3].wait()
    for k in reversed(range(parts)):
        value = product(pick, tok[:, columns(k, part)], 1, 0).astype(BF16)
        to = pl.ds((k % CORES) * part, part)
        if k >= CORES:
            rows_far[k // CORES - 1][:, to] = value
        else:
            for ke in range(groups):
                chunks[ke][:, to] = value[ke * capacity : (ke + 1) * capacity]
    copies[4].wait()
    for k in reversed(range(parts)):
        value = slot_gate * product(pick, cot[:, columns(k, part)], 1, 0)
        grads_out[k // CORES][:, pl.ds((k % CORES) * part, part)] = value.astype(BF16)


def split_kernel(groups, capacity, *refs):
    by_x, by_e = refs[:-groups], refs[-groups:]
    for ke in range(groups):
        for i, source in enumerate(by_x):
            by_e[ke][i * capacity : (i + 1) * capacity] = source[
                ke * capacity : (ke + 1) * capacity
            ]


def join_kernel(groups, spread, capacity, *refs):
    by_x, chunks = refs[:spread], refs[spread:]
    half = by_x[0].shape[1]
    for ke in range(groups):
        for kx in range(spread):
            chunks[ke][:, kx * half : (kx + 1) * half] = by_x[kx][
                ke * capacity : (ke + 1) * capacity
            ]


def far_kernel(groups, spread, capacity, *refs):
    by_e, by_x = refs[:groups], refs[groups:]
    for ke in range(groups):
        for kx in range(1, spread):
            by_x[kx - 1][ke * capacity : (ke + 1) * capacity] = by_e[ke][
                kx * capacity : (kx + 1) * capacity
            ]


def partial(rows, own, sib, outs):
    part = own.shape[0]
    total = product(rows[:, :part], own[...], 1, 0) + product(rows[:, part:], sib[...], 1, 0)
    slots = rows.shape[0] // len(outs)
    for kx, out in enumerate(outs):
        out[...] = total[kx * slots : (kx + 1) * slots].astype(out.dtype)


def own_and_far(groups, spread, capacity, refs):
    own, far = refs[:groups], refs[groups:]
    yield jnp.concatenate([c[...] for c in own], axis=0)
    for i in range(spread - 1):
        at = slice(i * capacity, (i + 1) * capacity)
        yield jnp.concatenate([c[at] for c in far], axis=0)


def pre_kernel(groups, spread, capacity, *refs):
    rows = jnp.concatenate(
        list(own_and_far(groups, spread, capacity, refs[: 2 * groups])), axis=0
    )
    own, sib, *outs = refs[2 * groups :]
    partial(rows, own, sib, outs)


def back_kernel(groups, spread, *refs):
    chunks, (out_own, out_sib, own, sib, *outs) = refs[:groups], refs[groups:]
    half = CORES * out_own.shape[0]
    rows = jnp.concatenate(
        [c[:, kx * half : (kx + 1) * half] for kx in range(spread) for c in chunks], axis=0
    )
    partial(rows, out_own, out_sib, outs)
    part = own.shape[1]
    own[...] = rows[:, :part]
    sib[...] = rows[:, part:]


def summed(refs):
    total = refs[0][...]
    for ref in refs[1:]:
        total += ref[...].astype(F32)
    return total


def hidden_kernel(*refs):
    pre, out = summed(refs[:-1]), refs[-1]
    feed = out.shape[1]
    gate_act, up_act = pre[:, :feed], pre[:, feed:]
    out[...] = (gate_act * (1.0 / (1.0 + jnp.exp(-gate_act))) * up_act).astype(BF16)


def d_pre_kernel(*refs):
    spread = len(refs) // 2
    pre, back, out = summed(refs[:spread]), summed(refs[spread:-1]), refs[-1]
    feed = back.shape[1]
    gate_act, up_act = pre[:, :feed], pre[:, feed:]
    sig = 1.0 / (1.0 + jnp.exp(-gate_act))
    out[:, :feed] = (back * up_act * (sig * (1.0 + gate_act * (1.0 - sig)))).astype(BF16)
    out[:, feed:] = (back * (gate_act * sig)).astype(BF16)


def width_product(left, weights, store):
    rows = jnp.concatenate([r[...] for r in left], axis=0)
    for kc, weight in enumerate(weights):
        store(kc, product(rows, weight[...], 1, 1).astype(BF16))


def expert_out_kernel(groups, spread, capacity, *refs):
    chunks = refs[-groups:]
    part = refs[spread].shape[0]

    def store(kc, value):
        for ke in range(groups):
            for kx in range(spread):
                at = (kx * groups + ke) * capacity
                chunks[ke][kx * capacity : (kx + 1) * capacity, kc * part : (kc + 1) * part] = value[
                    at : at + capacity
                ]

    width_product(refs[:spread], refs[spread : spread + CORES], store)


def d_rows_kernel(groups, spread, capacity, *refs):
    left, weights, outs = refs[:spread], refs[spread : spread + CORES], refs[spread + CORES :]
    chunks, far = outs[:groups], outs[groups:]
    part = weights[0].shape[0]
    slots = groups * capacity

    def store(kc, value):
        to = pl.ds(kc * part, part)
        for kx in range(1, spread):
            far[kx - 1][:, to] = value[kx * slots : (kx + 1) * slots]
        for ke in range(groups):
            chunks[ke][:, to] = value[ke * capacity : (ke + 1) * capacity]

    width_product(left, weights, store)


def weight_kernel(spread, own, sib, *refs):
    hidden, sib_hidden, out = refs[:spread], refs[spread:-1], refs[-1]
    left = jnp.concatenate([own[...], sib[...]], axis=0)
    right = jnp.concatenate([r[...] for r in (*hidden, *sib_hidden)], axis=0)
    out[...] = product(left, right, 0, 0)


def scatter(turned, groups_of_rows, out, held, sems):
    part = held.shape[2]
    copies = []
    for k, rows in enumerate(groups_of_rows):
        held[k] = product(turned, rows, 1, 0).astype(BF16)
        copies.append(pltpu.make_async_copy(held.at[k], out.at[:, columns(k, part)], sems.at[k]))
        copies[-1].start()
    for copy in copies:
        copy.wait()


def combine_kernel(groups, parts, capacity, turned, gate, *refs):
    chunks, far, (out, held, sems) = refs[:groups], refs[groups:-3], refs[-3:]
    part = held.shape[2]

    def weighted(k):
        cols = slice((k % CORES) * part, (k % CORES + 1) * part)
        if k < CORES:
            rows = jnp.concatenate([c[:capacity, cols] for c in chunks], axis=0)
        else:
            rows = far[k // CORES - 1][:, cols]
        rows = rows.astype(F32) * gate[:, :1]
        high = rows.astype(BF16)
        return jnp.concatenate([high, (rows - high.astype(F32)).astype(BF16)], axis=0)

    twice = jnp.concatenate([turned[...], turned[...]], axis=1)
    scatter(twice, map(weighted, range(parts)), out, held, sems)


def d_tokens_kernel(groups, spread, capacity, turned, *refs):
    chunks, (out, held, sems) = refs[: 2 * groups], refs[2 * groups :]
    part = held.shape[2]
    rows = own_and_far(groups, spread, capacity, chunks)
    rows = (r[:, kc * part : (kc + 1) * part] for r in rows for kc in range(CORES))
    scatter(turned[...], rows, out, held, sems)


def per_device(tokens, cotangent, route_ids, route_gates, served_order, w_in, w_out):
    groups = lax.axis_size("expert")
    parts = lax.axis_size("fsdp")
    spread = parts // CORES
    count, width = tokens.shape
    capacity = count * route_ids.shape[1] // EXPERTS
    feed = w_out.shape[2]
    slots = groups * capacity
    half = width // spread
    part = width // parts

    def bound(kernel, *sizes):
        return lambda *refs: kernel(*sizes, *refs)

    def to_core(value):
        return lax.ppermute(value, "fsdp", [(i, i ^ 1) for i in range(parts)])

    def to_x(values):
        return [
            lax.ppermute(value, "fsdp", [(i, i ^ ((k + 1) * CORES)) for i in range(parts)])
            for k, value in enumerate(values)
        ]

    def to_expert(chunks):
        return [
            lax.ppermute(value, "expert", [(i, i ^ ke) for i in range(groups)]) if ke else value
            for ke, value in enumerate(chunks)
        ]

    chunk = [shape((capacity, width))] * groups
    by_x = [shape((slots, half))] * spread
    own_chunk = [shape((capacity, half))] * groups
    far_chunk = [shape(((spread - 1) * capacity, half))] * groups
    in_own, out_own = w_in[0], w_out[0]
    in_sib, out_sib = to_core(in_own), to_core(out_own)
    outs = call(
        bound(slot_kernel, groups, spread),
        own_chunk + by_x[1:] + by_x + [shape((count, slots)), shape((slots, 128), F32)],
        (route_ids.T, route_gates.T, served_order, tokens, cotangent),
        far=5,
        scratch_shapes=[
            pltpu.VMEM(route_ids.shape[::-1], jnp.int32),
            pltpu.VMEM(route_gates.shape[::-1], F32),
            pltpu.VMEM(served_order.shape, jnp.int32),
            pltpu.VMEM(tokens.shape, BF16),
            pltpu.VMEM(cotangent.shape, BF16),
            pltpu.SemaphoreType.DMA((5,)),
        ],
    )
    turned, gate = outs[-2:]
    own, (*far, near), grads_far = (
        outs[:groups],
        outs[groups : groups + spread],
        outs[groups + spread : -2],
    )
    far = to_x(far)
    grads = [near, *to_x(grads_far)]
    *own, in_sib, out_sib = lax.optimization_barrier((*own, in_sib, out_sib))
    split = bound(split_kernel, groups, capacity)
    own = to_expert(own)
    far = to_expert(call(split, far_chunk, far, after=own[1:]))
    join = bound(join_kernel, groups, spread, capacity)
    grads = to_expert(call(join, chunk, grads))
    pre, *pre_far = call(
        bound(pre_kernel, groups, spread, capacity),
        [shape((slots, 2 * feed), F32)] + [shape((slots, 2 * feed))] * (spread - 1),
        (*own, *far, in_own, in_sib),
        cost=PRE_COST,
    )
    pre = (pre, *to_x(pre_far))
    (hidden,) = call(hidden_kernel, [shape((slots, feed))], pre)
    hidden = (hidden, *to_x([hidden] * (spread - 1)))
    own_grads, sib_grads, back, *back_far = call(
        bound(back_kernel, groups, spread),
        [shape((spread * slots, part))] * 2
        + [shape((slots, feed), F32)]
        + [shape((slots, feed))] * (spread - 1),
        (*grads, out_own, out_sib),
        cost=BACK_COST,
    )
    back = (back, *to_x(back_far))
    expert_out = to_expert(
        call(
            bound(expert_out_kernel, groups, spread, capacity),
            [shape((spread * capacity, half))] * groups,
            (*hidden, out_own, out_sib),
        )
    )
    (d_pre,) = call(
        d_pre_kernel, [shape((slots, 2 * feed))], (*pre, *back), after=hidden[1:]
    )
    d_pre = (d_pre, *to_x([d_pre] * (spread - 1)))
    outs = call(
        bound(d_rows_kernel, groups, spread, capacity),
        own_chunk + by_x[1:],
        (*d_pre, in_own, in_sib),
        after=expert_out[1:2],
    )
    own, d_far = to_expert(outs[:groups]), to_x(outs[groups:])
    d_rows = (*own, *to_expert(call(split, far_chunk, d_far, after=own[1:])))
    far = to_x(
        call(bound(far_kernel, groups, spread, capacity), by_x[1:], expert_out)
    )
    d_w_out, token = call(
        bound(weight_kernel, spread),
        [shape((part, feed), F32)],
        (own_grads, to_core(sib_grads), *hidden, *[to_core(value) for value in hidden]),
        token=True,
    )

    def scattered(kernel, operands, **kw):
        return call(
            kernel,
            [shape((count, width))],
            operands,
            out_specs=[pl.BlockSpec(memory_space=pltpu.HBM)]
            + [pl.BlockSpec(memory_space=pltpu.VMEM)] * kw.get("token", False),
            scratch_shapes=[
                pltpu.VMEM((parts, count, part), BF16),
                pltpu.SemaphoreType.DMA((parts,)),
            ],
            **kw,
        )

    combined, token = scattered(
        bound(combine_kernel, groups, parts, capacity),
        (turned, gate, *expert_out, *far),
        after=(token,),
        token=True,
    )
    (d_tokens,) = scattered(
        bound(d_tokens_kernel, groups, spread, capacity), (turned, *d_rows), after=(token,)
    )
    return combined, d_tokens, d_w_out[None]


def solution(mesh):
    rows = P(("replica", "expert", "fsdp"), None)
    weights = P("expert", "fsdp", None)
    return jax.shard_map(
        per_device,
        mesh=mesh,
        in_specs=(rows,) * 5 + (weights,) * 2,
        out_specs=(rows, rows, P(("replica", "expert"), "fsdp", None)),
        check_vma=False,
    )
```

```python
import jax
import jax.numpy as jnp
from jax import lax
from jax.experimental import pallas as pl
from jax.experimental.pallas import tpu as pltpu
from jax.sharding import PartitionSpec as P

EXPERTS = 128
CORES = 2
BACK_COST = 12000000000
VMEM = 40 * 1024 * 1024
F32 = jnp.float32
BF16 = jnp.bfloat16


def product(left, right, left_dim, right_dim, **kw):
    return lax.dot_general(
        left, right, (((left_dim,), (right_dim,)), ((), ())), preferred_element_type=F32, **kw
    )


def call(body, out_shape, args, far=0, cost=0, after=(), token=False, **kw):
    out_shape = [*out_shape] + [shape((8, 128), F32)] * token
    specs = [pl.BlockSpec(memory_space=pltpu.VMEM)] * (len(args) - far)
    specs += [pl.BlockSpec(memory_space=pltpu.HBM)] * far
    specs += [pl.BlockSpec(memory_space=pl.ANY)] * len(after)
    kw.setdefault("out_specs", [pl.BlockSpec(memory_space=pltpu.VMEM)] * len(out_shape))
    args = [
        pltpu.with_memory_space_constraint(arg, pltpu.HBM) if i >= len(args) - far else arg
        for i, arg in enumerate(args)
    ]
    count, first, last = len(args), len(args) + len(after), len(args) + len(after) + len(out_shape)

    def kernel(*refs):
        if token:
            refs[last - 1][...] = jnp.zeros(refs[last - 1].shape, F32)
        body(*refs[:count], *refs[first : last - token], *refs[last:])

    return pl.pallas_call(
        kernel,
        out_shape=out_shape,
        in_specs=specs,
        compiler_params=pltpu.CompilerParams(vmem_limit_bytes=VMEM),
        cost_estimate=pl.CostEstimate(flops=cost, bytes_accessed=0, transcendentals=0),
        **kw,
    )(*args, *after)


def shape(dims, kind=BF16):
    return jax.ShapeDtypeStruct(dims, kind)


def columns(k, part):
    return pl.ds(pl.multiple_of((lax.axis_index("fsdp") ^ k) * part, part), part)


def slot_kernel(spread, *refs):
    sources, rows_out, grads_out, refs = refs[:5], refs[5 : 5 + spread], refs[5 + spread : 5 + 2 * spread], refs[5 + 2 * spread :]
    turned_out, gate_out, ids, gates, order, tok, cot, sems = refs
    parts = spread * CORES
    copies = [
        pltpu.make_async_copy(source, target, sems.at[i])
        for i, (source, target) in enumerate(zip(sources, (ids, gates, order, tok, cot)))
    ]
    for copy in copies:
        copy.start()
    for copy in copies[:3]:
        copy.wait()
    choices, count = ids.shape
    slots = gate_out.shape[0]
    groups = lax.axis_size("expert")
    capacity = slots // groups
    part = tok.shape[1] // parts
    slot = lax.broadcasted_iota(jnp.int32, (slots, count), 0)
    wanted = ((slot // capacity) ^ lax.axis_index("expert")) * (EXPERTS // groups)
    routed = jnp.zeros((slots, count), F32)
    gate = jnp.zeros((slots, count), F32)
    for k in range(choices):
        hit = ids[k : k + 1, :] == wanted
        routed = jnp.where(hit, 1.0, routed)
        gate = jnp.where(hit, gates[k : k + 1, :], gate)
    row = lax.broadcasted_iota(jnp.int32, (count, count), 0)
    col = lax.broadcasted_iota(jnp.int32, (count, count), 1)
    served = jnp.where(order[...] == row, 1.0, 0.0).astype(BF16)
    earlier = jnp.where(row < col, 1.0, 0.0).astype(BF16)
    by_rank = product(routed.astype(BF16), served, 1, 0)
    before = product(by_rank.astype(BF16), earlier, 1, 0)
    taken = jnp.where(before.astype(jnp.int32) == slot % capacity, by_rank, 0.0).astype(BF16)
    pick = product(taken, served, 1, 1)
    turned_out[...] = product(served, taken, 1, 1).astype(BF16)
    slot_gate = jnp.sum(pick * gate, axis=1, keepdims=True)
    gate_out[...] = jnp.broadcast_to(slot_gate, gate_out.shape)
    pick = pick.astype(BF16)
    for copy, source, scale, outs in (
        (copies[3], tok, None, rows_out),
        (copies[4], cot, slot_gate, grads_out),
    ):
        copy.wait()
        for k in reversed(range(parts)):
            value = product(pick, source[:, columns(k, part)], 1, 0)
            value = value if scale is None else scale * value
            to = pl.ds((k % CORES) * part, part)
            outs[k // CORES][:, to] = value.astype(BF16)


def flip(chunks):
    return [chunks[0], *chunks[:0:-1]]


def join_kernel(groups, spread, capacity, *refs):
    by_x, chunks = refs[:spread], refs[spread:]
    half = by_x[0].shape[1]
    for ke in range(groups):
        for kx in range(spread):
            chunks[ke][:, kx * half : (kx + 1) * half] = by_x[kx][
                ke * capacity : (ke + 1) * capacity
            ]


def far_kernel(groups, spread, capacity, *refs):
    by_e, by_x = flip(refs[:groups]), refs[groups:]
    for ke in range(groups):
        for kx in range(1, spread):
            by_x[kx - 1][ke * capacity : (ke + 1) * capacity] = by_e[ke][
                kx * capacity : (kx + 1) * capacity
            ]


def partial(groups, spread, refs, outs):
    chunks, (own, sib) = flip(refs[:groups]), refs[groups:]
    part = own.shape[0]
    half = CORES * part
    rows = jnp.concatenate(
        [c[:, kx * half : (kx + 1) * half] for kx in range(spread) for c in chunks], axis=0
    )
    total = product(rows[:, :part], own[...], 1, 0) + product(rows[:, part:], sib[...], 1, 0)
    slots = rows.shape[0] // spread
    for kx in range(spread):
        outs[kx][...] = total[kx * slots : (kx + 1) * slots].astype(outs[kx].dtype)
    return rows


def pre_kernel(groups, spread, *refs):
    partial(groups, spread, refs[: groups + 2], refs[groups + 2 :])


def back_kernel(groups, spread, *refs):
    own, sib, *outs = refs[groups + 2 :]
    rows = partial(groups, spread, refs[: groups + 2], outs)
    part = own.shape[1]
    own[...] = rows[:, :part]
    sib[...] = rows[:, part:]


def summed(refs):
    total = refs[0][...]
    for ref in refs[1:]:
        total += ref[...].astype(F32)
    return total


def hidden_kernel(*refs):
    pre, out = summed(refs[:-1]), refs[-1]
    feed = out.shape[1]
    gate_act, up_act = pre[:, :feed], pre[:, feed:]
    out[...] = (gate_act * (1.0 / (1.0 + jnp.exp(-gate_act))) * up_act).astype(BF16)


def d_pre_kernel(*refs):
    spread = len(refs) // 2
    pre, back, out = summed(refs[:spread]), summed(refs[spread:-1]), refs[-1]
    feed = back.shape[1]
    gate_act, up_act = pre[:, :feed], pre[:, feed:]
    sig = 1.0 / (1.0 + jnp.exp(-gate_act))
    out[:, :feed] = (back * up_act * (sig * (1.0 + gate_act * (1.0 - sig)))).astype(BF16)
    out[:, feed:] = (back * (gate_act * sig)).astype(BF16)


def width_product(left, weights, store):
    rows = jnp.concatenate([r[...] for r in left], axis=0)
    for kc, weight in enumerate(weights):
        store(kc, product(rows, weight[...], 1, 1).astype(BF16))


def expert_out_kernel(groups, spread, capacity, *refs):
    chunks = refs[-groups:]
    part = refs[spread].shape[0]

    def store(kc, value):
        for ke in range(groups):
            for kx in range(spread):
                at = (kx * groups + ke) * capacity
                chunks[ke][kx * capacity : (kx + 1) * capacity, kc * part : (kc + 1) * part] = value[
                    at : at + capacity
                ]

    width_product(refs[:spread], refs[spread : spread + CORES], store)


def d_rows_kernel(spread, *refs):
    outs = refs[-spread:]
    part = refs[spread].shape[0]
    slots = outs[0].shape[0]

    def store(kc, value):
        for kx in range(spread):
            outs[kx][:, kc * part : (kc + 1) * part] = value[kx * slots : (kx + 1) * slots]

    width_product(refs[:spread], refs[spread : spread + CORES], store)


def weight_kernel(spread, own, sib, *refs):
    hidden, sib_hidden, out = refs[:spread], refs[spread:-1], refs[-1]
    left = jnp.concatenate([own[...], sib[...]], axis=0)
    right = jnp.concatenate([r[...] for r in (*hidden, *sib_hidden)], axis=0)
    out[...] = product(left, right, 0, 0)


def scatter(turned, groups_of_rows, out, held, sems):
    part = held.shape[2]
    copies = []
    for k, rows in enumerate(groups_of_rows):
        held[k] = product(turned, rows, 1, 0).astype(BF16)
        copies.append(pltpu.make_async_copy(held.at[k], out.at[:, columns(k, part)], sems.at[k]))
        copies[-1].start()
    for copy in copies:
        copy.wait()


def combine_kernel(groups, parts, capacity, turned, gate, *refs):
    chunks, far, (out, held, sems) = flip(refs[:groups]), refs[groups:-3], refs[-3:]
    part = held.shape[2]

    def weighted(k):
        cols = slice((k % CORES) * part, (k % CORES + 1) * part)
        if k < CORES:
            rows = jnp.concatenate([c[:capacity, cols] for c in chunks], axis=0)
        else:
            rows = far[k // CORES - 1][:, cols]
        rows = rows.astype(F32) * gate[:, :1]
        high = rows.astype(BF16)
        return jnp.concatenate([high, (rows - high.astype(F32)).astype(BF16)], axis=0)

    twice = jnp.concatenate([turned[...], turned[...]], axis=1)
    scatter(twice, map(weighted, range(parts)), out, held, sems)


def d_tokens_kernel(groups, parts, turned, *refs):
    chunks, (out, held, sems) = flip(refs[:groups]), refs[groups:]
    part = held.shape[2]
    rows = (
        jnp.concatenate([c[:, k * part : (k + 1) * part] for c in chunks], axis=0)
        for k in range(parts)
    )
    scatter(turned[...], rows, out, held, sems)


def per_device(tokens, cotangent, route_ids, route_gates, served_order, w_in, w_out):
    groups = lax.axis_size("expert")
    parts = lax.axis_size("fsdp")
    spread = parts // CORES
    count, width = tokens.shape
    capacity = count * route_ids.shape[1] // EXPERTS
    feed = w_out.shape[2]
    slots = groups * capacity
    half = width // spread
    part = width // parts

    def bound(kernel, *sizes):
        return lambda *refs: kernel(*sizes, *refs)

    def to_core(value):
        return lax.ppermute(value, "fsdp", [(i, i ^ 1) for i in range(parts)])

    def to_x(values):
        return [
            lax.ppermute(value, "fsdp", [(i, i ^ ((k + 1) * CORES)) for i in range(parts)])
            for k, value in enumerate(values)
        ]

    def to_expert(chunks):
        return [
            lax.ppermute(value, "expert", [(i, i ^ ke) for i in range(groups)]) if ke else value
            for ke, value in enumerate(chunks)
        ]

    chunk = [shape((capacity, width))] * groups
    by_x = [shape((slots, half))] * spread
    in_own, out_own = w_in[0], w_out[0]
    in_sib, out_sib = to_core(in_own), to_core(out_own)
    outs = call(
        bound(slot_kernel, spread),
        by_x * 2 + [shape((count, slots)), shape((slots, 128), F32)],
        (route_ids.T, route_gates.T, served_order, tokens, cotangent),
        far=5,
        scratch_shapes=[
            pltpu.VMEM(route_ids.shape[::-1], jnp.int32),
            pltpu.VMEM(route_gates.shape[::-1], F32),
            pltpu.VMEM(served_order.shape, jnp.int32),
            pltpu.VMEM(tokens.shape, BF16),
            pltpu.VMEM(cotangent.shape, BF16),
            pltpu.SemaphoreType.DMA((5,)),
        ],
    )
    turned, gate = outs[-2:]
    rows = [outs[0], *to_x(outs[1:spread])]
    grads = [outs[spread], *to_x(outs[spread + 1 : 2 * spread])]
    rows, in_sib, out_sib = lax.optimization_barrier((rows, in_sib, out_sib))
    join = bound(join_kernel, groups, spread, capacity)
    rows = to_expert(call(join, chunk, rows))
    grads = to_expert(call(join, chunk, grads))
    pre, *pre_far = call(
        bound(pre_kernel, groups, spread),
        [shape((slots, 2 * feed), F32)] + [shape((slots, 2 * feed))] * (spread - 1),
        (*flip(rows), in_own, in_sib),
    )
    pre = (pre, *to_x(pre_far))
    (hidden,) = call(hidden_kernel, [shape((slots, feed))], pre)
    hidden = (hidden, *to_x([hidden] * (spread - 1)))
    own_grads, sib_grads, back, *back_far = call(
        bound(back_kernel, groups, spread),
        [shape((spread * slots, part))] * 2
        + [shape((slots, feed), F32)]
        + [shape((slots, feed))] * (spread - 1),
        (*flip(grads), out_own, out_sib),
        cost=BACK_COST,
    )
    back = (back, *to_x(back_far))
    expert_out = to_expert(
        call(
            bound(expert_out_kernel, groups, spread, capacity),
            [shape((spread * capacity, half))] * groups,
            (*hidden, out_own, out_sib),
        )
    )
    (d_pre,) = call(
        d_pre_kernel, [shape((slots, 2 * feed))], (*pre, *back), after=hidden[1:]
    )
    d_pre = (d_pre, *to_x([d_pre] * (spread - 1)))
    near, *far = call(
        bound(d_rows_kernel, spread), by_x, (*d_pre, in_own, in_sib), after=expert_out[1:2]
    )
    d_rows = to_expert(call(join, chunk, (near, *to_x(far))))
    far = to_x(
        call(bound(far_kernel, groups, spread, capacity), by_x[1:], flip(expert_out))
    )
    d_w_out, token = call(
        bound(weight_kernel, spread),
        [shape((part, feed), F32)],
        (own_grads, to_core(sib_grads), *hidden, *[to_core(value) for value in hidden]),
        token=True,
    )

    def scattered(kernel, operands, **kw):
        return call(
            kernel,
            [shape((count, width))],
            operands,
            out_specs=[pl.BlockSpec(memory_space=pltpu.HBM)]
            + [pl.BlockSpec(memory_space=pltpu.VMEM)] * kw.get("token", False),
            scratch_shapes=[
                pltpu.VMEM((parts, count, part), BF16),
                pltpu.SemaphoreType.DMA((parts,)),
            ],
            **kw,
        )

    combined, token = scattered(
        bound(combine_kernel, groups, parts, capacity),
        (turned, gate, *flip(expert_out), *far),
        after=(token,),
        token=True,
    )
    (d_tokens,) = scattered(
        bound(d_tokens_kernel, groups, parts), (turned, *flip(d_rows)), after=(token,)
    )
    return combined, d_tokens, d_w_out[None]


def solution(mesh):
    rows = P(("replica", "expert", "fsdp"), None)
    weights = P("expert", "fsdp", None)
    return jax.shard_map(
        per_device,
        mesh=mesh,
        in_specs=(rows,) * 5 + (weights,) * 2,
        out_specs=(rows, rows, P(("replica", "expert"), "fsdp", None)),
        check_vma=False,
    )
```

```python
import jax
import jax.numpy as jnp
from jax import lax
from jax.experimental import pallas as pl
from jax.experimental.pallas import tpu as pltpu
from jax.sharding import PartitionSpec as P

EXPERTS = 128
CORES = 2
OUT_COST = 2000000000
BACK_COST = 12000000000
VMEM = 40 * 1024 * 1024
F32 = jnp.float32
BF16 = jnp.bfloat16


def product(left, right, left_dim, right_dim, **kw):
    return lax.dot_general(
        left, right, (((left_dim,), (right_dim,)), ((), ())), preferred_element_type=F32, **kw
    )


def call(body, out_shape, args, far=0, cost=0, after=(), token=False, **kw):
    out_shape = [*out_shape] + [shape((8, 128), F32)] * token
    specs = [pl.BlockSpec(memory_space=pltpu.VMEM)] * (len(args) - far)
    specs += [pl.BlockSpec(memory_space=pltpu.HBM)] * far
    specs += [pl.BlockSpec(memory_space=pl.ANY)] * len(after)
    kw.setdefault("out_specs", [pl.BlockSpec(memory_space=pltpu.VMEM)] * len(out_shape))
    args = [
        pltpu.with_memory_space_constraint(arg, pltpu.HBM) if i >= len(args) - far else arg
        for i, arg in enumerate(args)
    ]
    count, first, last = len(args), len(args) + len(after), len(args) + len(after) + len(out_shape)

    def kernel(*refs):
        if token:
            refs[last - 1][...] = jnp.zeros(refs[last - 1].shape, F32)
        body(*refs[:count], *refs[first : last - token], *refs[last:])

    return pl.pallas_call(
        kernel,
        out_shape=out_shape,
        in_specs=specs,
        compiler_params=pltpu.CompilerParams(vmem_limit_bytes=VMEM),
        cost_estimate=pl.CostEstimate(flops=cost, bytes_accessed=0, transcendentals=0),
        **kw,
    )(*args, *after)


def shape(dims, kind=BF16):
    return jax.ShapeDtypeStruct(dims, kind)


def columns(k, part):
    return pl.ds(pl.multiple_of((lax.axis_index("fsdp") ^ k) * part, part), part)


def slot_kernel(spread, *refs):
    sources, rows_out, grads_out, refs = refs[:5], refs[5 : 5 + spread], refs[5 + spread : 5 + 2 * spread], refs[5 + 2 * spread :]
    turned_out, gate_out, ids, gates, order, tok, cot, sems = refs
    parts = spread * CORES
    copies = [
        pltpu.make_async_copy(source, target, sems.at[i])
        for i, (source, target) in enumerate(zip(sources, (ids, gates, order, tok, cot)))
    ]
    for copy in copies:
        copy.start()
    for copy in copies[:3]:
        copy.wait()
    choices, count = ids.shape
    slots = gate_out.shape[0]
    groups = lax.axis_size("expert")
    capacity = slots // groups
    part = tok.shape[1] // parts
    slot = lax.broadcasted_iota(jnp.int32, (slots, count), 0)
    wanted = ((slot // capacity) ^ lax.axis_index("expert")) * (EXPERTS // groups)
    routed = jnp.zeros((slots, count), F32)
    gate = jnp.zeros((slots, count), F32)
    for k in range(choices):
        hit = ids[k : k + 1, :] == wanted
        routed = jnp.where(hit, 1.0, routed)
        gate = jnp.where(hit, gates[k : k + 1, :], gate)
    row = lax.broadcasted_iota(jnp.int32, (count, count), 0)
    col = lax.broadcasted_iota(jnp.int32, (count, count), 1)
    served = jnp.where(order[...] == row, 1.0, 0.0).astype(BF16)
    earlier = jnp.where(row < col, 1.0, 0.0).astype(BF16)
    by_rank = product(routed.astype(BF16), served, 1, 0)
    before = product(by_rank.astype(BF16), earlier, 1, 0)
    taken = jnp.where(before.astype(jnp.int32) == slot % capacity, by_rank, 0.0).astype(BF16)
    pick = product(taken, served, 1, 1)
    turned_out[...] = product(served, taken, 1, 1).astype(BF16)
    slot_gate = jnp.sum(pick * gate, axis=1, keepdims=True)
    gate_out[...] = jnp.broadcast_to(slot_gate, gate_out.shape)
    pick = pick.astype(BF16)
    for copy, source, scale, outs in (
        (copies[3], tok, None, rows_out),
        (copies[4], cot, slot_gate, grads_out),
    ):
        copy.wait()
        for k in reversed(range(parts)):
            value = product(pick, source[:, columns(k, part)], 1, 0)
            value = value if scale is None else scale * value
            to = pl.ds((k % CORES) * part, part)
            outs[k // CORES][:, to] = value.astype(BF16)


def flip(chunks):
    return [chunks[0], *chunks[:0:-1]]


def join_kernel(groups, spread, capacity, *refs):
    by_x, chunks = refs[:spread], refs[spread:]
    half = by_x[0].shape[1]
    for ke in range(groups):
        for kx in range(spread):
            chunks[ke][:, kx * half : (kx + 1) * half] = by_x[kx][
                ke * capacity : (ke + 1) * capacity
            ]


def far_kernel(groups, spread, capacity, *refs):
    by_e, by_x = flip(refs[:groups]), refs[groups:]
    for ke in range(groups):
        for kx in range(1, spread):
            by_x[kx - 1][ke * capacity : (ke + 1) * capacity] = by_e[ke][
                kx * capacity : (kx + 1) * capacity
            ]


def partial(groups, spread, refs, outs):
    chunks, (own, sib) = flip(refs[:groups]), refs[groups:]
    part = own.shape[0]
    half = CORES * part
    rows = jnp.concatenate(
        [c[:, kx * half : (kx + 1) * half] for kx in range(spread) for c in chunks], axis=0
    )
    total = product(rows[:, :part], own[...], 1, 0) + product(rows[:, part:], sib[...], 1, 0)
    slots = rows.shape[0] // spread
    for kx in range(spread):
        outs[kx][...] = total[kx * slots : (kx + 1) * slots].astype(outs[kx].dtype)
    return rows


def pre_kernel(groups, spread, *refs):
    partial(groups, spread, refs[: groups + 2], refs[groups + 2 :])


def back_kernel(groups, spread, *refs):
    own, sib, *outs = refs[groups + 2 :]
    rows = partial(groups, spread, refs[: groups + 2], outs)
    part = own.shape[1]
    own[...] = rows[:, :part]
    sib[...] = rows[:, part:]


def summed(refs):
    total = refs[0][...]
    for ref in refs[1:]:
        total += ref[...].astype(F32)
    return total


def hidden_kernel(*refs):
    pre, out = summed(refs[:-1]), refs[-1]
    feed = out.shape[1]
    gate_act, up_act = pre[:, :feed], pre[:, feed:]
    out[...] = (gate_act * (1.0 / (1.0 + jnp.exp(-gate_act))) * up_act).astype(BF16)


def d_pre_kernel(*refs):
    spread = len(refs) // 2
    pre, back, out = summed(refs[:spread]), summed(refs[spread:-1]), refs[-1]
    feed = back.shape[1]
    gate_act, up_act = pre[:, :feed], pre[:, feed:]
    sig = 1.0 / (1.0 + jnp.exp(-gate_act))
    out[:, :feed] = (back * up_act * (sig * (1.0 + gate_act * (1.0 - sig)))).astype(BF16)
    out[:, feed:] = (back * (gate_act * sig)).astype(BF16)


def width_product(left, weights, store):
    rows = jnp.concatenate([r[...] for r in left], axis=0)
    for kc, weight in enumerate(weights):
        store(kc, product(rows, weight[...], 1, 1).astype(BF16))


def expert_out_kernel(groups, spread, capacity, *refs):
    chunks = refs[-groups:]
    part = refs[spread].shape[0]

    def store(kc, value):
        for ke in range(groups):
            for kx in range(spread):
                at = (kx * groups + ke) * capacity
                chunks[ke][kx * capacity : (kx + 1) * capacity, kc * part : (kc + 1) * part] = value[
                    at : at + capacity
                ]

    width_product(refs[:spread], refs[spread : spread + CORES], store)


def d_rows_kernel(spread, *refs):
    outs = refs[-spread:]
    part = refs[spread].shape[0]
    slots = outs[0].shape[0]

    def store(kc, value):
        for kx in range(spread):
            outs[kx][:, kc * part : (kc + 1) * part] = value[kx * slots : (kx + 1) * slots]

    width_product(refs[:spread], refs[spread : spread + CORES], store)


def weight_kernel(spread, own, sib, *refs):
    hidden, sib_hidden, out = refs[:spread], refs[spread:-1], refs[-1]
    left = jnp.concatenate([own[...], sib[...]], axis=0)
    right = jnp.concatenate([r[...] for r in (*hidden, *sib_hidden)], axis=0)
    out[...] = product(left, right, 0, 0)


def scatter(turned, groups_of_rows, out, held, sems):
    part = held.shape[2]
    copies = []
    for k, rows in enumerate(groups_of_rows):
        held[k] = product(turned, rows, 1, 0).astype(BF16)
        copies.append(pltpu.make_async_copy(held.at[k], out.at[:, columns(k, part)], sems.at[k]))
        copies[-1].start()
    for copy in copies:
        copy.wait()


def combine_kernel(groups, parts, capacity, turned, gate, *refs):
    chunks, far, (out, held, sems) = flip(refs[:groups]), refs[groups:-3], refs[-3:]
    part = held.shape[2]

    def weighted(k):
        cols = slice((k % CORES) * part, (k % CORES + 1) * part)
        if k < CORES:
            rows = jnp.concatenate([c[:capacity, cols] for c in chunks], axis=0)
        else:
            rows = far[k // CORES - 1][:, cols]
        rows = rows.astype(F32) * gate[:, :1]
        high = rows.astype(BF16)
        return jnp.concatenate([high, (rows - high.astype(F32)).astype(BF16)], axis=0)

    twice = jnp.concatenate([turned[...], turned[...]], axis=1)
    scatter(twice, map(weighted, range(parts)), out, held, sems)


def d_tokens_kernel(groups, parts, turned, *refs):
    chunks, (out, held, sems) = flip(refs[:groups]), refs[groups:]
    part = held.shape[2]
    rows = (
        jnp.concatenate([c[:, k * part : (k + 1) * part] for c in chunks], axis=0)
        for k in range(parts)
    )
    scatter(turned[...], rows, out, held, sems)


def per_device(tokens, cotangent, route_ids, route_gates, served_order, w_in, w_out):
    groups = lax.axis_size("expert")
    parts = lax.axis_size("fsdp")
    spread = parts // CORES
    count, width = tokens.shape
    capacity = count * route_ids.shape[1] // EXPERTS
    feed = w_out.shape[2]
    slots = groups * capacity
    half = width // spread
    part = width // parts

    def bound(kernel, *sizes):
        return lambda *refs: kernel(*sizes, *refs)

    def to_core(value):
        return lax.ppermute(value, "fsdp", [(i, i ^ 1) for i in range(parts)])

    def to_x(values):
        return [
            lax.ppermute(value, "fsdp", [(i, i ^ ((k + 1) * CORES)) for i in range(parts)])
            for k, value in enumerate(values)
        ]

    def to_expert(chunks):
        return [
            lax.ppermute(value, "expert", [(i, i ^ ke) for i in range(groups)]) if ke else value
            for ke, value in enumerate(chunks)
        ]

    chunk = [shape((capacity, width))] * groups
    by_x = [shape((slots, half))] * spread
    in_own, out_own = w_in[0], w_out[0]
    in_sib, out_sib = to_core(in_own), to_core(out_own)
    outs = call(
        bound(slot_kernel, spread),
        by_x * 2 + [shape((count, slots)), shape((slots, 128), F32)],
        (route_ids.T, route_gates.T, served_order, tokens, cotangent),
        far=5,
        scratch_shapes=[
            pltpu.VMEM(route_ids.shape[::-1], jnp.int32),
            pltpu.VMEM(route_gates.shape[::-1], F32),
            pltpu.VMEM(served_order.shape, jnp.int32),
            pltpu.VMEM(tokens.shape, BF16),
            pltpu.VMEM(cotangent.shape, BF16),
            pltpu.SemaphoreType.DMA((5,)),
        ],
    )
    turned, gate = outs[-2:]
    rows = [outs[0], *to_x(outs[1:spread])]
    grads = [outs[spread], *to_x(outs[spread + 1 : 2 * spread])]
    rows, in_sib, out_sib = lax.optimization_barrier((rows, in_sib, out_sib))
    join = bound(join_kernel, groups, spread, capacity)
    rows = to_expert(call(join, chunk, rows))
    grads = to_expert(call(join, chunk, grads))
    pre, *pre_far = call(
        bound(pre_kernel, groups, spread),
        [shape((slots, 2 * feed), F32)] + [shape((slots, 2 * feed))] * (spread - 1),
        (*flip(rows), in_own, in_sib),
    )
    pre = (pre, *to_x(pre_far))
    (hidden,) = call(hidden_kernel, [shape((slots, feed))], pre)
    hidden = (hidden, *to_x([hidden] * (spread - 1)))
    own_grads, sib_grads, back, *back_far = call(
        bound(back_kernel, groups, spread),
        [shape((spread * slots, part))] * 2
        + [shape((slots, feed), F32)]
        + [shape((slots, feed))] * (spread - 1),
        (*flip(grads), out_own, out_sib),
        cost=BACK_COST,
    )
    back = (back, *to_x(back_far))
    expert_out = to_expert(
        call(
            bound(expert_out_kernel, groups, spread, capacity),
            [shape((spread * capacity, half))] * groups,
            (*hidden, out_own, out_sib),
            cost=OUT_COST,
        )
    )
    (d_pre,) = call(
        d_pre_kernel, [shape((slots, 2 * feed))], (*pre, *back), after=hidden[:1]
    )
    d_pre = (d_pre, *to_x([d_pre] * (spread - 1)))
    near, *far = call(
        bound(d_rows_kernel, spread), by_x, (*d_pre, in_own, in_sib), after=expert_out[1:2]
    )
    d_rows = to_expert(call(join, chunk, (near, *to_x(far))))
    far = to_x(
        call(bound(far_kernel, groups, spread, capacity), by_x[1:], flip(expert_out))
    )
    d_w_out, token = call(
        bound(weight_kernel, spread),
        [shape((part, feed), F32)],
        (own_grads, to_core(sib_grads), *hidden, *[to_core(value) for value in hidden]),
        token=True,
    )

    def scattered(kernel, operands, **kw):
        return call(
            kernel,
            [shape((count, width))],
            operands,
            out_specs=[pl.BlockSpec(memory_space=pltpu.HBM)]
            + [pl.BlockSpec(memory_space=pltpu.VMEM)] * kw.get("token", False),
            scratch_shapes=[
                pltpu.VMEM((parts, count, part), BF16),
                pltpu.SemaphoreType.DMA((parts,)),
            ],
            **kw,
        )

    combined, token = scattered(
        bound(combine_kernel, groups, parts, capacity),
        (turned, gate, *flip(expert_out), *far),
        after=(token,),
        token=True,
    )
    (d_tokens,) = scattered(
        bound(d_tokens_kernel, groups, parts), (turned, *flip(d_rows)), after=(token,)
    )
    return combined, d_tokens, d_w_out[None]


def solution(mesh):
    rows = P(("replica", "expert", "fsdp"), None)
    weights = P("expert", "fsdp", None)
    return jax.shard_map(
        per_device,
        mesh=mesh,
        in_specs=(rows,) * 5 + (weights,) * 2,
        out_specs=(rows, rows, P(("replica", "expert"), "fsdp", None)),
        check_vma=False,
    )
```

```python
import jax
import jax.numpy as jnp
from jax import lax
from jax.experimental import pallas as pl
from jax.experimental.pallas import tpu as pltpu
from jax.sharding import PartitionSpec as P

EXPERTS = 128
CORES = 2
OUT_COST = 2000000000
BACK_COST = 12000000000
VMEM = 40 * 1024 * 1024
F32 = jnp.float32
BF16 = jnp.bfloat16


def product(left, right, left_dim, right_dim, **kw):
    return lax.dot_general(
        left, right, (((left_dim,), (right_dim,)), ((), ())), preferred_element_type=F32, **kw
    )


def call(body, out_shape, args, far=0, cost=0, after=(), token=False, **kw):
    out_shape = [*out_shape] + [shape((8, 128), F32)] * token
    specs = [pl.BlockSpec(memory_space=pltpu.VMEM)] * (len(args) - far)
    specs += [pl.BlockSpec(memory_space=pltpu.HBM)] * far
    specs += [pl.BlockSpec(memory_space=pl.ANY)] * len(after)
    kw.setdefault("out_specs", [pl.BlockSpec(memory_space=pltpu.VMEM)] * len(out_shape))
    args = [
        pltpu.with_memory_space_constraint(arg, pltpu.HBM) if i >= len(args) - far else arg
        for i, arg in enumerate(args)
    ]
    count, first, last = len(args), len(args) + len(after), len(args) + len(after) + len(out_shape)

    def kernel(*refs):
        if token:
            refs[last - 1][...] = jnp.zeros(refs[last - 1].shape, F32)
        body(*refs[:count], *refs[first : last - token], *refs[last:])

    return pl.pallas_call(
        kernel,
        out_shape=out_shape,
        in_specs=specs,
        compiler_params=pltpu.CompilerParams(vmem_limit_bytes=VMEM),
        cost_estimate=pl.CostEstimate(flops=cost, bytes_accessed=0, transcendentals=0),
        **kw,
    )(*args, *after)


def shape(dims, kind=BF16):
    return jax.ShapeDtypeStruct(dims, kind)


def columns(k, part):
    return pl.ds(pl.multiple_of((lax.axis_index("fsdp") ^ k) * part, part), part)


def slot_kernel(spread, *refs):
    sources, rows_out, grads_out, refs = refs[:5], refs[5 : 5 + spread], refs[5 + spread : 5 + 2 * spread], refs[5 + 2 * spread :]
    turned_out, gate_out, ids, gates, order, tok, cot, sems = refs
    parts = spread * CORES
    copies = [
        pltpu.make_async_copy(source, target, sems.at[i])
        for i, (source, target) in enumerate(zip(sources, (ids, gates, order, tok, cot)))
    ]
    for copy in copies:
        copy.start()
    for copy in copies[:3]:
        copy.wait()
    choices, count = ids.shape
    slots = gate_out.shape[0]
    groups = lax.axis_size("expert")
    capacity = slots // groups
    part = tok.shape[1] // parts
    slot = lax.broadcasted_iota(jnp.int32, (slots, count), 0)
    wanted = ((slot // capacity) ^ lax.axis_index("expert")) * (EXPERTS // groups)
    routed = jnp.zeros((slots, count), F32)
    gate = jnp.zeros((slots, count), F32)
    for k in range(choices):
        hit = ids[k : k + 1, :] == wanted
        routed = jnp.where(hit, 1.0, routed)
        gate = jnp.where(hit, gates[k : k + 1, :], gate)
    row = lax.broadcasted_iota(jnp.int32, (count, count), 0)
    col = lax.broadcasted_iota(jnp.int32, (count, count), 1)
    served = jnp.where(order[...] == row, 1.0, 0.0).astype(BF16)
    earlier = jnp.where(row < col, 1.0, 0.0).astype(BF16)
    by_rank = product(routed.astype(BF16), served, 1, 0)
    before = product(by_rank.astype(BF16), earlier, 1, 0)
    taken = jnp.where(before.astype(jnp.int32) == slot % capacity, by_rank, 0.0).astype(BF16)
    pick = product(taken, served, 1, 1)
    turned_out[...] = product(served, taken, 1, 1).astype(BF16)
    slot_gate = jnp.sum(pick * gate, axis=1, keepdims=True)
    gate_out[...] = jnp.broadcast_to(slot_gate, gate_out.shape)
    pick = pick.astype(BF16)
    for copy, source, scale, outs in (
        (copies[3], tok, None, rows_out),
        (copies[4], cot, slot_gate, grads_out),
    ):
        copy.wait()
        for k in reversed(range(parts)):
            value = product(pick, source[:, columns(k, part)], 1, 0)
            value = value if scale is None else scale * value
            to = pl.ds((k % CORES) * part, part)
            outs[k // CORES][:, to] = value.astype(BF16)


def flip(chunks):
    return [chunks[0], *chunks[:0:-1]]


def join_kernel(groups, spread, capacity, *refs):
    by_x, chunks = refs[:spread], refs[spread:]
    half = by_x[0].shape[1]
    for ke in range(groups):
        for kx in range(spread):
            chunks[ke][:, kx * half : (kx + 1) * half] = by_x[kx][
                ke * capacity : (ke + 1) * capacity
            ]


def far_kernel(groups, spread, capacity, *refs):
    by_e, by_x = flip(refs[:groups]), refs[groups:]
    for ke in range(groups):
        for kx in range(1, spread):
            by_x[kx - 1][ke * capacity : (ke + 1) * capacity] = by_e[ke][
                kx * capacity : (kx + 1) * capacity
            ]


def partial(groups, spread, refs, outs):
    chunks, (own, sib) = flip(refs[:groups]), refs[groups:]
    part = own.shape[0]
    half = CORES * part
    rows = jnp.concatenate(
        [c[:, kx * half : (kx + 1) * half] for kx in range(spread) for c in chunks], axis=0
    )
    total = product(rows[:, :part], own[...], 1, 0) + product(rows[:, part:], sib[...], 1, 0)
    slots = rows.shape[0] // spread
    for kx in range(spread):
        outs[kx][...] = total[kx * slots : (kx + 1) * slots].astype(outs[kx].dtype)
    return rows


def pre_kernel(groups, spread, *refs):
    partial(groups, spread, refs[: groups + 2], refs[groups + 2 :])


def back_kernel(groups, spread, *refs):
    own, sib, *outs = refs[groups + 2 :]
    rows = partial(groups, spread, refs[: groups + 2], outs)
    part = own.shape[1]
    own[...] = rows[:, :part]
    sib[...] = rows[:, part:]


def summed(refs):
    total = refs[0][...]
    for ref in refs[1:]:
        total += ref[...].astype(F32)
    return total


def hidden_kernel(*refs):
    pre, out = summed(refs[:-1]), refs[-1]
    feed = out.shape[1]
    gate_act, up_act = pre[:, :feed], pre[:, feed:]
    out[...] = (gate_act * (1.0 / (1.0 + jnp.exp(-gate_act))) * up_act).astype(BF16)


def d_pre_kernel(*refs):
    spread = len(refs) // 2
    pre, back, out = summed(refs[:spread]), summed(refs[spread:-1]), refs[-1]
    feed = back.shape[1]
    gate_act, up_act = pre[:, :feed], pre[:, feed:]
    sig = 1.0 / (1.0 + jnp.exp(-gate_act))
    out[:, :feed] = (back * up_act * (sig * (1.0 + gate_act * (1.0 - sig)))).astype(BF16)
    out[:, feed:] = (back * (gate_act * sig)).astype(BF16)


def width_product(left, weights, store):
    rows = jnp.concatenate([r[...] for r in left], axis=0)
    for kc, weight in enumerate(weights):
        store(kc, product(rows, weight[...], 1, 1).astype(BF16))


def expert_out_kernel(groups, spread, capacity, *refs):
    chunks = refs[-groups:]
    part = refs[spread].shape[0]

    def store(kc, value):
        for ke in range(groups):
            for kx in range(spread):
                at = (kx * groups + ke) * capacity
                chunks[ke][kx * capacity : (kx + 1) * capacity, kc * part : (kc + 1) * part] = value[
                    at : at + capacity
                ]

    width_product(refs[:spread], refs[spread : spread + CORES], store)


def d_rows_kernel(spread, *refs):
    outs = refs[-spread:]
    part = refs[spread].shape[0]
    slots = outs[0].shape[0]

    def store(kc, value):
        for kx in range(spread):
            outs[kx][:, kc * part : (kc + 1) * part] = value[kx * slots : (kx + 1) * slots]

    width_product(refs[:spread], refs[spread : spread + CORES], store)


def weight_kernel(spread, own, sib, *refs):
    hidden, sib_hidden, out = refs[:spread], refs[spread:-1], refs[-1]
    left = jnp.concatenate([own[...], sib[...]], axis=0)
    right = jnp.concatenate([r[...] for r in (*hidden, *sib_hidden)], axis=0)
    out[...] = product(left, right, 0, 0)


def scatter(turned, groups_of_rows, out, held, sems):
    part = held.shape[2]
    copies = []
    for k, rows in enumerate(groups_of_rows):
        held[k] = product(turned, rows, 1, 0).astype(BF16)
        copies.append(pltpu.make_async_copy(held.at[k], out.at[:, columns(k, part)], sems.at[k]))
        copies[-1].start()
    for copy in copies:
        copy.wait()


def combine_kernel(groups, parts, capacity, turned, gate, *refs):
    chunks, far, (out, held, sems) = flip(refs[:groups]), refs[groups:-3], refs[-3:]
    part = held.shape[2]

    def weighted(k):
        cols = slice((k % CORES) * part, (k % CORES + 1) * part)
        if k < CORES:
            rows = jnp.concatenate([c[:capacity, cols] for c in chunks], axis=0)
        else:
            rows = far[k // CORES - 1][:, cols]
        rows = rows.astype(F32) * gate[:, :1]
        high = rows.astype(BF16)
        return jnp.concatenate([high, (rows - high.astype(F32)).astype(BF16)], axis=0)

    twice = jnp.concatenate([turned[...], turned[...]], axis=1)
    scatter(twice, map(weighted, range(parts)), out, held, sems)


def d_tokens_kernel(groups, parts, turned, *refs):
    chunks, (out, held, sems) = flip(refs[:groups]), refs[groups:]
    part = held.shape[2]
    rows = (
        jnp.concatenate([c[:, k * part : (k + 1) * part] for c in chunks], axis=0)
        for k in range(parts)
    )
    scatter(turned[...], rows, out, held, sems)


def per_device(tokens, cotangent, route_ids, route_gates, served_order, w_in, w_out):
    groups = lax.axis_size("expert")
    parts = lax.axis_size("fsdp")
    spread = parts // CORES
    count, width = tokens.shape
    capacity = count * route_ids.shape[1] // EXPERTS
    feed = w_out.shape[2]
    slots = groups * capacity
    half = width // spread
    part = width // parts

    def bound(kernel, *sizes):
        return lambda *refs: kernel(*sizes, *refs)

    def to_core(value):
        return lax.ppermute(value, "fsdp", [(i, i ^ 1) for i in range(parts)])

    def to_x(values):
        return [
            lax.ppermute(value, "fsdp", [(i, i ^ ((k + 1) * CORES)) for i in range(parts)])
            for k, value in enumerate(values)
        ]

    def to_expert(chunks):
        return [
            lax.ppermute(value, "expert", [(i, i ^ ke) for i in range(groups)]) if ke else value
            for ke, value in enumerate(chunks)
        ]

    chunk = [shape((capacity, width))] * groups
    by_x = [shape((slots, half))] * spread
    in_own, out_own = w_in[0], w_out[0]
    in_sib, out_sib = to_core(in_own), to_core(out_own)
    outs = call(
        bound(slot_kernel, spread),
        by_x * 2 + [shape((count, slots)), shape((slots, 128), F32)],
        (route_ids.T, route_gates.T, served_order, tokens, cotangent),
        far=5,
        scratch_shapes=[
            pltpu.VMEM(route_ids.shape[::-1], jnp.int32),
            pltpu.VMEM(route_gates.shape[::-1], F32),
            pltpu.VMEM(served_order.shape, jnp.int32),
            pltpu.VMEM(tokens.shape, BF16),
            pltpu.VMEM(cotangent.shape, BF16),
            pltpu.SemaphoreType.DMA((5,)),
        ],
    )
    turned, gate = outs[-2:]
    rows = [outs[0], *to_x(outs[1:spread])]
    grads = [outs[spread], *to_x(outs[spread + 1 : 2 * spread])]
    rows, in_sib, out_sib = lax.optimization_barrier((rows, in_sib, out_sib))
    join = bound(join_kernel, groups, spread, capacity)
    rows = to_expert(call(join, chunk, rows))
    grads = to_expert(call(join, chunk, grads))
    pre, *pre_far = call(
        bound(pre_kernel, groups, spread),
        [shape((slots, 2 * feed), F32)] + [shape((slots, 2 * feed))] * (spread - 1),
        (*flip(rows), in_own, in_sib),
    )
    pre = (pre, *to_x(pre_far))
    (hidden,) = call(hidden_kernel, [shape((slots, feed))], pre)
    hidden = (hidden, *to_x([hidden] * (spread - 1)))
    own_grads, sib_grads, back, *back_far = call(
        bound(back_kernel, groups, spread),
        [shape((spread * slots, part))] * 2
        + [shape((slots, feed), F32)]
        + [shape((slots, feed))] * (spread - 1),
        (*flip(grads), out_own, out_sib),
        cost=BACK_COST,
    )
    back = (back, *to_x(back_far))
    expert_out = to_expert(
        call(
            bound(expert_out_kernel, groups, spread, capacity),
            [shape((spread * capacity, half))] * groups,
            (*hidden, out_own, out_sib),
            cost=OUT_COST,
        )
    )
    (d_pre,) = call(
        d_pre_kernel, [shape((slots, 2 * feed))], (*pre, *back), after=hidden[:1]
    )
    d_pre = (d_pre, *to_x([d_pre] * (spread - 1)))
    near, *far = call(
        bound(d_rows_kernel, spread), by_x, (*d_pre, in_own, in_sib)
    )
    d_rows = to_expert(call(join, chunk, (near, *to_x(far))))
    far = to_x(
        call(bound(far_kernel, groups, spread, capacity), by_x[1:], flip(expert_out))
    )
    d_w_out, token = call(
        bound(weight_kernel, spread),
        [shape((part, feed), F32)],
        (own_grads, to_core(sib_grads), *hidden, *[to_core(value) for value in hidden]),
        token=True,
    )

    def scattered(kernel, operands, **kw):
        return call(
            kernel,
            [shape((count, width))],
            operands,
            out_specs=[pl.BlockSpec(memory_space=pltpu.HBM)]
            + [pl.BlockSpec(memory_space=pltpu.VMEM)] * kw.get("token", False),
            scratch_shapes=[
                pltpu.VMEM((parts, count, part), BF16),
                pltpu.SemaphoreType.DMA((parts,)),
            ],
            **kw,
        )

    combined, token = scattered(
        bound(combine_kernel, groups, parts, capacity),
        (turned, gate, *flip(expert_out), *far),
        after=(token,),
        token=True,
    )
    (d_tokens,) = scattered(
        bound(d_tokens_kernel, groups, parts), (turned, *flip(d_rows)), after=(token,)
    )
    return combined, d_tokens, d_w_out[None]


def solution(mesh):
    rows = P(("replica", "expert", "fsdp"), None)
    weights = P("expert", "fsdp", None)
    return jax.shard_map(
        per_device,
        mesh=mesh,
        in_specs=(rows,) * 5 + (weights,) * 2,
        out_specs=(rows, rows, P(("replica", "expert"), "fsdp", None)),
        check_vma=False,
    )
```

```python
import jax
import jax.numpy as jnp
from jax import lax
from jax.experimental import pallas as pl
from jax.experimental.pallas import tpu as pltpu
from jax.sharding import PartitionSpec as P

EXPERTS = 128
CORES = 2
OUT_COST = 2000000000
BACK_COST = 12000000000
VMEM = 40 * 1024 * 1024
F32 = jnp.float32
BF16 = jnp.bfloat16


def product(left, right, left_dim, right_dim, **kw):
    return lax.dot_general(
        left, right, (((left_dim,), (right_dim,)), ((), ())), preferred_element_type=F32, **kw
    )


def call(body, out_shape, args, far=0, cost=0, after=(), token=False, **kw):
    out_shape = [*out_shape] + [shape((8, 128), F32)] * token
    specs = [pl.BlockSpec(memory_space=pltpu.VMEM)] * (len(args) - far)
    specs += [pl.BlockSpec(memory_space=pltpu.HBM)] * far
    specs += [pl.BlockSpec(memory_space=pl.ANY)] * len(after)
    kw.setdefault("out_specs", [pl.BlockSpec(memory_space=pltpu.VMEM)] * len(out_shape))
    args = [
        pltpu.with_memory_space_constraint(arg, pltpu.HBM) if i >= len(args) - far else arg
        for i, arg in enumerate(args)
    ]
    count, first, last = len(args), len(args) + len(after), len(args) + len(after) + len(out_shape)

    def kernel(*refs):
        if token:
            refs[last - 1][...] = jnp.zeros(refs[last - 1].shape, F32)
        body(*refs[:count], *refs[first : last - token], *refs[last:])

    return pl.pallas_call(
        kernel,
        out_shape=out_shape,
        in_specs=specs,
        compiler_params=pltpu.CompilerParams(vmem_limit_bytes=VMEM),
        cost_estimate=pl.CostEstimate(flops=cost, bytes_accessed=0, transcendentals=0),
        **kw,
    )(*args, *after)


def shape(dims, kind=BF16):
    return jax.ShapeDtypeStruct(dims, kind)


def columns(k, part):
    return pl.ds(pl.multiple_of((lax.axis_index("fsdp") ^ k) * part, part), part)


def slot_kernel(spread, *refs):
    sources, rows_out, refs = refs[:5], refs[5 : 5 + spread], refs[5 + spread :]
    pick_out, turned_out, gate_out, cot, ids, gates, order, tok, sems = refs
    parts = spread * CORES
    copies = [
        pltpu.make_async_copy(source, target, sems.at[i])
        for i, (source, target) in enumerate(zip(sources, (ids, gates, order, tok, cot)))
    ]
    for copy in copies:
        copy.start()
    for copy in copies[:3]:
        copy.wait()
    choices, count = ids.shape
    slots = gate_out.shape[0]
    groups = lax.axis_size("expert")
    capacity = slots // groups
    part = tok.shape[1] // parts
    slot = lax.broadcasted_iota(jnp.int32, (slots, count), 0)
    wanted = ((slot // capacity) ^ lax.axis_index("expert")) * (EXPERTS // groups)
    routed = jnp.zeros((slots, count), F32)
    gate = jnp.zeros((slots, count), F32)
    for k in range(choices):
        hit = ids[k : k + 1, :] == wanted
        routed = jnp.where(hit, 1.0, routed)
        gate = jnp.where(hit, gates[k : k + 1, :], gate)
    row = lax.broadcasted_iota(jnp.int32, (count, count), 0)
    col = lax.broadcasted_iota(jnp.int32, (count, count), 1)
    served = jnp.where(order[...] == row, 1.0, 0.0).astype(BF16)
    earlier = jnp.where(row < col, 1.0, 0.0).astype(BF16)
    by_rank = product(routed.astype(BF16), served, 1, 0)
    before = product(by_rank.astype(BF16), earlier, 1, 0)
    taken = jnp.where(before.astype(jnp.int32) == slot % capacity, by_rank, 0.0).astype(BF16)
    pick = product(taken, served, 1, 1)
    turned_out[...] = product(served, taken, 1, 1).astype(BF16)
    slot_gate = jnp.sum(pick * gate, axis=1, keepdims=True)
    gate_out[...] = jnp.broadcast_to(slot_gate, gate_out.shape)
    pick = pick.astype(BF16)
    pick_out[...] = pick
    copies[3].wait()
    for k in reversed(range(parts)):
        value = product(pick, tok[:, columns(k, part)], 1, 0)
        rows_out[k // CORES][:, pl.ds((k % CORES) * part, part)] = value.astype(BF16)
    copies[4].wait()


def grads_kernel(spread, pick, gate, cot, *outs):
    parts = spread * CORES
    part = cot.shape[1] // parts
    for k in reversed(range(parts)):
        value = gate[:, :1] * product(pick[...], cot[:, columns(k, part)], 1, 0)
        outs[k // CORES][:, pl.ds((k % CORES) * part, part)] = value.astype(BF16)


def flip(chunks):
    return [chunks[0], *chunks[:0:-1]]


def join_kernel(groups, spread, capacity, *refs):
    by_x, chunks = refs[:spread], refs[spread:]
    half = by_x[0].shape[1]
    for ke in range(groups):
        for kx in range(spread):
            chunks[ke][:, kx * half : (kx + 1) * half] = by_x[kx][
                ke * capacity : (ke + 1) * capacity
            ]


def far_kernel(groups, spread, capacity, *refs):
    by_e, by_x = flip(refs[:groups]), refs[groups:]
    for ke in range(groups):
        for kx in range(1, spread):
            by_x[kx - 1][ke * capacity : (ke + 1) * capacity] = by_e[ke][
                kx * capacity : (kx + 1) * capacity
            ]


def partial(groups, spread, refs, outs):
    chunks, (own, sib) = flip(refs[:groups]), refs[groups:]
    part = own.shape[0]
    half = CORES * part
    rows = jnp.concatenate(
        [c[:, kx * half : (kx + 1) * half] for kx in range(spread) for c in chunks], axis=0
    )
    total = product(rows[:, :part], own[...], 1, 0) + product(rows[:, part:], sib[...], 1, 0)
    slots = rows.shape[0] // spread
    for kx in range(spread):
        outs[kx][...] = total[kx * slots : (kx + 1) * slots].astype(outs[kx].dtype)
    return rows


def pre_kernel(groups, spread, *refs):
    partial(groups, spread, refs[: groups + 2], refs[groups + 2 :])


def back_kernel(groups, spread, *refs):
    own, sib, *outs = refs[groups + 2 :]
    rows = partial(groups, spread, refs[: groups + 2], outs)
    part = own.shape[1]
    own[...] = rows[:, :part]
    sib[...] = rows[:, part:]


def summed(refs):
    total = refs[0][...]
    for ref in refs[1:]:
        total += ref[...].astype(F32)
    return total


def hidden_kernel(*refs):
    pre, out = summed(refs[:-1]), refs[-1]
    feed = out.shape[1]
    gate_act, up_act = pre[:, :feed], pre[:, feed:]
    out[...] = (gate_act * (1.0 / (1.0 + jnp.exp(-gate_act))) * up_act).astype(BF16)


def d_pre_kernel(*refs):
    spread = len(refs) // 2
    pre, back, out = summed(refs[:spread]), summed(refs[spread:-1]), refs[-1]
    feed = back.shape[1]
    gate_act, up_act = pre[:, :feed], pre[:, feed:]
    sig = 1.0 / (1.0 + jnp.exp(-gate_act))
    out[:, :feed] = (back * up_act * (sig * (1.0 + gate_act * (1.0 - sig)))).astype(BF16)
    out[:, feed:] = (back * (gate_act * sig)).astype(BF16)


def width_product(left, weights, store):
    rows = jnp.concatenate([r[...] for r in left], axis=0)
    for kc, weight in enumerate(weights):
        store(kc, product(rows, weight[...], 1, 1).astype(BF16))


def expert_out_kernel(groups, spread, capacity, *refs):
    chunks = refs[-groups:]
    part = refs[spread].shape[0]

    def store(kc, value):
        for ke in range(groups):
            for kx in range(spread):
                at = (kx * groups + ke) * capacity
                chunks[ke][kx * capacity : (kx + 1) * capacity, kc * part : (kc + 1) * part] = value[
                    at : at + capacity
                ]

    width_product(refs[:spread], refs[spread : spread + CORES], store)


def d_rows_kernel(spread, *refs):
    outs = refs[-spread:]
    part = refs[spread].shape[0]
    slots = outs[0].shape[0]

    def store(kc, value):
        for kx in range(spread):
            outs[kx][:, kc * part : (kc + 1) * part] = value[kx * slots : (kx + 1) * slots]

    width_product(refs[:spread], refs[spread : spread + CORES], store)


def weight_kernel(spread, own, sib, *refs):
    hidden, sib_hidden, out = refs[:spread], refs[spread:-1], refs[-1]
    left = jnp.concatenate([own[...], sib[...]], axis=0)
    right = jnp.concatenate([r[...] for r in (*hidden, *sib_hidden)], axis=0)
    out[...] = product(left, right, 0, 0)


def scatter(turned, groups_of_rows, out, held, sems):
    part = held.shape[2]
    copies = []
    for k, rows in enumerate(groups_of_rows):
        held[k] = product(turned, rows, 1, 0).astype(BF16)
        copies.append(pltpu.make_async_copy(held.at[k], out.at[:, columns(k, part)], sems.at[k]))
        copies[-1].start()
    for copy in copies:
        copy.wait()


def combine_kernel(groups, parts, capacity, turned, gate, *refs):
    chunks, far, (out, held, sems) = flip(refs[:groups]), refs[groups:-3], refs[-3:]
    part = held.shape[2]

    def weighted(k):
        cols = slice((k % CORES) * part, (k % CORES + 1) * part)
        if k < CORES:
            rows = jnp.concatenate([c[:capacity, cols] for c in chunks], axis=0)
        else:
            rows = far[k // CORES - 1][:, cols]
        rows = rows.astype(F32) * gate[:, :1]
        high = rows.astype(BF16)
        return jnp.concatenate([high, (rows - high.astype(F32)).astype(BF16)], axis=0)

    twice = jnp.concatenate([turned[...], turned[...]], axis=1)
    scatter(twice, map(weighted, range(parts)), out, held, sems)


def d_tokens_kernel(groups, parts, turned, *refs):
    chunks, (out, held, sems) = flip(refs[:groups]), refs[groups:]
    part = held.shape[2]
    rows = (
        jnp.concatenate([c[:, k * part : (k + 1) * part] for c in chunks], axis=0)
        for k in range(parts)
    )
    scatter(turned[...], rows, out, held, sems)


def per_device(tokens, cotangent, route_ids, route_gates, served_order, w_in, w_out):
    groups = lax.axis_size("expert")
    parts = lax.axis_size("fsdp")
    spread = parts // CORES
    count, width = tokens.shape
    capacity = count * route_ids.shape[1] // EXPERTS
    feed = w_out.shape[2]
    slots = groups * capacity
    half = width // spread
    part = width // parts

    def bound(kernel, *sizes):
        return lambda *refs: kernel(*sizes, *refs)

    def to_core(value):
        return lax.ppermute(value, "fsdp", [(i, i ^ 1) for i in range(parts)])

    def to_x(values):
        return [
            lax.ppermute(value, "fsdp", [(i, i ^ ((k + 1) * CORES)) for i in range(parts)])
            for k, value in enumerate(values)
        ]

    def to_expert(chunks):
        return [
            lax.ppermute(value, "expert", [(i, i ^ ke) for i in range(groups)]) if ke else value
            for ke, value in enumerate(chunks)
        ]

    chunk = [shape((capacity, width))] * groups
    by_x = [shape((slots, half))] * spread
    in_own, out_own = w_in[0], w_out[0]
    *rows, pick, turned, gate, cotangent = call(
        bound(slot_kernel, spread),
        by_x
        + [shape((slots, count)), shape((count, slots)), shape((slots, 128), F32)]
        + [shape(cotangent.shape)],
        (route_ids.T, route_gates.T, served_order, tokens, cotangent),
        far=5,
        scratch_shapes=[
            pltpu.VMEM(route_ids.shape[::-1], jnp.int32),
            pltpu.VMEM(route_gates.shape[::-1], F32),
            pltpu.VMEM(served_order.shape, jnp.int32),
            pltpu.VMEM(tokens.shape, BF16),
            pltpu.SemaphoreType.DMA((5,)),
        ],
    )
    rows[1:] = to_x(rows[1:])
    grads = list(call(bound(grads_kernel, spread), by_x, (pick, gate, cotangent)))
    grads[1:] = to_x(grads[1:])
    in_own, out_own, _ = lax.optimization_barrier((in_own, out_own, turned))
    in_sib, out_sib = to_core(in_own), to_core(out_own)
    rows, in_sib, out_sib = lax.optimization_barrier((rows, in_sib, out_sib))
    join = bound(join_kernel, groups, spread, capacity)
    rows = to_expert(call(join, chunk, rows))
    grads = to_expert(call(join, chunk, grads))
    pre, *pre_far = call(
        bound(pre_kernel, groups, spread),
        [shape((slots, 2 * feed), F32)] + [shape((slots, 2 * feed))] * (spread - 1),
        (*flip(rows), in_own, in_sib),
    )
    pre = (pre, *to_x(pre_far))
    (hidden,) = call(hidden_kernel, [shape((slots, feed))], pre)
    hidden = (hidden, *to_x([hidden] * (spread - 1)))
    own_grads, sib_grads, back, *back_far = call(
        bound(back_kernel, groups, spread),
        [shape((spread * slots, part))] * 2
        + [shape((slots, feed), F32)]
        + [shape((slots, feed))] * (spread - 1),
        (*flip(grads), out_own, out_sib),
        cost=BACK_COST,
    )
    back = (back, *to_x(back_far))
    expert_out = to_expert(
        call(
            bound(expert_out_kernel, groups, spread, capacity),
            [shape((spread * capacity, half))] * groups,
            (*hidden, out_own, out_sib),
            cost=OUT_COST,
        )
    )
    (d_pre,) = call(
        d_pre_kernel, [shape((slots, 2 * feed))], (*pre, *back), after=hidden[:1]
    )
    d_pre = (d_pre, *to_x([d_pre] * (spread - 1)))
    near, *far = call(
        bound(d_rows_kernel, spread), by_x, (*d_pre, in_own, in_sib)
    )
    d_rows = to_expert(call(join, chunk, (near, *to_x(far))))
    far = to_x(
        call(bound(far_kernel, groups, spread, capacity), by_x[1:], flip(expert_out))
    )
    d_w_out, token = call(
        bound(weight_kernel, spread),
        [shape((part, feed), F32)],
        (own_grads, to_core(sib_grads), *hidden, *[to_core(value) for value in hidden]),
        token=True,
    )

    def scattered(kernel, operands, **kw):
        return call(
            kernel,
            [shape((count, width))],
            operands,
            out_specs=[pl.BlockSpec(memory_space=pltpu.HBM)]
            + [pl.BlockSpec(memory_space=pltpu.VMEM)] * kw.get("token", False),
            scratch_shapes=[
                pltpu.VMEM((parts, count, part), BF16),
                pltpu.SemaphoreType.DMA((parts,)),
            ],
            **kw,
        )

    combined, token = scattered(
        bound(combine_kernel, groups, parts, capacity),
        (turned, gate, *flip(expert_out), *far),
        after=(token,),
        token=True,
    )
    (d_tokens,) = scattered(
        bound(d_tokens_kernel, groups, parts), (turned, *flip(d_rows)), after=(token,)
    )
    return combined, d_tokens, d_w_out[None]


def solution(mesh):
    rows = P(("replica", "expert", "fsdp"), None)
    weights = P("expert", "fsdp", None)
    return jax.shard_map(
        per_device,
        mesh=mesh,
        in_specs=(rows,) * 5 + (weights,) * 2,
        out_specs=(rows, rows, P(("replica", "expert"), "fsdp", None)),
        check_vma=False,
    )
```

```python
import jax
import jax.numpy as jnp
from jax import lax
from jax.experimental import pallas as pl
from jax.experimental.pallas import tpu as pltpu
from jax.sharding import PartitionSpec as P

EXPERTS = 128
CORES = 2
OUT_COST = 2000000000
PRE_COST = 4500000000
JOIN_COST = 1000000000
BACK_COST = 3000000000
VMEM = 40 * 1024 * 1024
F32 = jnp.float32
BF16 = jnp.bfloat16


def product(left, right, left_dim, right_dim, **kw):
    return lax.dot_general(
        left, right, (((left_dim,), (right_dim,)), ((), ())), preferred_element_type=F32, **kw
    )


def call(body, out_shape, args, far=0, cost=0, after=(), token=False, **kw):
    out_shape = [*out_shape] + [shape((8, 128), F32)] * token
    specs = [pl.BlockSpec(memory_space=pltpu.VMEM)] * (len(args) - far)
    specs += [pl.BlockSpec(memory_space=pltpu.HBM)] * far
    specs += [pl.BlockSpec(memory_space=pl.ANY)] * len(after)
    kw.setdefault("out_specs", [pl.BlockSpec(memory_space=pltpu.VMEM)] * len(out_shape))
    args = [
        pltpu.with_memory_space_constraint(arg, pltpu.HBM) if i >= len(args) - far else arg
        for i, arg in enumerate(args)
    ]
    count, first, last = len(args), len(args) + len(after), len(args) + len(after) + len(out_shape)

    def kernel(*refs):
        if token:
            refs[last - 1][...] = jnp.zeros(refs[last - 1].shape, F32)
        body(*refs[:count], *refs[first : last - token], *refs[last:])

    return pl.pallas_call(
        kernel,
        out_shape=out_shape,
        in_specs=specs,
        compiler_params=pltpu.CompilerParams(vmem_limit_bytes=VMEM),
        cost_estimate=pl.CostEstimate(flops=cost, bytes_accessed=0, transcendentals=0),
        **kw,
    )(*args, *after)


def shape(dims, kind=BF16):
    return jax.ShapeDtypeStruct(dims, kind)


def columns(k, part):
    return pl.ds(pl.multiple_of((lax.axis_index("fsdp") ^ k) * part, part), part)


def slot_kernel(spread, *refs):
    sources, refs = refs[:5], refs[5:]
    rows_out, refs = refs[: 2 * spread - 1], refs[2 * spread - 1 :]
    grads_out, refs = refs[:spread], refs[spread:]
    turned_out, gate_out, ids, gates, order, tok, cot, sems = refs
    parts = spread * CORES
    copies = [
        pltpu.make_async_copy(source, target, sems.at[i])
        for i, (source, target) in enumerate(zip(sources, (ids, gates, order, tok, cot)))
    ]
    for copy in copies:
        copy.start()
    for copy in copies[:3]:
        copy.wait()
    choices, count = ids.shape
    slots = gate_out.shape[0]
    groups = lax.axis_size("expert")
    capacity = slots // groups
    part = tok.shape[1] // parts
    slot = lax.broadcasted_iota(jnp.int32, (slots, count), 0)
    wanted = ((slot // capacity) ^ lax.axis_index("expert")) * (EXPERTS // groups)
    routed = jnp.zeros((slots, count), F32)
    gate = jnp.zeros((slots, count), F32)
    for k in range(choices):
        hit = ids[k : k + 1, :] == wanted
        routed = jnp.where(hit, 1.0, routed)
        gate = jnp.where(hit, gates[k : k + 1, :], gate)
    row = lax.broadcasted_iota(jnp.int32, (count, count), 0)
    col = lax.broadcasted_iota(jnp.int32, (count, count), 1)
    served = jnp.where(order[...] == row, 1.0, 0.0).astype(BF16)
    earlier = jnp.where(row < col, 1.0, 0.0).astype(BF16)
    by_rank = product(routed.astype(BF16), served, 1, 0)
    before = product(by_rank.astype(BF16), earlier, 1, 0)
    taken = jnp.where(before.astype(jnp.int32) == slot % capacity, by_rank, 0.0).astype(BF16)
    pick = product(taken, served, 1, 1)
    turned_out[...] = product(served, taken, 1, 1).astype(BF16)
    slot_gate = jnp.sum(pick * gate, axis=1, keepdims=True)
    gate_out[...] = jnp.broadcast_to(slot_gate, gate_out.shape)
    pick = pick.astype(BF16)
    copies[3].wait()
    for k in reversed(range(parts)):
        value = product(pick, tok[:, columns(k, part)], 1, 0).astype(BF16)
        put_halves(rows_out, k // CORES, pl.ds((k % CORES) * part, part), value)
    copies[4].wait()
    for k in reversed(range(parts)):
        value = slot_gate * product(pick, cot[:, columns(k, part)], 1, 0)
        grads_out[k // CORES][:, pl.ds((k % CORES) * part, part)] = value.astype(BF16)


def put_halves(outs, kx, cols, value):
    half = value.shape[0] // 2
    if kx:
        outs[2 * kx - 1][:, cols] = value[half:]
        outs[2 * kx][:, cols] = value[:half]
    else:
        outs[0][:, cols] = value


def flip(chunks):
    return [chunks[0], *chunks[:0:-1]]


def join_kernel(groups, spread, capacity, first, *refs):
    by_x, chunks = refs[:spread], refs[spread:]
    half = by_x[0].shape[1]
    for i, chunk in enumerate(chunks):
        for kx in range(spread):
            at = (i if kx else i + first) * capacity
            chunk[:, kx * half : (kx + 1) * half] = by_x[kx][at : at + capacity]


def far_kernel(groups, spread, capacity, *refs):
    by_e, by_x = flip(refs[:groups]), refs[groups:]
    for ke in range(groups):
        for kx in range(1, spread):
            by_x[kx - 1][ke * capacity : (ke + 1) * capacity] = by_e[ke][
                kx * capacity : (kx + 1) * capacity
            ]


def partial(groups, spread, refs, outs):
    chunks, (own, sib) = flip(refs[:groups]), refs[groups:]
    part = own.shape[0]
    half = CORES * part
    rows = jnp.concatenate(
        [c[:, kx * half : (kx + 1) * half] for kx in range(spread) for c in chunks], axis=0
    )
    total = product(rows[:, :part], own[...], 1, 0) + product(rows[:, part:], sib[...], 1, 0)
    slots = rows.shape[0] // spread
    for kx in range(spread):
        outs[kx][...] = total[kx * slots : (kx + 1) * slots].astype(outs[kx].dtype)
    return rows


def pre_kernel(groups, spread, *refs):
    partial(groups, spread, refs[: groups + 2], refs[groups + 2 :])


def back_kernel(groups, spread, *refs):
    own, sib, *outs = refs[groups + 2 :]
    rows = partial(groups, spread, refs[: groups + 2], outs)
    part = own.shape[1]
    own[...] = rows[:, :part]
    sib[...] = rows[:, part:]


def summed(refs):
    total = refs[0][...]
    for ref in refs[1:]:
        total += ref[...].astype(F32)
    return total


def hidden_kernel(*refs):
    pre, out = summed(refs[:-1]), refs[-1]
    feed = out.shape[1]
    gate_act, up_act = pre[:, :feed], pre[:, feed:]
    out[...] = (gate_act * (1.0 / (1.0 + jnp.exp(-gate_act))) * up_act).astype(BF16)


def d_pre_kernel(*refs):
    spread = len(refs) // 2
    pre, back, out = summed(refs[:spread]), summed(refs[spread:-1]), refs[-1]
    feed = back.shape[1]
    gate_act, up_act = pre[:, :feed], pre[:, feed:]
    sig = 1.0 / (1.0 + jnp.exp(-gate_act))
    out[:, :feed] = (back * up_act * (sig * (1.0 + gate_act * (1.0 - sig)))).astype(BF16)
    out[:, feed:] = (back * (gate_act * sig)).astype(BF16)


def width_product(left, weights, store):
    rows = jnp.concatenate([r[...] for r in left], axis=0)
    for kc, weight in enumerate(weights):
        store(kc, product(rows, weight[...], 1, 1).astype(BF16))


def expert_out_kernel(groups, spread, capacity, *refs):
    chunks = refs[-groups:]
    part = refs[spread].shape[0]

    def store(kc, value):
        for ke in range(groups):
            for kx in range(spread):
                at = (kx * groups + ke) * capacity
                chunks[ke][kx * capacity : (kx + 1) * capacity, kc * part : (kc + 1) * part] = value[
                    at : at + capacity
                ]

    width_product(refs[:spread], refs[spread : spread + CORES], store)


def d_rows_kernel(spread, *refs):
    outs = refs[-spread:]
    part = refs[spread].shape[0]
    slots = outs[0].shape[0]

    def store(kc, value):
        for kx in range(spread):
            outs[kx][:, kc * part : (kc + 1) * part] = value[kx * slots : (kx + 1) * slots]

    width_product(refs[:spread], refs[spread : spread + CORES], store)


def weight_kernel(spread, own, sib, *refs):
    hidden, sib_hidden, out = refs[:spread], refs[spread:-1], refs[-1]
    left = jnp.concatenate([own[...], sib[...]], axis=0)
    right = jnp.concatenate([r[...] for r in (*hidden, *sib_hidden)], axis=0)
    out[...] = product(left, right, 0, 0)


def scatter(turned, groups_of_rows, out, held, sems):
    part = held.shape[2]
    copies = []
    for k, rows in enumerate(groups_of_rows):
        held[k] = product(turned, rows, 1, 0).astype(BF16)
        copies.append(pltpu.make_async_copy(held.at[k], out.at[:, columns(k, part)], sems.at[k]))
        copies[-1].start()
    for copy in copies:
        copy.wait()


def combine_kernel(groups, parts, capacity, turned, gate, *refs):
    chunks, far, (out, held, sems) = flip(refs[:groups]), refs[groups:-3], refs[-3:]
    part = held.shape[2]

    def weighted(k):
        cols = slice((k % CORES) * part, (k % CORES + 1) * part)
        if k < CORES:
            rows = jnp.concatenate([c[:capacity, cols] for c in chunks], axis=0)
        else:
            rows = far[k // CORES - 1][:, cols]
        rows = rows.astype(F32) * gate[:, :1]
        high = rows.astype(BF16)
        return jnp.concatenate([high, (rows - high.astype(F32)).astype(BF16)], axis=0)

    twice = jnp.concatenate([turned[...], turned[...]], axis=1)
    scatter(twice, map(weighted, range(parts)), out, held, sems)


def d_tokens_kernel(groups, parts, turned, *refs):
    chunks, (out, held, sems) = flip(refs[:groups]), refs[groups:]
    part = held.shape[2]
    rows = (
        jnp.concatenate([c[:, k * part : (k + 1) * part] for c in chunks], axis=0)
        for k in range(parts)
    )
    scatter(turned[...], rows, out, held, sems)


def per_device(tokens, cotangent, route_ids, route_gates, served_order, w_in, w_out):
    groups = lax.axis_size("expert")
    parts = lax.axis_size("fsdp")
    spread = parts // CORES
    count, width = tokens.shape
    capacity = count * route_ids.shape[1] // EXPERTS
    feed = w_out.shape[2]
    slots = groups * capacity
    half = width // spread
    part = width // parts

    def bound(kernel, *sizes):
        return lambda *refs: kernel(*sizes, *refs)

    def to_core(value):
        return lax.ppermute(value, "fsdp", [(i, i ^ 1) for i in range(parts)])

    def to_x(values):
        return [
            lax.ppermute(value, "fsdp", [(i, i ^ ((k + 1) * CORES)) for i in range(parts)])
            for k, value in enumerate(values)
        ]

    def to_expert(chunks):
        return [
            lax.ppermute(value, "expert", [(i, i ^ ke) for i in range(groups)]) if ke else value
            for ke, value in enumerate(chunks)
        ]

    chunk = [shape((capacity, width))] * groups
    by_x = [shape((slots, half))] * spread
    by_halves = [shape((slots, half))] + [shape((slots // 2, half))] * (2 * spread - 2)
    in_own, out_own = w_in[0], w_out[0]
    in_sib, out_sib = to_core(in_own), to_core(out_own)
    outs = call(
        bound(slot_kernel, spread),
        by_halves + by_x + [shape((count, slots)), shape((slots, 128), F32)],
        (route_ids.T, route_gates.T, served_order, tokens, cotangent),
        far=5,
        scratch_shapes=[
            pltpu.VMEM(route_ids.shape[::-1], jnp.int32),
            pltpu.VMEM(route_gates.shape[::-1], F32),
            pltpu.VMEM(served_order.shape, jnp.int32),
            pltpu.VMEM(tokens.shape, BF16),
            pltpu.VMEM(cotangent.shape, BF16),
            pltpu.SemaphoreType.DMA((5,)),
        ],
    )
    turned, gate = outs[-2:]
    near, *far = outs[: 2 * spread - 1]
    grads = outs[2 * spread - 1 : -2]

    near, in_sib, out_sib = lax.optimization_barrier((near, in_sib, out_sib))
    high, low = to_x(far[::2]), to_x(far[1::2])
    middle = groups // 2
    high = call(
        bound(join_kernel, groups, spread, capacity, middle),
        chunk[middle:],
        (near, *high),
        cost=JOIN_COST,
    )
    low = call(bound(join_kernel, groups, spread, capacity, 0), chunk[:middle], (near, *low))
    rows = to_expert([*low, *high])
    grads = [grads[0], *to_x(grads[1:])]
    join = bound(join_kernel, groups, spread, capacity, 0)
    grads = to_expert(call(join, chunk, grads))
    pre, *pre_far = call(
        bound(pre_kernel, groups, spread),
        [shape((slots, 2 * feed), F32)] + [shape((slots, 2 * feed))] * (spread - 1),
        (*flip(rows), in_own, in_sib),
        cost=PRE_COST,
    )
    pre = (pre, *to_x(pre_far))
    (hidden,) = call(hidden_kernel, [shape((slots, feed))], pre)
    hidden = (hidden, *to_x([hidden] * (spread - 1)))
    own_grads, sib_grads, back, *back_far = call(
        bound(back_kernel, groups, spread),
        [shape((spread * slots, part))] * 2
        + [shape((slots, feed), F32)]
        + [shape((slots, feed))] * (spread - 1),
        (*flip(grads), out_own, out_sib),
        cost=BACK_COST,
    )
    back = (back, *to_x(back_far))
    expert_out = to_expert(
        call(
            bound(expert_out_kernel, groups, spread, capacity),
            [shape((spread * capacity, half))] * groups,
            (*hidden, out_own, out_sib),
            cost=OUT_COST,
        )
    )
    (d_pre,) = call(
        d_pre_kernel, [shape((slots, 2 * feed))], (*pre, *back), after=hidden[:1]
    )
    d_pre = (d_pre, *to_x([d_pre] * (spread - 1)))
    near, *far = call(
        bound(d_rows_kernel, spread), by_x, (*d_pre, in_own, in_sib)
    )
    d_rows = to_expert(call(join, chunk, (near, *to_x(far))))
    far = to_x(
        call(bound(far_kernel, groups, spread, capacity), by_x[1:], flip(expert_out))
    )
    d_w_out, token = call(
        bound(weight_kernel, spread),
        [shape((part, feed), F32)],
        (own_grads, to_core(sib_grads), *hidden, *[to_core(value) for value in hidden]),
        token=True,
    )

    def scattered(kernel, operands, **kw):
        return call(
            kernel,
            [shape((count, width))],
            operands,
            out_specs=[pl.BlockSpec(memory_space=pltpu.HBM)]
            + [pl.BlockSpec(memory_space=pltpu.VMEM)] * kw.get("token", False),
            scratch_shapes=[
                pltpu.VMEM((parts, count, part), BF16),
                pltpu.SemaphoreType.DMA((parts,)),
            ],
            **kw,
        )

    combined, token = scattered(
        bound(combine_kernel, groups, parts, capacity),
        (turned, gate, *flip(expert_out), *far),
        after=(token,),
        token=True,
    )
    (d_tokens,) = scattered(
        bound(d_tokens_kernel, groups, parts), (turned, *flip(d_rows)), after=(token,)
    )
    return combined, d_tokens, d_w_out[None]


def solution(mesh):
    rows = P(("replica", "expert", "fsdp"), None)
    weights = P("expert", "fsdp", None)
    return jax.shard_map(
        per_device,
        mesh=mesh,
        in_specs=(rows,) * 5 + (weights,) * 2,
        out_specs=(rows, rows, P(("replica", "expert"), "fsdp", None)),
        check_vma=False,
    )
```

```python
import jax
import jax.numpy as jnp
from jax import lax
from jax.experimental import pallas as pl
from jax.experimental.pallas import tpu as pltpu
from jax.sharding import PartitionSpec as P

EXPERTS = 128
CORES = 2
OUT_COST = 2000000000
PRE_COST = 4500000000
JOIN_COST = 1000000000
BACK_COST = 3000000000
VMEM = 40 * 1024 * 1024
F32 = jnp.float32
BF16 = jnp.bfloat16


def product(left, right, left_dim, right_dim, **kw):
    return lax.dot_general(
        left, right, (((left_dim,), (right_dim,)), ((), ())), preferred_element_type=F32, **kw
    )


def call(body, out_shape, args, far=0, cost=0, after=(), token=False, **kw):
    out_shape = [*out_shape] + [shape((8, 128), F32)] * token
    specs = [pl.BlockSpec(memory_space=pltpu.VMEM)] * (len(args) - far)
    specs += [pl.BlockSpec(memory_space=pltpu.HBM)] * far
    specs += [pl.BlockSpec(memory_space=pl.ANY)] * len(after)
    kw.setdefault("out_specs", [pl.BlockSpec(memory_space=pltpu.VMEM)] * len(out_shape))
    args = [
        pltpu.with_memory_space_constraint(arg, pltpu.HBM) if i >= len(args) - far else arg
        for i, arg in enumerate(args)
    ]
    count, first, last = len(args), len(args) + len(after), len(args) + len(after) + len(out_shape)

    def kernel(*refs):
        if token:
            refs[last - 1][...] = jnp.zeros(refs[last - 1].shape, F32)
        body(*refs[:count], *refs[first : last - token], *refs[last:])

    return pl.pallas_call(
        kernel,
        out_shape=out_shape,
        in_specs=specs,
        compiler_params=pltpu.CompilerParams(vmem_limit_bytes=VMEM),
        cost_estimate=pl.CostEstimate(flops=cost, bytes_accessed=0, transcendentals=0),
        **kw,
    )(*args, *after)


def shape(dims, kind=BF16):
    return jax.ShapeDtypeStruct(dims, kind)


def columns(k, part):
    return pl.ds(pl.multiple_of((lax.axis_index("fsdp") ^ k) * part, part), part)


def slot_kernel(spread, *refs):
    sources, refs = refs[:5], refs[5:]
    rows_out, refs = refs[: 2 * spread - 1], refs[2 * spread - 1 :]
    grads_out, refs = refs[:spread], refs[spread:]
    turned_out, gate_out, ids, gates, order, tok, cot, sems = refs
    parts = spread * CORES
    copies = [
        pltpu.make_async_copy(source, target, sems.at[i])
        for i, (source, target) in enumerate(zip(sources, (ids, gates, order, tok, cot)))
    ]
    for copy in copies:
        copy.start()
    for copy in copies[:3]:
        copy.wait()
    choices, count = ids.shape
    slots = gate_out.shape[0]
    groups = lax.axis_size("expert")
    capacity = slots // groups
    part = tok.shape[1] // parts
    slot = lax.broadcasted_iota(jnp.int32, (slots, count), 0)
    wanted = ((slot // capacity) ^ lax.axis_index("expert")) * (EXPERTS // groups)
    routed = jnp.zeros((slots, count), F32)
    gate = jnp.zeros((slots, count), F32)
    for k in range(choices):
        hit = ids[k : k + 1, :] == wanted
        routed = jnp.where(hit, 1.0, routed)
        gate = jnp.where(hit, gates[k : k + 1, :], gate)
    row = lax.broadcasted_iota(jnp.int32, (count, count), 0)
    col = lax.broadcasted_iota(jnp.int32, (count, count), 1)
    served = jnp.where(order[...] == row, 1.0, 0.0).astype(BF16)
    earlier = jnp.where(row < col, 1.0, 0.0).astype(BF16)
    by_rank = product(routed.astype(BF16), served, 1, 0)
    before = product(by_rank.astype(BF16), earlier, 1, 0)
    taken = jnp.where(before.astype(jnp.int32) == slot % capacity, by_rank, 0.0).astype(BF16)
    pick = product(taken, served, 1, 1)
    turned_out[...] = product(served, taken, 1, 1).astype(BF16)
    slot_gate = jnp.sum(pick * gate, axis=1, keepdims=True)
    gate_out[...] = jnp.broadcast_to(slot_gate, gate_out.shape)
    pick = pick.astype(BF16)
    copies[3].wait()
    for k in reversed(range(parts)):
        value = product(pick, tok[:, columns(k, part)], 1, 0).astype(BF16)
        put_halves(rows_out, k // CORES, pl.ds((k % CORES) * part, part), value)
    copies[4].wait()
    for k in reversed(range(parts)):
        value = slot_gate * product(pick, cot[:, columns(k, part)], 1, 0)
        grads_out[k // CORES][:, pl.ds((k % CORES) * part, part)] = value.astype(BF16)


def put_halves(outs, kx, cols, value):
    half = value.shape[0] // 2
    if kx:
        outs[2 * kx - 1][:, cols] = value[half:]
        outs[2 * kx][:, cols] = value[:half]
    else:
        outs[0][:, cols] = value


def flip(chunks):
    return [chunks[0], *chunks[:0:-1]]


def join_kernel(groups, spread, capacity, first, *refs):
    by_x, chunks = refs[:spread], refs[spread:]
    half = by_x[0].shape[1]
    for i, chunk in enumerate(chunks):
        for kx in range(spread):
            at = (i if kx else i + first) * capacity
            chunk[:, kx * half : (kx + 1) * half] = by_x[kx][at : at + capacity]


def far_kernel(groups, spread, capacity, *refs):
    by_e, by_x = flip(refs[:groups]), refs[groups:]
    for ke in range(groups):
        for kx in range(1, spread):
            by_x[kx - 1][ke * capacity : (ke + 1) * capacity] = by_e[ke][
                kx * capacity : (kx + 1) * capacity
            ]


def partial(groups, spread, refs, outs):
    chunks, (own, sib) = flip(refs[:groups]), refs[groups:]
    part = own.shape[0]
    half = CORES * part
    rows = jnp.concatenate(
        [c[:, kx * half : (kx + 1) * half] for kx in range(spread) for c in chunks], axis=0
    )
    total = product(rows[:, :part], own[...], 1, 0) + product(rows[:, part:], sib[...], 1, 0)
    slots = rows.shape[0] // spread
    for kx in range(spread):
        outs[kx][...] = total[kx * slots : (kx + 1) * slots].astype(outs[kx].dtype)
    return rows


def pre_kernel(groups, spread, *refs):
    partial(groups, spread, refs[: groups + 2], refs[groups + 2 :])


def back_kernel(groups, spread, *refs):
    own, sib, *outs = refs[groups + 2 :]
    rows = partial(groups, spread, refs[: groups + 2], outs)
    part = own.shape[1]
    own[...] = rows[:, :part]
    sib[...] = rows[:, part:]


def summed(refs):
    total = refs[0][...]
    for ref in refs[1:]:
        total += ref[...].astype(F32)
    return total


def hidden_kernel(*refs):
    pre, out = summed(refs[:-1]), refs[-1]
    feed = out.shape[1]
    gate_act, up_act = pre[:, :feed], pre[:, feed:]
    out[...] = (gate_act * (1.0 / (1.0 + jnp.exp(-gate_act))) * up_act).astype(BF16)


def d_pre_kernel(*refs):
    spread = len(refs) // 2
    pre, back, out = summed(refs[:spread]), summed(refs[spread:-1]), refs[-1]
    feed = back.shape[1]
    gate_act, up_act = pre[:, :feed], pre[:, feed:]
    sig = 1.0 / (1.0 + jnp.exp(-gate_act))
    out[:, :feed] = (back * up_act * (sig * (1.0 + gate_act * (1.0 - sig)))).astype(BF16)
    out[:, feed:] = (back * (gate_act * sig)).astype(BF16)


def width_product(left, weights, store):
    rows = jnp.concatenate([r[...] for r in left], axis=0)
    for kc, weight in enumerate(weights):
        store(kc, product(rows, weight[...], 1, 1).astype(BF16))


def expert_out_kernel(groups, spread, capacity, *refs):
    chunks = refs[-groups:]
    part = refs[spread].shape[0]

    def store(kc, value):
        for ke in range(groups):
            for kx in range(spread):
                at = (kx * groups + ke) * capacity
                chunks[ke][kx * capacity : (kx + 1) * capacity, kc * part : (kc + 1) * part] = value[
                    at : at + capacity
                ]

    width_product(refs[:spread], refs[spread : spread + CORES], store)


def d_rows_kernel(spread, *refs):
    outs = refs[-spread:]
    part = refs[spread].shape[0]
    slots = outs[0].shape[0]

    def store(kc, value):
        for kx in range(spread):
            outs[kx][:, kc * part : (kc + 1) * part] = value[kx * slots : (kx + 1) * slots]

    width_product(refs[:spread], refs[spread : spread + CORES], store)


def weight_kernel(spread, own, sib, *refs):
    hidden, sib_hidden, out = refs[:spread], refs[spread:-1], refs[-1]
    left = jnp.concatenate([own[...], sib[...]], axis=0)
    right = jnp.concatenate([r[...] for r in (*hidden, *sib_hidden)], axis=0)
    out[...] = product(left, right, 0, 0)


def scatter(turned, groups_of_rows, out, held, sems):
    part = held.shape[2]
    copies = []
    for k, rows in enumerate(groups_of_rows):
        held[k] = product(turned, rows, 1, 0).astype(BF16)
        copies.append(pltpu.make_async_copy(held.at[k], out.at[:, columns(k, part)], sems.at[k]))
        copies[-1].start()
    for copy in copies:
        copy.wait()


def combine_kernel(groups, parts, capacity, turned, gate, *refs):
    chunks, far, (out, held, sems) = flip(refs[:groups]), refs[groups:-3], refs[-3:]
    part = held.shape[2]

    def weighted(k):
        cols = slice((k % CORES) * part, (k % CORES + 1) * part)
        if k < CORES:
            rows = jnp.concatenate([c[:capacity, cols] for c in chunks], axis=0)
        else:
            rows = far[k // CORES - 1][:, cols]
        rows = rows.astype(F32) * gate[:, :1]
        high = rows.astype(BF16)
        return jnp.concatenate([high, (rows - high.astype(F32)).astype(BF16)], axis=0)

    twice = jnp.concatenate([turned[...], turned[...]], axis=1)
    scatter(twice, map(weighted, range(parts)), out, held, sems)


def d_tokens_kernel(groups, parts, turned, *refs):
    chunks, (out, held, sems) = flip(refs[:groups]), refs[groups:]
    part = held.shape[2]
    rows = (
        jnp.concatenate([c[:, k * part : (k + 1) * part] for c in chunks], axis=0)
        for k in range(parts)
    )
    scatter(turned[...], rows, out, held, sems)


def per_device(tokens, cotangent, route_ids, route_gates, served_order, w_in, w_out):
    groups = lax.axis_size("expert")
    parts = lax.axis_size("fsdp")
    spread = parts // CORES
    count, width = tokens.shape
    capacity = count * route_ids.shape[1] // EXPERTS
    feed = w_out.shape[2]
    slots = groups * capacity
    half = width // spread
    part = width // parts

    def bound(kernel, *sizes):
        return lambda *refs: kernel(*sizes, *refs)

    def to_core(value):
        return lax.ppermute(value, "fsdp", [(i, i ^ 1) for i in range(parts)])

    def to_x(values):
        return [
            lax.ppermute(value, "fsdp", [(i, i ^ ((k + 1) * CORES)) for i in range(parts)])
            for k, value in enumerate(values)
        ]

    def to_expert(chunks):
        return [
            lax.ppermute(value, "expert", [(i, i ^ ke) for i in range(groups)]) if ke else value
            for ke, value in enumerate(chunks)
        ]

    chunk = [shape((capacity, width))] * groups
    by_x = [shape((slots, half))] * spread
    by_halves = [shape((slots, half))] + [shape((slots // 2, half))] * (2 * spread - 2)
    in_own, out_own = w_in[0], w_out[0]
    in_sib, out_sib = to_core(in_own), to_core(out_own)
    outs = call(
        bound(slot_kernel, spread),
        by_halves + by_x + [shape((count, slots)), shape((slots, 128), F32)],
        (route_ids.T, route_gates.T, served_order, tokens, cotangent),
        far=5,
        scratch_shapes=[
            pltpu.VMEM(route_ids.shape[::-1], jnp.int32),
            pltpu.VMEM(route_gates.shape[::-1], F32),
            pltpu.VMEM(served_order.shape, jnp.int32),
            pltpu.VMEM(tokens.shape, BF16),
            pltpu.VMEM(cotangent.shape, BF16),
            pltpu.SemaphoreType.DMA((5,)),
        ],
    )
    turned, gate = outs[-2:]
    near, *far = outs[: 2 * spread - 1]
    grads = outs[2 * spread - 1 : -2]

    near, in_sib, out_sib = lax.optimization_barrier((near, in_sib, out_sib))
    high, low = to_x(far[::2]), to_x(far[1::2])
    middle = groups // 2
    high = call(
        bound(join_kernel, groups, spread, capacity, middle),
        chunk[middle:],
        (near, *high),
        cost=JOIN_COST,
    )
    low = call(bound(join_kernel, groups, spread, capacity, 0), chunk[:middle], (near, *low))
    rows = to_expert([*low, *high])
    grads = [grads[0], *to_x(grads[1:])]
    join = bound(join_kernel, groups, spread, capacity, 0)
    grads = to_expert(call(join, chunk, grads))
    pre, *pre_far = call(
        bound(pre_kernel, groups, spread),
        [shape((slots, 2 * feed), F32)] + [shape((slots, 2 * feed))] * (spread - 1),
        (*flip(rows), in_own, in_sib),
        cost=PRE_COST,
    )
    pre = (pre, *to_x(pre_far))
    (hidden,) = call(hidden_kernel, [shape((slots, feed))], pre)
    hidden = (hidden, *to_x([hidden] * (spread - 1)))
    own_grads, sib_grads, back, *back_far = call(
        bound(back_kernel, groups, spread),
        [shape((spread * slots, part))] * 2
        + [shape((slots, feed), F32)]
        + [shape((slots, feed))] * (spread - 1),
        (*flip(grads), out_own, out_sib),
        cost=BACK_COST,
    )
    back = (back, *to_x(back_far))
    expert_out = to_expert(
        call(
            bound(expert_out_kernel, groups, spread, capacity),
            [shape((spread * capacity, half))] * groups,
            (*hidden, out_own, out_sib),
            cost=OUT_COST,
        )
    )
    (d_pre,) = call(
        d_pre_kernel, [shape((slots, 2 * feed))], (*pre, *back), after=hidden[:1]
    )
    d_pre = (d_pre, *to_x([d_pre] * (spread - 1)))
    near, *far = call(
        bound(d_rows_kernel, spread), by_x, (*d_pre, in_own, in_sib)
    )
    d_w_out, token = call(
        bound(weight_kernel, spread),
        [shape((part, feed), F32)],
        (own_grads, to_core(sib_grads), *hidden, *[to_core(value) for value in hidden]),
        token=True,
    )

    d_rows = to_expert(call(join, chunk, (near, *to_x(far)), after=(token,)))
    far = to_x(
        call(bound(far_kernel, groups, spread, capacity), by_x[1:], flip(expert_out))
    )
    def scattered(kernel, operands, **kw):
        return call(
            kernel,
            [shape((count, width))],
            operands,
            out_specs=[pl.BlockSpec(memory_space=pltpu.HBM)]
            + [pl.BlockSpec(memory_space=pltpu.VMEM)] * kw.get("token", False),
            scratch_shapes=[
                pltpu.VMEM((parts, count, part), BF16),
                pltpu.SemaphoreType.DMA((parts,)),
            ],
            **kw,
        )

    combined, token = scattered(
        bound(combine_kernel, groups, parts, capacity),
        (turned, gate, *flip(expert_out), *far),
        token=True,
    )
    (d_tokens,) = scattered(
        bound(d_tokens_kernel, groups, parts), (turned, *flip(d_rows)), after=(token,)
    )
    return combined, d_tokens, d_w_out[None]


def solution(mesh):
    rows = P(("replica", "expert", "fsdp"), None)
    weights = P("expert", "fsdp", None)
    return jax.shard_map(
        per_device,
        mesh=mesh,
        in_specs=(rows,) * 5 + (weights,) * 2,
        out_specs=(rows, rows, P(("replica", "expert"), "fsdp", None)),
        check_vma=False,
    )
```

```python
import jax
import jax.numpy as jnp
from jax import lax
from jax.experimental import pallas as pl
from jax.experimental.pallas import tpu as pltpu
from jax.sharding import PartitionSpec as P

EXPERTS = 128
CORES = 2
OUT_COST = 2000000000
PRE_COST = 4500000000
JOIN_COST = 1000000000
BACK_COST = 3000000000
VMEM = 40 * 1024 * 1024
F32 = jnp.float32
BF16 = jnp.bfloat16


def product(left, right, left_dim, right_dim, **kw):
    return lax.dot_general(
        left, right, (((left_dim,), (right_dim,)), ((), ())), preferred_element_type=F32, **kw
    )


def call(body, out_shape, args, far=0, cost=0, after=(), token=False, **kw):
    out_shape = [*out_shape] + [shape((8, 128), F32)] * token
    specs = [pl.BlockSpec(memory_space=pltpu.VMEM)] * (len(args) - far)
    specs += [pl.BlockSpec(memory_space=pltpu.HBM)] * far
    specs += [pl.BlockSpec(memory_space=pl.ANY)] * len(after)
    kw.setdefault("out_specs", [pl.BlockSpec(memory_space=pltpu.VMEM)] * len(out_shape))
    args = [
        pltpu.with_memory_space_constraint(arg, pltpu.HBM) if i >= len(args) - far else arg
        for i, arg in enumerate(args)
    ]
    count, first, last = len(args), len(args) + len(after), len(args) + len(after) + len(out_shape)

    def kernel(*refs):
        if token:
            refs[last - 1][...] = jnp.zeros(refs[last - 1].shape, F32)
        body(*refs[:count], *refs[first : last - token], *refs[last:])

    return pl.pallas_call(
        kernel,
        out_shape=out_shape,
        in_specs=specs,
        compiler_params=pltpu.CompilerParams(vmem_limit_bytes=VMEM),
        cost_estimate=pl.CostEstimate(flops=cost, bytes_accessed=0, transcendentals=0),
        **kw,
    )(*args, *after)


def shape(dims, kind=BF16):
    return jax.ShapeDtypeStruct(dims, kind)


def columns(k, part):
    return pl.ds(pl.multiple_of((lax.axis_index("fsdp") ^ k) * part, part), part)


def slot_kernel(spread, *refs):
    sources, refs = refs[:5], refs[5:]
    rows_out, refs = refs[: 2 * spread - 1], refs[2 * spread - 1 :]
    grads_out, refs = refs[:spread], refs[spread:]
    turned_out, gate_out, ids, gates, order, tok, cot, sems = refs
    parts = spread * CORES
    copies = [
        pltpu.make_async_copy(source, target, sems.at[i])
        for i, (source, target) in enumerate(zip(sources, (ids, gates, order, tok, cot)))
    ]
    for copy in copies:
        copy.start()
    for copy in copies[:3]:
        copy.wait()
    choices, count = ids.shape
    slots = gate_out.shape[0]
    groups = lax.axis_size("expert")
    capacity = slots // groups
    part = tok.shape[1] // parts
    slot = lax.broadcasted_iota(jnp.int32, (slots, count), 0)
    wanted = ((slot // capacity) ^ lax.axis_index("expert")) * (EXPERTS // groups)
    routed = jnp.zeros((slots, count), F32)
    gate = jnp.zeros((slots, count), F32)
    for k in range(choices):
        hit = ids[k : k + 1, :] == wanted
        routed = jnp.where(hit, 1.0, routed)
        gate = jnp.where(hit, gates[k : k + 1, :], gate)
    row = lax.broadcasted_iota(jnp.int32, (count, count), 0)
    col = lax.broadcasted_iota(jnp.int32, (count, count), 1)
    served = jnp.where(order[...] == row, 1.0, 0.0).astype(BF16)
    earlier = jnp.where(row < col, 1.0, 0.0).astype(BF16)
    by_rank = product(routed.astype(BF16), served, 1, 0)
    before = product(by_rank.astype(BF16), earlier, 1, 0)
    taken = jnp.where(before.astype(jnp.int32) == slot % capacity, by_rank, 0.0).astype(BF16)
    pick = product(taken, served, 1, 1)
    turned_out[...] = product(served, taken, 1, 1).astype(BF16)
    slot_gate = jnp.sum(pick * gate, axis=1, keepdims=True)
    gate_out[...] = jnp.broadcast_to(slot_gate, gate_out.shape)
    pick = pick.astype(BF16)
    copies[3].wait()
    for k in reversed(range(parts)):
        value = product(pick, tok[:, columns(k, part)], 1, 0).astype(BF16)
        put_halves(rows_out, k // CORES, pl.ds((k % CORES) * part, part), value)
    copies[4].wait()
    for k in reversed(range(parts)):
        value = slot_gate * product(pick, cot[:, columns(k, part)], 1, 0)
        grads_out[k // CORES][:, pl.ds((k % CORES) * part, part)] = value.astype(BF16)


def put_halves(outs, kx, cols, value):
    half = value.shape[0] // 2
    if kx:
        outs[2 * kx - 1][:, cols] = value[half:]
        outs[2 * kx][:, cols] = value[:half]
    else:
        outs[0][:, cols] = value


def farthest_first(groups):
    return [groups - 1, *range(1, groups - 1)]


def far_half_first(groups):
    return [*range(groups // 2, groups), *range(1, groups // 2)]


def arrange(chunks, order):
    return [chunks[0], *[chunks[ke] for ke in order(len(chunks))]]


def restore(chunks, order):
    out = list(chunks)
    for i, ke in enumerate(order(len(chunks))):
        out[ke] = chunks[i + 1]
    return out


def join_kernel(groups, spread, capacity, first, *refs):
    by_x, chunks = refs[:spread], refs[spread:]
    half = by_x[0].shape[1]
    for i, chunk in enumerate(chunks):
        for kx in range(spread):
            at = (i if kx else i + first) * capacity
            chunk[:, kx * half : (kx + 1) * half] = by_x[kx][at : at + capacity]


def far_kernel(groups, spread, capacity, *refs):
    by_e, by_x = restore(refs[:groups], far_half_first), refs[groups:]
    for ke in range(groups):
        for kx in range(1, spread):
            by_x[kx - 1][ke * capacity : (ke + 1) * capacity] = by_e[ke][
                kx * capacity : (kx + 1) * capacity
            ]


def partial(groups, spread, refs, outs):
    chunks, (own, sib) = restore(refs[:groups], farthest_first), refs[groups:]
    part = own.shape[0]
    half = CORES * part
    rows = jnp.concatenate(
        [c[:, kx * half : (kx + 1) * half] for kx in range(spread) for c in chunks], axis=0
    )
    total = product(rows[:, :part], own[...], 1, 0) + product(rows[:, part:], sib[...], 1, 0)
    slots = rows.shape[0] // spread
    for kx in range(spread):
        outs[kx][...] = total[kx * slots : (kx + 1) * slots].astype(outs[kx].dtype)
    return rows


def pre_kernel(groups, spread, *refs):
    partial(groups, spread, refs[: groups + 2], refs[groups + 2 :])


def back_kernel(groups, spread, *refs):
    own, sib, *outs = refs[groups + 2 :]
    rows = partial(groups, spread, refs[: groups + 2], outs)
    part = own.shape[1]
    own[...] = rows[:, :part]
    sib[...] = rows[:, part:]


def summed(refs):
    total = refs[0][...]
    for ref in refs[1:]:
        total += ref[...].astype(F32)
    return total


def hidden_kernel(*refs):
    pre, out = summed(refs[:-1]), refs[-1]
    feed = out.shape[1]
    gate_act, up_act = pre[:, :feed], pre[:, feed:]
    out[...] = (gate_act * (1.0 / (1.0 + jnp.exp(-gate_act))) * up_act).astype(BF16)


def d_pre_kernel(*refs):
    spread = len(refs) // 2
    pre, back, out = summed(refs[:spread]), summed(refs[spread:-1]), refs[-1]
    feed = back.shape[1]
    gate_act, up_act = pre[:, :feed], pre[:, feed:]
    sig = 1.0 / (1.0 + jnp.exp(-gate_act))
    out[:, :feed] = (back * up_act * (sig * (1.0 + gate_act * (1.0 - sig)))).astype(BF16)
    out[:, feed:] = (back * (gate_act * sig)).astype(BF16)


def width_product(left, weights, store):
    rows = jnp.concatenate([r[...] for r in left], axis=0)
    for kc, weight in enumerate(weights):
        store(kc, product(rows, weight[...], 1, 1).astype(BF16))


def expert_out_kernel(groups, spread, capacity, *refs):
    chunks = refs[-groups:]
    part = refs[spread].shape[0]

    def store(kc, value):
        for ke in range(groups):
            for kx in range(spread):
                at = (kx * groups + ke) * capacity
                chunks[ke][kx * capacity : (kx + 1) * capacity, kc * part : (kc + 1) * part] = value[
                    at : at + capacity
                ]

    width_product(refs[:spread], refs[spread : spread + CORES], store)


def d_rows_kernel(spread, *refs):
    outs = refs[-spread:]
    part = refs[spread].shape[0]
    slots = outs[0].shape[0]

    def store(kc, value):
        for kx in range(spread):
            outs[kx][:, kc * part : (kc + 1) * part] = value[kx * slots : (kx + 1) * slots]

    width_product(refs[:spread], refs[spread : spread + CORES], store)


def weight_kernel(spread, own, sib, *refs):
    hidden, sib_hidden, out = refs[:spread], refs[spread:-1], refs[-1]
    left = jnp.concatenate([own[...], sib[...]], axis=0)
    right = jnp.concatenate([r[...] for r in (*hidden, *sib_hidden)], axis=0)
    out[...] = product(left, right, 0, 0)


def scatter(turned, groups_of_rows, out, held, sems):
    part = held.shape[2]
    copies = []
    for k, rows in enumerate(groups_of_rows):
        held[k] = product(turned, rows, 1, 0).astype(BF16)
        copies.append(pltpu.make_async_copy(held.at[k], out.at[:, columns(k, part)], sems.at[k]))
        copies[-1].start()
    for copy in copies:
        copy.wait()


def combine_kernel(groups, parts, capacity, turned, gate, *refs):
    chunks, far, (out, held, sems) = refs[:groups], refs[groups:-3], refs[-3:]
    chunks = restore(chunks, far_half_first)
    part = held.shape[2]

    def weighted(k):
        cols = slice((k % CORES) * part, (k % CORES + 1) * part)
        if k < CORES:
            rows = jnp.concatenate([c[:capacity, cols] for c in chunks], axis=0)
        else:
            rows = far[k // CORES - 1][:, cols]
        rows = rows.astype(F32) * gate[:, :1]
        high = rows.astype(BF16)
        return jnp.concatenate([high, (rows - high.astype(F32)).astype(BF16)], axis=0)

    twice = jnp.concatenate([turned[...], turned[...]], axis=1)
    scatter(twice, map(weighted, range(parts)), out, held, sems)


def d_tokens_kernel(groups, parts, turned, *refs):
    chunks, (out, held, sems) = restore(refs[:groups], far_half_first), refs[groups:]
    part = held.shape[2]
    rows = (
        jnp.concatenate([c[:, k * part : (k + 1) * part] for c in chunks], axis=0)
        for k in range(parts)
    )
    scatter(turned[...], rows, out, held, sems)


def per_device(tokens, cotangent, route_ids, route_gates, served_order, w_in, w_out):
    groups = lax.axis_size("expert")
    parts = lax.axis_size("fsdp")
    spread = parts // CORES
    count, width = tokens.shape
    capacity = count * route_ids.shape[1] // EXPERTS
    feed = w_out.shape[2]
    slots = groups * capacity
    half = width // spread
    part = width // parts

    def bound(kernel, *sizes):
        return lambda *refs: kernel(*sizes, *refs)

    def to_core(value):
        return lax.ppermute(value, "fsdp", [(i, i ^ 1) for i in range(parts)])

    def to_x(values):
        return [
            lax.ppermute(value, "fsdp", [(i, i ^ ((k + 1) * CORES)) for i in range(parts)])
            for k, value in enumerate(values)
        ]

    def to_expert(chunks):
        return [
            lax.ppermute(value, "expert", [(i, i ^ ke) for i in range(groups)]) if ke else value
            for ke, value in enumerate(chunks)
        ]

    chunk = [shape((capacity, width))] * groups
    by_x = [shape((slots, half))] * spread
    by_halves = [shape((slots, half))] + [shape((slots // 2, half))] * (2 * spread - 2)
    in_own, out_own = w_in[0], w_out[0]
    in_sib, out_sib = to_core(in_own), to_core(out_own)
    outs = call(
        bound(slot_kernel, spread),
        by_halves + by_x + [shape((count, slots)), shape((slots, 128), F32)],
        (route_ids.T, route_gates.T, served_order, tokens, cotangent),
        far=5,
        scratch_shapes=[
            pltpu.VMEM(route_ids.shape[::-1], jnp.int32),
            pltpu.VMEM(route_gates.shape[::-1], F32),
            pltpu.VMEM(served_order.shape, jnp.int32),
            pltpu.VMEM(tokens.shape, BF16),
            pltpu.VMEM(cotangent.shape, BF16),
            pltpu.SemaphoreType.DMA((5,)),
        ],
    )
    turned, gate = outs[-2:]
    near, *far = outs[: 2 * spread - 1]
    grads = outs[2 * spread - 1 : -2]

    near, in_sib, out_sib = lax.optimization_barrier((near, in_sib, out_sib))
    high, low = to_x(far[::2]), to_x(far[1::2])
    middle = groups // 2
    high = call(
        bound(join_kernel, groups, spread, capacity, middle),
        chunk[middle:],
        (near, *high),
        cost=JOIN_COST,
    )
    low = call(bound(join_kernel, groups, spread, capacity, 0), chunk[:middle], (near, *low))
    rows = to_expert([*low, *high])
    grads = [grads[0], *to_x(grads[1:])]
    join = bound(join_kernel, groups, spread, capacity, 0)
    grads = to_expert(call(join, chunk, grads))
    pre, *pre_far = call(
        bound(pre_kernel, groups, spread),
        [shape((slots, 2 * feed), F32)] + [shape((slots, 2 * feed))] * (spread - 1),
        (*arrange(rows, farthest_first), in_own, in_sib),
        cost=PRE_COST,
    )
    pre = (pre, *to_x(pre_far))
    (hidden,) = call(hidden_kernel, [shape((slots, feed))], pre)
    hidden = (hidden, *to_x([hidden] * (spread - 1)))
    own_grads, sib_grads, back, *back_far = call(
        bound(back_kernel, groups, spread),
        [shape((spread * slots, part))] * 2
        + [shape((slots, feed), F32)]
        + [shape((slots, feed))] * (spread - 1),
        (*arrange(grads, farthest_first), out_own, out_sib),
        cost=BACK_COST,
    )
    back = (back, *to_x(back_far))
    expert_out = to_expert(
        call(
            bound(expert_out_kernel, groups, spread, capacity),
            [shape((spread * capacity, half))] * groups,
            (*hidden, out_own, out_sib),
            cost=OUT_COST,
        )
    )
    (d_pre,) = call(
        d_pre_kernel, [shape((slots, 2 * feed))], (*pre, *back), after=hidden[:1]
    )
    d_pre = (d_pre, *to_x([d_pre] * (spread - 1)))
    near, *far = call(
        bound(d_rows_kernel, spread), by_x, (*d_pre, in_own, in_sib)
    )
    d_rows = to_expert(call(join, chunk, (near, *to_x(far))))
    far = to_x(
        call(bound(far_kernel, groups, spread, capacity), by_x[1:], arrange(expert_out, far_half_first))
    )
    d_w_out, token = call(
        bound(weight_kernel, spread),
        [shape((part, feed), F32)],
        (own_grads, to_core(sib_grads), *hidden, *[to_core(value) for value in hidden]),
        token=True,
    )

    def scattered(kernel, operands, **kw):
        return call(
            kernel,
            [shape((count, width))],
            operands,
            out_specs=[pl.BlockSpec(memory_space=pltpu.HBM)]
            + [pl.BlockSpec(memory_space=pltpu.VMEM)] * kw.get("token", False),
            scratch_shapes=[
                pltpu.VMEM((parts, count, part), BF16),
                pltpu.SemaphoreType.DMA((parts,)),
            ],
            **kw,
        )

    combined, token = scattered(
        bound(combine_kernel, groups, parts, capacity),
        (turned, gate, *arrange(expert_out, far_half_first), *far),
        after=(token,),
        token=True,
    )
    (d_tokens,) = scattered(
        bound(d_tokens_kernel, groups, parts), (turned, *arrange(d_rows, far_half_first)), after=(token,)
    )
    return combined, d_tokens, d_w_out[None]


def solution(mesh):
    rows = P(("replica", "expert", "fsdp"), None)
    weights = P("expert", "fsdp", None)
    return jax.shard_map(
        per_device,
        mesh=mesh,
        in_specs=(rows,) * 5 + (weights,) * 2,
        out_specs=(rows, rows, P(("replica", "expert"), "fsdp", None)),
        check_vma=False,
    )
```

```python
import jax
import jax.numpy as jnp
from jax import lax
from jax.experimental import pallas as pl
from jax.experimental.pallas import tpu as pltpu
from jax.sharding import PartitionSpec as P

EXPERTS = 128
CORES = 2
OUT_COST = 2000000000
PRE_COST = 4500000000
JOIN_COST = 1000000000
BACK_COST = 3000000000
VMEM = 40 * 1024 * 1024
F32 = jnp.float32
BF16 = jnp.bfloat16


def product(left, right, left_dim, right_dim, **kw):
    return lax.dot_general(
        left, right, (((left_dim,), (right_dim,)), ((), ())), preferred_element_type=F32, **kw
    )


def call(body, out_shape, args, far=0, cost=0, after=(), token=False, **kw):
    out_shape = [*out_shape] + [shape((8, 128), F32)] * token
    specs = [pl.BlockSpec(memory_space=pltpu.VMEM)] * (len(args) - far)
    specs += [pl.BlockSpec(memory_space=pltpu.HBM)] * far
    specs += [pl.BlockSpec(memory_space=pl.ANY)] * len(after)
    kw.setdefault("out_specs", [pl.BlockSpec(memory_space=pltpu.VMEM)] * len(out_shape))
    args = [
        pltpu.with_memory_space_constraint(arg, pltpu.HBM) if i >= len(args) - far else arg
        for i, arg in enumerate(args)
    ]
    count, first, last = len(args), len(args) + len(after), len(args) + len(after) + len(out_shape)

    def kernel(*refs):
        if token:
            refs[last - 1][...] = jnp.zeros(refs[last - 1].shape, F32)
        body(*refs[:count], *refs[first : last - token], *refs[last:])

    return pl.pallas_call(
        kernel,
        out_shape=out_shape,
        in_specs=specs,
        compiler_params=pltpu.CompilerParams(vmem_limit_bytes=VMEM),
        cost_estimate=pl.CostEstimate(flops=cost, bytes_accessed=0, transcendentals=0),
        **kw,
    )(*args, *after)


def shape(dims, kind=BF16):
    return jax.ShapeDtypeStruct(dims, kind)


def columns(k, part):
    return pl.ds(pl.multiple_of((lax.axis_index("fsdp") ^ k) * part, part), part)


def slot_kernel(spread, *refs):
    sources, refs = refs[:5], refs[5:]
    rows_out, refs = refs[: 2 * spread - 1], refs[2 * spread - 1 :]
    grads_out, refs = refs[:spread], refs[spread:]
    turned_out, gate_out, ids, gates, order, tok, cot, sems = refs
    parts = spread * CORES
    copies = [
        pltpu.make_async_copy(source, target, sems.at[i])
        for i, (source, target) in enumerate(zip(sources, (ids, gates, order, tok, cot)))
    ]
    for copy in copies:
        copy.start()
    for copy in copies[:3]:
        copy.wait()
    choices, count = ids.shape
    slots = gate_out.shape[0]
    groups = lax.axis_size("expert")
    capacity = slots // groups
    part = tok.shape[1] // parts
    slot = lax.broadcasted_iota(jnp.int32, (slots, count), 0)
    wanted = ((slot // capacity) ^ lax.axis_index("expert")) * (EXPERTS // groups)
    routed = jnp.zeros((slots, count), F32)
    gate = jnp.zeros((slots, count), F32)
    for k in range(choices):
        hit = ids[k : k + 1, :] == wanted
        routed = jnp.where(hit, 1.0, routed)
        gate = jnp.where(hit, gates[k : k + 1, :], gate)
    row = lax.broadcasted_iota(jnp.int32, (count, count), 0)
    col = lax.broadcasted_iota(jnp.int32, (count, count), 1)
    served = jnp.where(order[...] == row, 1.0, 0.0).astype(BF16)
    earlier = jnp.where(row < col, 1.0, 0.0).astype(BF16)
    by_rank = product(routed.astype(BF16), served, 1, 0)
    before = product(by_rank.astype(BF16), earlier, 1, 0)
    taken = jnp.where(before.astype(jnp.int32) == slot % capacity, by_rank, 0.0).astype(BF16)
    pick = product(taken, served, 1, 1)
    turned_out[...] = product(served, taken, 1, 1).astype(BF16)
    slot_gate = jnp.sum(pick * gate, axis=1, keepdims=True)
    gate_out[...] = jnp.broadcast_to(slot_gate, gate_out.shape)
    pick = pick.astype(BF16)
    copies[3].wait()
    for k in reversed(range(parts)):
        value = product(pick, tok[:, columns(k, part)], 1, 0).astype(BF16)
        put_halves(rows_out, k // CORES, pl.ds((k % CORES) * part, part), value)
    copies[4].wait()
    for k in reversed(range(parts)):
        value = slot_gate * product(pick, cot[:, columns(k, part)], 1, 0)
        grads_out[k // CORES][:, pl.ds((k % CORES) * part, part)] = value.astype(BF16)


def put_halves(outs, kx, cols, value):
    half = value.shape[0] // 2
    if kx:
        outs[2 * kx - 1][:, cols] = value[half:]
        outs[2 * kx][:, cols] = value[:half]
    else:
        outs[0][:, cols] = value


def farthest_first(groups):
    return [*range(groups - 1, 0, -1)]


def nearest_first(groups):
    return [*range(1, groups)]


def far_half_first(groups):
    return [*range(groups // 2, groups), *range(1, groups // 2)]


def arrange(chunks, order):
    return [chunks[0], *[chunks[ke] for ke in order(len(chunks))]]


def restore(chunks, order):
    out = list(chunks)
    for i, ke in enumerate(order(len(chunks))):
        out[ke] = chunks[i + 1]
    return out


def join_kernel(groups, spread, capacity, first, *refs):
    by_x, chunks = refs[:spread], refs[spread:]
    half = by_x[0].shape[1]
    for i, chunk in enumerate(chunks):
        for kx in range(spread):
            at = (i if kx else i + first) * capacity
            chunk[:, kx * half : (kx + 1) * half] = by_x[kx][at : at + capacity]


def far_kernel(groups, spread, capacity, *refs):
    by_e, by_x = restore(refs[:groups], far_half_first), refs[groups:]
    for ke in range(groups):
        for kx in range(1, spread):
            by_x[kx - 1][ke * capacity : (ke + 1) * capacity] = by_e[ke][
                kx * capacity : (kx + 1) * capacity
            ]


def partial(groups, spread, refs, outs, order):
    chunks, (own, sib) = restore(refs[:groups], order), refs[groups:]
    part = own.shape[0]
    half = CORES * part
    rows = jnp.concatenate(
        [c[:, kx * half : (kx + 1) * half] for kx in range(spread) for c in chunks], axis=0
    )
    total = product(rows[:, :part], own[...], 1, 0) + product(rows[:, part:], sib[...], 1, 0)
    slots = rows.shape[0] // spread
    for kx in range(spread):
        outs[kx][...] = total[kx * slots : (kx + 1) * slots].astype(outs[kx].dtype)
    return rows


def pre_kernel(groups, spread, *refs):
    partial(groups, spread, refs[: groups + 2], refs[groups + 2 :], farthest_first)


def back_kernel(groups, spread, *refs):
    own, sib, *outs = refs[groups + 2 :]
    rows = partial(groups, spread, refs[: groups + 2], outs, nearest_first)
    part = own.shape[1]
    own[...] = rows[:, :part]
    sib[...] = rows[:, part:]


def summed(refs):
    total = refs[0][...]
    for ref in refs[1:]:
        total += ref[...].astype(F32)
    return total


def hidden_kernel(*refs):
    pre, out = summed(refs[:-1]), refs[-1]
    feed = out.shape[1]
    gate_act, up_act = pre[:, :feed], pre[:, feed:]
    out[...] = (gate_act * (1.0 / (1.0 + jnp.exp(-gate_act))) * up_act).astype(BF16)


def d_pre_kernel(*refs):
    spread = len(refs) // 2
    pre, back, out = summed(refs[:spread]), summed(refs[spread:-1]), refs[-1]
    feed = back.shape[1]
    gate_act, up_act = pre[:, :feed], pre[:, feed:]
    sig = 1.0 / (1.0 + jnp.exp(-gate_act))
    out[:, :feed] = (back * up_act * (sig * (1.0 + gate_act * (1.0 - sig)))).astype(BF16)
    out[:, feed:] = (back * (gate_act * sig)).astype(BF16)


def width_product(left, weights, store):
    rows = jnp.concatenate([r[...] for r in left], axis=0)
    for kc, weight in enumerate(weights):
        store(kc, product(rows, weight[...], 1, 1).astype(BF16))


def expert_out_kernel(groups, spread, capacity, *refs):
    chunks = refs[-groups:]
    part = refs[spread].shape[0]

    def store(kc, value):
        for ke in range(groups):
            for kx in range(spread):
                at = (kx * groups + ke) * capacity
                chunks[ke][kx * capacity : (kx + 1) * capacity, kc * part : (kc + 1) * part] = value[
                    at : at + capacity
                ]

    width_product(refs[:spread], refs[spread : spread + CORES], store)


def d_rows_kernel(spread, *refs):
    outs = refs[-spread:]
    part = refs[spread].shape[0]
    slots = outs[0].shape[0]

    def store(kc, value):
        for kx in range(spread):
            outs[kx][:, kc * part : (kc + 1) * part] = value[kx * slots : (kx + 1) * slots]

    width_product(refs[:spread], refs[spread : spread + CORES], store)


def weight_kernel(spread, own, sib, *refs):
    hidden, sib_hidden, out = refs[:spread], refs[spread:-1], refs[-1]
    left = jnp.concatenate([own[...], sib[...]], axis=0)
    right = jnp.concatenate([r[...] for r in (*hidden, *sib_hidden)], axis=0)
    out[...] = product(left, right, 0, 0)


def scatter(turned, groups_of_rows, out, held, sems):
    part = held.shape[2]
    copies = []
    for k, rows in enumerate(groups_of_rows):
        held[k] = product(turned, rows, 1, 0).astype(BF16)
        copies.append(pltpu.make_async_copy(held.at[k], out.at[:, columns(k, part)], sems.at[k]))
        copies[-1].start()
    for copy in copies:
        copy.wait()


def combine_kernel(groups, parts, capacity, turned, gate, *refs):
    chunks, far, (out, held, sems) = refs[:groups], refs[groups:-3], refs[-3:]
    chunks = restore(chunks, far_half_first)
    part = held.shape[2]

    def weighted(k):
        cols = slice((k % CORES) * part, (k % CORES + 1) * part)
        if k < CORES:
            rows = jnp.concatenate([c[:capacity, cols] for c in chunks], axis=0)
        else:
            rows = far[k // CORES - 1][:, cols]
        rows = rows.astype(F32) * gate[:, :1]
        high = rows.astype(BF16)
        return jnp.concatenate([high, (rows - high.astype(F32)).astype(BF16)], axis=0)

    twice = jnp.concatenate([turned[...], turned[...]], axis=1)
    scatter(twice, map(weighted, range(parts)), out, held, sems)


def d_tokens_kernel(groups, parts, turned, *refs):
    chunks, (out, held, sems) = restore(refs[:groups], far_half_first), refs[groups:]
    part = held.shape[2]
    rows = (
        jnp.concatenate([c[:, k * part : (k + 1) * part] for c in chunks], axis=0)
        for k in range(parts)
    )
    scatter(turned[...], rows, out, held, sems)


def per_device(tokens, cotangent, route_ids, route_gates, served_order, w_in, w_out):
    groups = lax.axis_size("expert")
    parts = lax.axis_size("fsdp")
    spread = parts // CORES
    count, width = tokens.shape
    capacity = count * route_ids.shape[1] // EXPERTS
    feed = w_out.shape[2]
    slots = groups * capacity
    half = width // spread
    part = width // parts

    def bound(kernel, *sizes):
        return lambda *refs: kernel(*sizes, *refs)

    def to_core(value):
        return lax.ppermute(value, "fsdp", [(i, i ^ 1) for i in range(parts)])

    def to_x(values):
        return [
            lax.ppermute(value, "fsdp", [(i, i ^ ((k + 1) * CORES)) for i in range(parts)])
            for k, value in enumerate(values)
        ]

    def to_expert(chunks):
        return [
            lax.ppermute(value, "expert", [(i, i ^ ke) for i in range(groups)]) if ke else value
            for ke, value in enumerate(chunks)
        ]

    chunk = [shape((capacity, width))] * groups
    by_x = [shape((slots, half))] * spread
    by_halves = [shape((slots, half))] + [shape((slots // 2, half))] * (2 * spread - 2)
    in_own, out_own = w_in[0], w_out[0]
    in_sib, out_sib = to_core(in_own), to_core(out_own)
    outs = call(
        bound(slot_kernel, spread),
        by_halves + by_x + [shape((count, slots)), shape((slots, 128), F32)],
        (route_ids.T, route_gates.T, served_order, tokens, cotangent),
        far=5,
        scratch_shapes=[
            pltpu.VMEM(route_ids.shape[::-1], jnp.int32),
            pltpu.VMEM(route_gates.shape[::-1], F32),
            pltpu.VMEM(served_order.shape, jnp.int32),
            pltpu.VMEM(tokens.shape, BF16),
            pltpu.VMEM(cotangent.shape, BF16),
            pltpu.SemaphoreType.DMA((5,)),
        ],
    )
    turned, gate = outs[-2:]
    near, *far = outs[: 2 * spread - 1]
    grads = outs[2 * spread - 1 : -2]

    near, in_sib, out_sib = lax.optimization_barrier((near, in_sib, out_sib))
    high, low = to_x(far[::2]), to_x(far[1::2])
    middle = groups // 2
    high = call(
        bound(join_kernel, groups, spread, capacity, middle),
        chunk[middle:],
        (near, *high),
        cost=JOIN_COST,
    )
    low = call(bound(join_kernel, groups, spread, capacity, 0), chunk[:middle], (near, *low))
    rows = to_expert([*low, *high])
    grads = [grads[0], *to_x(grads[1:])]
    join = bound(join_kernel, groups, spread, capacity, 0)
    grads = to_expert(call(join, chunk, grads))
    pre, *pre_far = call(
        bound(pre_kernel, groups, spread),
        [shape((slots, 2 * feed), F32)] + [shape((slots, 2 * feed))] * (spread - 1),
        (*arrange(rows, farthest_first), in_own, in_sib),
        cost=PRE_COST,
    )
    pre = (pre, *to_x(pre_far))
    (hidden,) = call(hidden_kernel, [shape((slots, feed))], pre)
    hidden = (hidden, *to_x([hidden] * (spread - 1)))
    own_grads, sib_grads, back, *back_far = call(
        bound(back_kernel, groups, spread),
        [shape((spread * slots, part))] * 2
        + [shape((slots, feed), F32)]
        + [shape((slots, feed))] * (spread - 1),
        (*arrange(grads, nearest_first), out_own, out_sib),
        cost=BACK_COST,
    )
    back = (back, *to_x(back_far))
    expert_out = to_expert(
        call(
            bound(expert_out_kernel, groups, spread, capacity),
            [shape((spread * capacity, half))] * groups,
            (*hidden, out_own, out_sib),
            cost=OUT_COST,
        )
    )
    (d_pre,) = call(
        d_pre_kernel, [shape((slots, 2 * feed))], (*pre, *back), after=hidden[:1]
    )
    d_pre = (d_pre, *to_x([d_pre] * (spread - 1)))
    near, *far = call(
        bound(d_rows_kernel, spread), by_x, (*d_pre, in_own, in_sib)
    )
    d_rows = to_expert(call(join, chunk, (near, *to_x(far))))
    far = to_x(
        call(bound(far_kernel, groups, spread, capacity), by_x[1:], arrange(expert_out, far_half_first))
    )
    d_w_out, token = call(
        bound(weight_kernel, spread),
        [shape((part, feed), F32)],
        (own_grads, to_core(sib_grads), *hidden, *[to_core(value) for value in hidden]),
        token=True,
    )

    def scattered(kernel, operands, **kw):
        return call(
            kernel,
            [shape((count, width))],
            operands,
            out_specs=[pl.BlockSpec(memory_space=pltpu.HBM)]
            + [pl.BlockSpec(memory_space=pltpu.VMEM)] * kw.get("token", False),
            scratch_shapes=[
                pltpu.VMEM((parts, count, part), BF16),
                pltpu.SemaphoreType.DMA((parts,)),
            ],
            **kw,
        )

    combined, token = scattered(
        bound(combine_kernel, groups, parts, capacity),
        (turned, gate, *arrange(expert_out, far_half_first), *far),
        after=(token,),
        token=True,
    )
    (d_tokens,) = scattered(
        bound(d_tokens_kernel, groups, parts), (turned, *arrange(d_rows, far_half_first)), after=(token,)
    )
    return combined, d_tokens, d_w_out[None]


def solution(mesh):
    rows = P(("replica", "expert", "fsdp"), None)
    weights = P("expert", "fsdp", None)
    return jax.shard_map(
        per_device,
        mesh=mesh,
        in_specs=(rows,) * 5 + (weights,) * 2,
        out_specs=(rows, rows, P(("replica", "expert"), "fsdp", None)),
        check_vma=False,
    )
```
